32 devices in a mesh: dp: 8 (over z, y), chan: 4 (over x, core).
Axes of the slice: x: 2, y: 2, z: 4, core: 2. Of those that a mesh axis runs over, the one named last changes fastest.
Arguments:
- x_in: float32 [1024, 1024], P('dp', 'chan'), may hold values from -6 to 6
- norm_gain: float32 [2, 1024], P(None, 'chan'), may hold values from 0.5 to 1.5
- in_weight: bfloat16 [2, 1024, 2, 2048], P(None, None, None, 'chan'), may hold values from -0.1875 to 0.1875
- conv_weight: float32 [2, 4, 2048], P(None, None, 'chan'), may hold values from -3 to 3
- conv_bias: float32 [2, 2048], P(None, 'chan'), may hold values from -1.5 to 1.5
- xproj_weight: bfloat16 [2, 96, 2048], P(None, None, 'chan'), may hold values from -0.125 to 0.125
- dt_weight: bfloat16 [2, 64, 2048], P(None, None, 'chan'), may hold values from -0.75 to 0.75
- dt_bias: float32 [2, 2048], P(None, 'chan'), may hold values from -3 to -1
- a_log: float32 [2, 16, 2048], P(None, None, 'chan'), may hold values from -7 to 1.5
- skip_gain: float32 [2, 2048], P(None, 'chan'), may hold values from 0.5 to 1.5
- out_weight: bfloat16 [2, 2048, 1024], P(None, 'chan'), may hold values from -0.125 to 0.125
- seq_lengths: int32 [4], replicated, may hold values from 1 to 897, 1024 in all
- char_mask: int32 [1024], P('dp'), may hold values 0 or 1
- out_probe: float32 [1024, 1024], P('dp', 'chan'), may hold values from -6 to 6
Outputs:
- block_out: float32 [1024, 1024], P('dp', 'chan')
- input_grad: float32 [1024, 1024], P('dp', 'chan')
- gain_grad: float32 [2, 1024], P(None, 'chan')
- in_weight_grad: float32 [2, 1024, 2, 2048], P(None, None, None, 'chan')
- conv_weight_grad: float32 [2, 4, 2048], P(None, None, 'chan')
- conv_bias_grad: float32 [2, 2048], P(None, 'chan')
- xproj_grad: float32 [2, 96, 2048], P(None, None, 'chan')
- dt_weight_grad: float32 [2, 64, 2048], P(None, None, 'chan')
- dt_bias_grad: float32 [2, 2048], P(None, 'chan')
- a_log_grad: float32 [2, 16, 2048], P(None, None, 'chan')
- skip_grad: float32 [2, 2048], P(None, 'chan')
- out_weight_grad: float32 [2, 2048, 1024], P(None, 'chan')
The draws below stay inside these ranges and needn't reach their ends.
Inputs may be any that keep to these rules, and one draw needn't show every extreme that they name: `seq_lengths`: the lengths sum to 1024; the longest is exactly 897.
All inputs are finite; a program needn't handle non-finite values. No bound on the sum of `char_mask` on one device may be relied on, other than what follows from the above.
Results may differ from the reference program's by a relative error of at most 0.02.
Values may be sent and summed in bfloat16 or wider, within the bound.
A program may use at most 192 MiB of HBM per device.

```python
import math
import jax
import jax.numpy as jnp
import numpy as np
from jax import lax

D = 1024
E = 2048
STATE = 16
CONV = 4
RANK = 64
LAYERS = 2
NSEQ = 4
TOKENS = 1024
MOST_LEN = 897
XDIM = 96


def plant(result, key, low, top_value):
    spot = [jax.random.randint(jax.random.fold_in(key, axis), (), 0, length) for axis, length in enumerate(result.shape)]
    main_axis = result.shape.index(max(result.shape))
    beside = spot[:main_axis] + [(spot[main_axis] + 1) % result.shape[main_axis]] + spot[main_axis + 1:]
    return result.at[tuple(spot)].set(low).at[tuple(beside)].set(top_value)


def shard_levels(rng, extent, cuts, low, high):
    factor_of = 1.0
    for position, parts in cuts:
        draws = jax.random.uniform(jax.random.fold_in(jax.random.fold_in(rng, 6), position), (parts,), jnp.float32, low / len(cuts), high / len(cuts))
        factor_of = factor_of * jnp.repeat(jnp.exp(draws), extent[position] // parts).reshape((-1,) + (1,) * (len(extent) - 1 - position))
    return factor_of


def split_up(count, total, most, lean):
    loads = [(1 << 20) // math.isqrt(grade ** lean) + 1 for grade in range(2, count + 1)]
    spare, counts = total - most - (count - 1), [1] * (count - 1)
    while spare > 0:
        candidates = [i for i in range(count - 1) if counts[i] < most]
        whole, budget = sum([loads[i] for i in candidates]), spare
        for i in candidates:
            more = min(most - counts[i], max(1, budget * loads[i] // whole), spare)
            counts[i] = counts[i] + more
            spare = spare - more
    return np.array([most] + counts)


def ragged_sizes(rng, number_of, total, bound, slope):
    if number_of == 2:
        one = jax.random.randint(rng, (), max(1, total - bound), min(bound, total - 1) + 1)
        return jnp.stack([one, total - one])
    lengths = jnp.asarray(split_up(number_of, total, bound, slope), jnp.int32)
    pairs = (number_of - 1) // 2
    donor, taker = lengths[1:1 + 2 * pairs:2], lengths[2:2 + 2 * pairs:2]
    margin = jnp.minimum(donor - 1, bound - taker)
    moved = jax.random.randint(jax.random.fold_in(rng, 1), (pairs,), 0, 1 << 20) % (margin + 1)
    lengths = lengths.at[1:1 + 2 * pairs:2].set(donor - moved).at[2:2 + 2 * pairs:2].set(taker + moved)
    return lengths[jax.random.permutation(jax.random.fold_in(rng, 2), number_of)]


def scatter_about(rng, extent, scale, bound, cuts=(), held_as=jnp.bfloat16):
    result = scale * jax.random.normal(rng, extent, jnp.float32)
    if cuts:
        result = result * shard_levels(rng, extent, cuts, -0.22, 0.18)
    return jnp.clip(result, -bound, bound).astype(held_as)


def setup_inputs(seed: int = 0) -> dict:
    key_list = jax.random.split(jax.random.key(seed), 15)
    return {
        "x_in": scatter_about(key_list[0], (TOKENS, D), 1.0, 6.0, ((0, 8), (1, 4)), jnp.float32),
        "norm_gain": jnp.clip(1.0 + 0.1 * jax.random.normal(key_list[1], (LAYERS, D), jnp.float32), 0.5, 1.5),
        "in_weight": scatter_about(key_list[2], (LAYERS, D, 2, E), D ** -0.5, 0.1875, ((3, 4),)),
        "conv_weight": scatter_about(key_list[3], (LAYERS, CONV, E), CONV ** -0.5, 3.0, ((2, 4),), jnp.float32),
        "conv_bias": scatter_about(key_list[4], (LAYERS, E), 0.3, 1.5, ((1, 4),), jnp.float32),
        "xproj_weight": scatter_about(key_list[5], (LAYERS, XDIM, E), E ** -0.5, 0.125, ((2, 4),)),
        "dt_weight": scatter_about(key_list[6], (LAYERS, RANK, E), RANK ** -0.5, 0.75, ((2, 4),)),
        "dt_bias": jnp.clip(-3.0 + 2.0 * jax.random.uniform(key_list[7], (LAYERS, E), jnp.float32) ** shard_levels(key_list[7], (LAYERS, E), ((1, 4),), -0.2, 0.2), -3.0, -1.0),
        "a_log": jnp.clip(-7.0 + 8.5 * jax.random.uniform(key_list[8], (LAYERS, STATE, E), jnp.float32) ** shard_levels(key_list[8], (LAYERS, STATE, E), ((2, 4),), -0.2, 0.2), -7.0, 1.5),
        "skip_gain": jnp.clip(1.0 + 0.1 * jax.random.normal(key_list[9], (LAYERS, E), jnp.float32), 0.5, 1.5),
        "out_weight": scatter_about(key_list[10], (LAYERS, E, D), E ** -0.5, 0.125, ((1, 4),)),
        "seq_lengths": ragged_sizes(key_list[11], NSEQ, TOKENS, MOST_LEN, 1).astype(jnp.int32),
        "char_mask": plant((jax.random.randint(key_list[12], (TOKENS,), 0, 4) < 3).astype(jnp.int32), jax.random.fold_in(key_list[12], 1), 0, 1),
        "out_probe": scatter_about(key_list[13], (TOKENS, D), 1.0, 6.0, ((0, 8), (1, 4)), jnp.float32),
    }


epsilon = 1e-05
scan_span = 64

@jax.custom_vjp
def low(v):
    return lax.optimization_barrier(v.astype(jnp.bfloat16)).astype(jnp.float32)

@jax.custom_vjp
def low_back(v):
    return v

def low_keep(v):
    return (low(v), None)

def low_pass(kept, grad):
    return (grad,)

def back_keep(v):
    return (v, None)

def back_low(kept, grad):
    return (low(grad),)
low.defvjp(low_keep, low_pass)
low_back.defvjp(back_keep, back_low)

def product(left, right):
    return jnp.dot(left, right, precision=lax.Precision.HIGHEST, preferred_element_type=jnp.float32)

def seq_offsets(seq_lengths):
    starts = (jnp.cumsum(seq_lengths) - seq_lengths).astype(jnp.int32)
    positions = jnp.arange(TOKENS, dtype=jnp.int32)
    seq_first = lax.optimization_barrier(jnp.max(jnp.where(starts[None, :] <= positions[:, None], starts[None, :], 0), axis=1)).astype(jnp.int32)
    return (positions - seq_first).astype(jnp.int32)

def block_runner(a_matrix):

    def token_step(state, item):
        step_size, inputs_u, b_row, c_row, keeping = item
        state = jnp.exp(step_size[None, :] * a_matrix) * keeping * state + (step_size * inputs_u)[None, :] * b_row[:, None]
        return (state, lax.optimization_barrier(jnp.sum(c_row[:, None] * state, axis=0)))

    def run_block(state, block):
        return lax.scan(token_step, state, block)
    return jax.checkpoint(run_block)

def selective_scan(step_size, inputs_u, b_matrix, c_matrix, keeping, a_matrix):
    blocks = TOKENS // scan_span
    shaped = (step_size.reshape(blocks, scan_span, E), inputs_u.reshape(blocks, scan_span, E), b_matrix.reshape(blocks, scan_span, STATE), c_matrix.reshape(blocks, scan_span, STATE), keeping.reshape(blocks, scan_span))
    start_state = jnp.zeros((STATE, E), jnp.float32)
    final_state, outputs = lax.scan(block_runner(a_matrix), start_state, shaped)
    return outputs.reshape(TOKENS, E)

def mamba_layer(x_rows, gain_row, w_in, w_conv, b_conv, w_x, w_dt, b_dt, a_row, skip_row, w_out, offsets):
    inv_rms = lax.rsqrt(lax.optimization_barrier(jnp.mean(x_rows * x_rows, axis=1, keepdims=True)) + epsilon)
    hidden = low(x_rows * inv_rms * gain_row[None, :])
    mixed_rows = low(low_back(product(hidden, w_in.reshape(D, 2 * E))))
    inner_in = mixed_rows[:, :E]
    gate_in = mixed_rows[:, E:]
    padded = jnp.concatenate([jnp.zeros((CONV - 1, E), jnp.float32), inner_in], axis=0)
    conv_out = jnp.zeros((TOKENS, E), jnp.float32) + b_conv[None, :]
    for tap_index in range(CONV):
        valid = (offsets >= CONV - 1 - tap_index).astype(jnp.float32)[:, None]
        conv_out = conv_out + w_conv[tap_index][None, :] * padded[tap_index:tap_index + TOKENS] * valid
    activated = low(jax.nn.silu(conv_out))
    projected = low_back(product(activated, w_x.T))
    step_in = low(projected[:, :RANK])
    b_matrix = projected[:, RANK:RANK + STATE]
    c_matrix = projected[:, RANK + STATE:]
    step_size = jax.nn.softplus(low_back(product(step_in, w_dt)) + b_dt[None, :])
    keeping = (offsets > 0).astype(jnp.float32)
    scanned = selective_scan(step_size, activated, b_matrix, c_matrix, keeping, -jnp.exp(a_row)) + skip_row[None, :] * activated
    gated_rows = low(scanned * jax.nn.silu(gate_in))
    return x_rows + low_back(product(gated_rows, w_out))

def reference(x_in, norm_gain, in_weight, conv_weight, conv_bias, xproj_weight, dt_weight, dt_bias, a_log, skip_gain, out_weight, seq_lengths, char_mask, out_probe):
    offsets = seq_offsets(seq_lengths)

    def forward(stream, gains, w_ins, w_convs, b_convs, w_xs, w_dts, b_dts, a_rows, skips, w_outs):
        for layer_index in range(LAYERS):
            stream = mamba_layer(stream, gains[layer_index], w_ins[layer_index], w_convs[layer_index], b_convs[layer_index], w_xs[layer_index], w_dts[layer_index], b_dts[layer_index], a_rows[layer_index], skips[layer_index], w_outs[layer_index], offsets)
        return stream
    block_out, pullback = jax.vjp(forward, x_in.astype(jnp.float32), norm_gain.astype(jnp.float32), in_weight.astype(jnp.float32), conv_weight.astype(jnp.float32), conv_bias.astype(jnp.float32), xproj_weight.astype(jnp.float32), dt_weight.astype(jnp.float32), dt_bias.astype(jnp.float32), a_log.astype(jnp.float32), skip_gain.astype(jnp.float32), out_weight.astype(jnp.float32))
    cotangent = out_probe * char_mask.astype(jnp.float32)[:, None]
    input_grad, gain_grad, in_weight_grad, conv_weight_grad, conv_bias_grad, xproj_grad, dt_weight_grad, dt_bias_grad, a_log_grad, skip_grad, out_weight_grad = pullback(cotangent)
    return (block_out, input_grad, gain_grad, in_weight_grad, conv_weight_grad, conv_bias_grad, xproj_grad, dt_weight_grad, dt_bias_grad, a_log_grad, skip_grad, out_weight_grad)
```

```python
import functools
from types import SimpleNamespace

import jax
import jax.numpy as jnp
from jax import lax
from jax.experimental import pallas as pl
from jax.experimental.pallas import tpu as pltpu
from jax.sharding import PartitionSpec as P

MESH = pl.DeviceIdType.MESH
LANES = 128
ROWS = 8
HALO = 16
EPSILON = 1e-05
RESET = 1e30
F32 = jnp.float32
BF16 = jnp.bfloat16


def dot(left, right, dims=((1,), (0,)), precision=None):
    return lax.dot_general(
        left, right, (dims, ((), ())), precision=precision, preferred_element_type=F32
    )


def silu_slope(value, sig):
    return sig * (1.0 + value * (1.0 - sig))


def wide(column, width):
    return jnp.concatenate([column] * (width // column.shape[1]), axis=1)


def sizes_of(mesh, x_in, in_weight, xproj_weight, dt_weight, a_log, conv_weight):
    z = SimpleNamespace()
    z.ndp = mesh.shape["dp"]
    z.nch = mesh.shape["chan"]
    z.toks, z.quarter = x_in.shape
    z.width = in_weight.shape[1]
    z.chans = in_weight.shape[3]
    z.layers = in_weight.shape[0]
    z.xdim = xproj_weight.shape[1]
    z.rank = dt_weight.shape[1]
    z.states = a_log.shape[1]
    z.taps = conv_weight.shape[1]
    z.half = z.width // 2
    z.total = z.toks * z.ndp
    z.groups = z.chans // LANES
    z.span = 2 * z.groups
    z.pack = -(-(z.xdim + z.rank + z.states + z.taps + 3) // 128) * 128
    z.shared = z.pack % (16 * z.ndp) == 0
    z.piece = z.pack // z.ndp if z.shared else z.pack
    return z


def scratch_of(z):
    t, d, c, n = z.toks, z.width, z.chans, z.ndp
    ext = t + HALO
    vm = pltpu.VMEM
    by_token = [vm((t, c), F32) for _ in range(9)]
    layer = dict(
        hid=vm((ext, d), BF16),
        inv=vm((ext, LANES), F32),
        xs=vm((ext, d), F32),
        inner=vm((ext, c), F32),
        gate=by_token[0],
        slope=by_token[1],
        actf=by_token[2],
        pre=by_token[3],
        step=by_token[4],
        stepk=by_token[5],
        u=by_token[6],
        scan=by_token[7],
        ds=by_token[8],
        act=vm((t, c), BF16),
        gated=vm((t, c), BF16),
        psend=vm((z.xdim, t), BF16),
        pland=vm((z.nch, z.xdim, t), BF16),
        stept=vm((z.rank, t), BF16),
        bce=vm((t, 2 * z.states, LANES), F32),
        dec=vm((t, z.states, c), F32),
        st=vm((t + 1, z.states, c), F32),
        ssend=vm((8, c), F32),
        ssum=vm((n, 8, c), F32),
        carry=vm((2, z.states, c), BF16),
        sland=vm((n, z.states, c), BF16),
        rland=vm((n, z.states, c), BF16),
        bsend=vm((z.xdim, t), BF16),
        bland=vm((z.nch, z.xdim, t), BF16),
        bhalo=vm((z.nch, z.xdim, t), BF16),
        esend=vm((2 * HALO, c), F32),
        eland=vm((2 * HALO, c), F32),
        dm=vm((t, 2 * c), BF16),
        ht=vm((z.quarter, t), BF16),
        gt=vm((c, t), BF16),
        gq=vm((t, d), BF16),
        g=vm((t, d), F32),
        pack=vm((z.pack, c), F32),
        packb=vm((z.pack, c), BF16),
        rsland=vm((n, z.piece, c), BF16),
        small=vm((z.pack, c), BF16),
        gnsend=vm((8, z.quarter), F32),
        gnland=vm((n, 8, z.quarter), F32),
    )
    halves = [vm((t, z.half), BF16) for _ in range(4)]
    reduction = dict(
        a_send=halves[0],
        a_land=halves[1],
        b_send=halves[2],
        b_land=halves[3],
        full=vm((ext, d), F32),
    )
    return dict(
        layers=[dict(layer) for _ in range(z.layers)],
        reductions=[dict(reduction) for _ in range(4)],
        b_halo=vm((2, HALO, z.half), BF16),
        hq=vm((t, z.quarter), BF16),
        cq=vm((t, z.quarter), BF16),
        cot=vm((t, z.quarter), F32),
        meta=vm((16, z.quarter), F32),
        metas=vm((z.nch, 16, z.quarter), F32),
        metah=vm((z.nch, 16, z.quarter), F32),
        gfull=vm((8, d), F32),
        vm=vm((3, ext, LANES), F32),
        dst=vm((t, c), F32),
        adj=vm((t, c), F32),
        dact=vm((t, c), F32),
        dgated=vm((t, c), F32),
        dc=vm((ext, c), F32),
        grow=vm((8, d), F32),
        raw=vm((z.layers, d * z.span, LANES), BF16),
        stage=vm((LANES * z.span, LANES), F32),
        wi=vm((z.layers, d, 2 * c), BF16),
        wo=vm((z.layers, c, d), BF16),
    )


def block_kernel(z, sems, refs):
    v = SimpleNamespace(**refs)
    L = [SimpleNamespace(**one) for one in v.layers]
    R = [SimpleNamespace(**one) for one in v.reductions]
    t, d, c, n = z.toks, z.width, z.chans, z.ndp
    ext = t + HALO
    half, quarter, groups = z.half, z.quarter, z.groups
    rank, ns = z.rank, z.states

    dp = lax.axis_index("dp")
    ch = lax.axis_index("chan")
    bit = lax.rem(ch, 2)
    side = lax.div(ch, 2)
    across = {2: lax.rem(ch + 2, 4)}
    across[1] = ch + 1 - 2 * bit
    across[3] = lax.rem(across[1] + 2, 4)
    pair = lax.rem(dp, 2)
    twin = dp + 1 - 2 * pair
    rank_q = lax.div(dp, 2)
    nq = n // 2
    has_next = dp + 1 < n
    has_prev = dp > 0
    q_cols = pl.ds(pl.multiple_of(ch * quarter, quarter), quarter)
    h_mine = pl.ds(pl.multiple_of(bit * half, half), half)
    h_other = pl.ds(pl.multiple_of((1 - bit) * half, half), half)

    drains = []
    counter = [0]

    def alloc(count):
        base = counter[0]
        counter[0] += count
        return base

    def remote(src, dst, index, target):
        return pltpu.make_async_remote_copy(
            src_ref=src,
            dst_ref=dst,
            send_sem=v.ss.at[index],
            recv_sem=v.rs.at[index],
            device_id=target,
            device_id_type=MESH,
        )

    def send(src, dst, target):
        copy = remote(src, dst, alloc(1), target)
        copy.start()
        drains.append(copy.wait_send)
        return copy

    def chan_send(src, dst):
        return [send(src, dst, (dp, across[p])) for p in (2, 3, 1)]

    def edge_send(pairs, step):
        there, here = (has_next, has_prev) if step > 0 else (has_prev, has_next)
        copies = [
            remote(src, dst, alloc(1), (dp + step, chan)) for src, dst, chan in pairs
        ]

        @pl.when(there)
        def _():
            for copy in copies:
                copy.start()

        def drain():
            @pl.when(there)
            def _():
                for copy in copies:
                    copy.wait_send()

        drains.append(drain)

        def arrive():
            @pl.when(here)
            def _():
                for copy in copies:
                    copy.wait_recv()

        return arrive

    def dp_send(src_of, dst, low, high):
        base = alloc(n)

        def copy_of(o):
            to = lax.rem(dp + o, n)
            return remote(src_of(to), dst, base + o, (to, ch))

        def each(act):
            def body(o, carry):
                act(copy_of(o))
                return carry

            return body

        lax.fori_loop(low, high, each(lambda copy: copy.start()), 0)
        drains.append(
            lambda: lax.fori_loop(low, high, each(lambda copy: copy.wait_send()), 0)
        )

        def arrive(first, last):
            lax.fori_loop(first, last, each(lambda copy: copy.wait_recv()), 0)

        return arrive

    def gather(src, place):
        first, second = alloc(nq), alloc(nq)
        local = pltpu.make_async_copy(src, place(dp), v.ls.at[alloc_local()])
        local.start()

        def hop(o):
            to = lax.rem(rank_q + o, nq) * 2 + pair
            return remote(src, place(dp), first + o, (to, ch))

        def relay(o):
            origin = lax.rem(rank_q - o + nq, nq) * 2 + pair
            return remote(place(origin), place(origin), second + o, (twin, ch))

        own = remote(src, place(dp), second, (twin, ch))

        def start(o, carry):
            hop(o).start()
            return carry

        lax.fori_loop(1, nq, start, 0)
        own.start()

        def forward():
            def body(o, carry):
                hop(o).wait_recv()
                relay(o).start()
                return carry

            lax.fori_loop(1, nq, body, 0)

        def finish():
            def body(o, carry):
                hop(o).wait_send()
                relay(o).wait()
                return carry

            lax.fori_loop(1, nq, body, 0)
            own.wait()
            local.wait()

        return SimpleNamespace(forward=forward, finish=finish)

    locals_used = [2 * z.layers]

    def alloc_local():
        locals_used[0] += 1
        return locals_used[0] - 1

    loads = []
    for l in range(z.layers):
        loads.append(
            (
                pltpu.make_async_copy(
                    v.w_in.at[pl.ds(l * d * z.span, d * z.span), :],
                    v.raw.at[l],
                    v.ls.at[2 * l],
                ),
                pltpu.make_async_copy(v.w_out.at[l], v.wo.at[l], v.ls.at[2 * l + 1]),
            )
        )
        for copy in loads[l]:
            copy.start()

    def load_in(l):
        loads[l][0].wait()
        rows = LANES * z.span

        def body(k, carry):
            at = pl.ds(pl.multiple_of(k * rows, rows), rows)
            to = pl.ds(pl.multiple_of(k * LANES, LANES), LANES)
            v.stage[...] = v.raw[l, at, :].astype(F32)
            for g in range(groups):
                for side_of in range(2):
                    col = side_of * c + g * LANES
                    v.wi[l, to, col : col + LANES] = v.stage[
                        pl.ds(2 * g + side_of, LANES, stride=z.span), :
                    ].astype(BF16)
            return carry

        lax.fori_loop(0, d // LANES, body, 0)

    barrier = pltpu.get_barrier_semaphore()
    for p in (1, 2, 3):
        pl.semaphore_signal(
            barrier, inc=1, device_id=(dp, across[p]), device_id_type=MESH
        )

    def greet(o, carry):
        pl.semaphore_signal(
            barrier, inc=1, device_id=(lax.rem(dp + o, n), ch), device_id_type=MESH
        )
        return carry

    lax.fori_loop(1, n, greet, 0)
    for step in (1, n - 1):
        for p in (1, 2, 3):
            pl.semaphore_signal(
                barrier,
                inc=1,
                device_id=(lax.rem(dp + step, n), across[p]),
                device_id_type=MESH,
            )

    xq = v.x[...]
    v.hq[...] = (xq * v.gain[0:1, :]).astype(BF16)
    v.meta[...] = jnp.zeros_like(v.meta)
    v.meta[0 : z.layers, :] = v.gain[...]
    v.meta[8:16, 0:t] = dot(
        jnp.ones((8, quarter), F32), xq * xq, ((1,), (1,)), lax.Precision.HIGHEST
    )
    mask = jnp.broadcast_to(v.mask[...].astype(F32), (8, t))
    cot = v.probe[...] * jnp.transpose(mask)[:, 0:1]
    v.cot[...] = cot
    v.cq[...] = cot.astype(BF16)

    @pl.when(jnp.logical_not(has_prev))
    def _():
        L[0].hid[0:HALO, :] = jnp.zeros((HALO, d), BF16)
        L[0].xs[0:HALO, :] = jnp.zeros((HALO, d), F32)
        v.metah[...] = jnp.zeros_like(v.metah)
        v.b_halo[...] = jnp.zeros_like(v.b_halo)

    @pl.when(jnp.logical_not(has_next))
    def _():
        for l in range(z.layers):
            L[l].bhalo[...] = jnp.zeros_like(L[l].bhalo)
            L[l].eland[...] = jnp.zeros_like(L[l].eland)

    pl.semaphore_wait(barrier, 3 + (n - 1) + 6)

    own = pl.ds(HALO, t)
    head = pl.ds(0, HALO)
    tail = pl.ds(t - HALO, HALO)
    everyone = [ch, across[1], across[2], across[3]]
    got_h = chan_send(v.hq, L[0].hid.at[own, q_cols])
    got_m = chan_send(v.meta, v.metas.at[ch])
    got_edge = edge_send(
        [(v.hq.at[tail, :], L[0].hid.at[head, q_cols], k) for k in everyone]
        + [(v.meta, v.metah.at[ch], k) for k in everyone],
        1,
    )
    got_x = chan_send(v.x, L[0].xs.at[own, q_cols])
    got_xedge = edge_send(
        [(v.x.at[tail, :], L[0].xs.at[head, q_cols], k) for k in everyone], 1
    )
    got_c = chan_send(v.cq, L[1].gq.at[:, q_cols])
    got_g = chan_send(v.cot, L[1].g.at[:, q_cols])
    L[0].hid[own, q_cols] = v.hq[...]
    v.metas[ch] = v.meta[...]
    L[0].xs[own, q_cols] = xq
    L[1].gq[:, q_cols] = v.cq[...]
    L[1].g[:, q_cols] = cot

    position = dp * t + lax.broadcasted_iota(jnp.int32, (ext, LANES), 0)
    first = jnp.zeros((ext, LANES), jnp.int32)
    start = jnp.int32(0)
    for s in range(v.lengths.shape[0]):
        first = jnp.where(position >= start, start, first)
        start = start + v.lengths[s]
    offset = position - first
    for k in range(z.taps - 1):
        v.vm[k] = jnp.where(offset >= z.taps - 1 - k, 1.0, 0.0).astype(F32)

    def valid(k, rows, width):
        return wide(v.vm[k, rows, :], width)

    def a_of(l):
        return -jnp.exp(v.a_log[l])

    def lane(g):
        return slice(g * LANES, (g + 1) * LANES)

    def fwd_head(l):
        hid, inv = L[l].hid, L[l].inv
        scale = wide(inv[...], c)
        mixed = dot(hid[...], v.wi[l, :, 0:c])
        inner = (scale * mixed).astype(BF16).astype(F32)
        L[l].inner[...] = inner
        conv = jnp.broadcast_to(v.conv_b[l : l + 1, :], (t, c))
        for k in range(z.taps):
            at = HALO - z.taps + 1 + k
            term = v.conv_w[l, k : k + 1, :] * L[l].inner[at : at + t, :]
            conv = conv + (term if k == z.taps - 1 else term * valid(k, slice(0, t), c))
        sig = jax.nn.sigmoid(conv)
        act = (conv * sig).astype(BF16)
        L[l].act[...] = act
        L[l].actf[...] = act.astype(F32)
        part = dot(v.w_x[l], act, ((1,), (1,))).astype(BF16)
        L[l].psend[...] = part
        got = chan_send(L[l].psend, L[l].pland.at[ch])
        L[l].pland[ch] = part
        L[l].slope[...] = silu_slope(conv, sig)
        gate = dot(hid[own, :], v.wi[l, :, c : 2 * c])
        L[l].gate[...] = (wide(inv[own, :], c) * gate).astype(BF16).astype(F32)
        return got

    def fwd_mid(l, got):
        for copy in got:
            copy.wait_recv()
        land = L[l].pland
        proj = land[0].astype(F32)
        for k in range(1, z.nch):
            proj = proj + land[k].astype(F32)
        stept = proj[0:rank, :].astype(BF16)
        L[l].stept[...] = stept
        pre = dot(stept, v.w_dt[l], ((0,), (0,))) + v.dt_b[l : l + 1, :]
        step = jnp.maximum(pre, 0.0) + jnp.log1p(jnp.exp(-jnp.abs(pre)))
        stepk = step + (1.0 - valid(z.taps - 2, slice(0, t), c)) * RESET
        L[l].pre[...] = pre
        L[l].step[...] = step
        L[l].stepk[...] = stepk
        L[l].u[...] = step * L[l].actf[...]
        L[l].ssend[...] = jnp.broadcast_to(
            jnp.sum(stepk, axis=0, keepdims=True), (8, c)
        )
        got_s = dp_send(lambda to: L[l].ssend, L[l].ssum.at[dp], 1, n)
        bc = proj[rank : rank + 2 * ns, :]
        lanes = lax.broadcasted_iota(jnp.int32, (2 * ns, t), 1)
        bce = L[l].bce

        def spread(block, carry):
            for i in range(ROWS):
                tok = block * ROWS + i
                column = jnp.sum(
                    jnp.where(lanes == tok, bc, 0.0), axis=1, keepdims=True
                )
                bce[tok] = jnp.broadcast_to(column, (2 * ns, LANES))
            return carry

        lax.fori_loop(0, t // ROWS, spread, 0)
        return got_s

    def scan_sum(l):
        a = a_of(l)
        stepk, u, bce, dec = L[l].stepk, L[l].u, L[l].bce, L[l].dec

        def body(block, state):
            state = list(state)
            rows = pl.ds(pl.multiple_of(block * ROWS, ROWS), ROWS)
            sk, uu = stepk[rows, :], u[rows, :]
            for i in range(ROWS):
                tok = block * ROWS + i
                b = bce[tok, 0:ns, :]
                for g in range(groups):
                    e = jnp.exp(sk[i : i + 1, lane(g)] * a[:, lane(g)])
                    dec[tok, :, lane(g)] = e
                    state[g] = e * state[g] + uu[i : i + 1, lane(g)] * b
            return tuple(state)

        zero = jnp.zeros((ns, LANES), F32)
        return lax.fori_loop(0, t // ROWS, body, (zero,) * groups)

    def back_sum(l):
        ds, bce, dec = L[l].ds, L[l].bce, L[l].dec

        def body(k, flow):
            flow = list(flow)
            block = t // ROWS - 1 - k
            rows = pl.ds(pl.multiple_of(block * ROWS, ROWS), ROWS)
            dd = ds[rows, :]
            for i in reversed(range(ROWS)):
                tok = block * ROWS + i
                cc = bce[tok, ns : 2 * ns, :]
                for g in range(groups):
                    lam = cc * dd[i : i + 1, lane(g)] + flow[g]
                    flow[g] = dec[tok, :, lane(g)] * lam
            return tuple(flow)

        zero = jnp.zeros((ns, LANES), F32)
        return lax.fori_loop(0, t // ROWS, body, (zero,) * groups)

    def put(ref, k, parts):
        for g in range(groups):
            ref[k, :, lane(g)] = parts[g].astype(BF16)

    def carry_in(l, land, order, count):
        a = a_of(l)

        def body(k, carry):
            j = order(k)
            return (
                jnp.exp(a * L[l].ssum[j, 0:1, :]) * carry + land[j].astype(F32)
            )

        return lax.fori_loop(0, count, body, jnp.zeros((ns, c), F32))

    def scan_out(l, carry):
        u, bce, dec, st = L[l].u, L[l].bce, L[l].dec, L[l].st
        y = L[l].scan
        st[0] = carry

        def body(block, state):
            state = list(state)
            rows = pl.ds(pl.multiple_of(block * ROWS, ROWS), ROWS)
            uu = u[rows, :]
            outs = [[] for _ in range(groups)]
            for i in range(ROWS):
                tok = block * ROWS + i
                b = bce[tok, 0:ns, :]
                cc = bce[tok, ns : 2 * ns, :]
                for g in range(groups):
                    s = dec[tok, :, lane(g)] * state[g] + uu[i : i + 1, lane(g)] * b
                    st[tok + 1, :, lane(g)] = s
                    state[g] = s
                    outs[g].append(jnp.sum(cc * s, axis=0, keepdims=True))
            for g in range(groups):
                y[rows, lane(g)] = jnp.concatenate(outs[g], axis=0)
            return tuple(state)

        lax.fori_loop(
            0, t // ROWS, body, tuple(carry[:, lane(g)] for g in range(groups))
        )
        scanned = y[...] + v.skip[l : l + 1, :] * L[l].actf[...]
        y[...] = scanned
        gate = L[l].gate[...]
        gated = (scanned * gate * jax.nn.sigmoid(gate)).astype(BF16)
        L[l].gated[...] = gated
        return gated

    def reduce_a(k, part_of):
        send_ref, keep_ref = R[k].a_send, R[k].full
        send_ref[...] = part_of(h_other).astype(BF16)
        got = send(send_ref, R[k].a_land, (dp, across[1]))
        keep_ref[own, h_mine] = part_of(h_mine)
        return got

    def reduce_b(k, got, edge):
        got.wait_recv()
        b_send = R[k].b_send
        b_send[...] = (
            R[k].full[own, h_mine]
            + R[k].a_land[...].astype(F32)
        ).astype(BF16)
        got = send(b_send, R[k].b_land, (dp, across[2]))
        arrive = None
        if edge:
            arrive = edge_send(
                [
                    (b_send.at[tail, :], v.b_halo.at[side], chan)
                    for chan in (ch, across[2])
                ],
                1,
            )
        return got, arrive

    def reduce_c(k, got, arrive):
        got.wait_recv()
        full = R[k].full
        full[own, h_mine] = R[k].b_send[...].astype(F32) + R[k].b_land[...].astype(F32)
        region = full.at[own, h_mine]
        if arrive is not None:
            arrive()
            full[head, h_mine] = v.b_halo[0].astype(F32) + v.b_halo[1].astype(F32)
            region = full.at[:, h_mine]
        return send(region, region, (dp, across[1]))

    def reduce_all(k, part_of, edge=False):
        a = reduce_a(k, part_of)
        b, arrive = reduce_b(k, a, edge)
        reduce_c(k, b, arrive).wait_recv()

    def out_part(l):
        return lambda cols: dot(L[l].gated[...], v.wo[l, :, cols])

    def in_part(l):
        return lambda cols: dot(L[l].dm[...], v.wi[l, cols, :], ((1,), (1,)))

    def back_gate(l):
        dgated = dot(L[l].gq[...], v.wo[l], ((1,), (1,)))
        gate = L[l].gate[...]
        v.dgated[...] = dgated
        L[l].ds[...] = dgated * gate * jax.nn.sigmoid(gate)

    def back_dgate(l):
        gate = L[l].gate[...]
        sig = jax.nn.sigmoid(gate)
        dgate = v.dgated[...] * L[l].scan[...] * silu_slope(gate, sig)
        L[l].dm[:, c : 2 * c] = (wide(L[l].inv[own, :], c) * dgate).astype(
            BF16
        )

    def back_scan(l, flow_in):
        a = a_of(l)
        ds, u, bce, dec, st = L[l].ds, L[l].u, L[l].bce, L[l].dec, L[l].st
        stepk, actf = L[l].stepk, L[l].actf
        lanes = lax.broadcasted_iota(jnp.int32, (ns, t), 1)

        def body(k, carry):
            flow, acc, acc_b, acc_c = list(carry[0]), list(carry[1]), carry[2], carry[3]
            block = t // ROWS - 1 - k
            rows = pl.ds(pl.multiple_of(block * ROWS, ROWS), ROWS)
            dd, uu, sk, aa = ds[rows, :], u[rows, :], stepk[rows, :], actf[rows, :]
            d_step = [[] for _ in range(groups)]
            d_adj = [[] for _ in range(groups)]
            for i in reversed(range(ROWS)):
                tok = block * ROWS + i
                b = bce[tok, 0:ns, :]
                cc = bce[tok, ns : 2 * ns, :]
                sum_b = jnp.zeros((ns, LANES), F32)
                sum_c = jnp.zeros((ns, LANES), F32)
                for g in range(groups):
                    drow = dd[i : i + 1, lane(g)]
                    lam = cc * drow + flow[g]
                    flow[g] = dec[tok, :, lane(g)] * lam
                    rate = flow[g] * st[tok, :, lane(g)]
                    acc[g] = acc[g] + rate * sk[i : i + 1, lane(g)]
                    adj = jnp.sum(lam * b, axis=0, keepdims=True)
                    d_adj[g].insert(0, adj)
                    d_step[g].insert(
                        0,
                        jnp.sum(rate * a[:, lane(g)], axis=0, keepdims=True)
                        + adj * aa[i : i + 1, lane(g)],
                    )
                    sum_b = sum_b + lam * uu[i : i + 1, lane(g)]
                    sum_c = sum_c + st[tok + 1, :, lane(g)] * drow
                acc_b = jnp.where(
                    lanes == tok, jnp.sum(sum_b, axis=1, keepdims=True), acc_b
                )
                acc_c = jnp.where(
                    lanes == tok, jnp.sum(sum_c, axis=1, keepdims=True), acc_c
                )
            for g in range(groups):
                v.dst[rows, lane(g)] = jnp.concatenate(d_step[g], axis=0)
                v.adj[rows, lane(g)] = jnp.concatenate(d_adj[g], axis=0)
            return (tuple(flow), tuple(acc), acc_b, acc_c)

        zero = jnp.zeros((ns, LANES), F32)
        _, acc, acc_b, acc_c = lax.fori_loop(
            0,
            t // ROWS,
            body,
            (
                tuple(flow_in[:, lane(g)] for g in range(groups)),
                (zero,) * groups,
                jnp.zeros((ns, t), F32),
                jnp.zeros((ns, t), F32),
            ),
        )
        at = z.xdim + rank
        for g in range(groups):
            L[l].pack[at : at + ns, lane(g)] = acc[g] * a[:, lane(g)]
        return acc_b, acc_c

    def back_mid(l, acc_b, acc_c):
        pack = L[l].pack
        actf = L[l].actf[...]
        ds = L[l].ds[...]
        dpre = v.dst[...] * jax.nn.sigmoid(L[l].pre[...])
        dpre_q = dpre.astype(BF16)
        bsend = L[l].bsend
        bsend[0:rank, :] = dot(v.w_dt[l], dpre_q, ((1,), (1,))).astype(BF16)
        bsend[rank : rank + ns, :] = acc_b.astype(BF16)
        bsend[rank + ns : rank + 2 * ns, :] = acc_c.astype(BF16)
        got = chan_send(bsend, L[l].bland.at[ch])
        L[l].bland[ch] = bsend[...]
        dact = ds * v.skip[l : l + 1, :] + L[l].step[...] * v.adj[...]
        v.dact[...] = dact
        L[l].esend[0:HALO, :] = dact[0:HALO, :]
        L[l].esend[HALO : 2 * HALO, :] = L[l].slope[0:HALO, :]
        edge = edge_send(
            [(L[l].esend, L[l].eland, ch)]
            + [(bsend, L[l].bhalo.at[ch], k) for k in everyone],
            -1,
        )
        pack[z.xdim : z.xdim + rank, :] = dot(L[l].stept[...], dpre_q)
        at = z.xdim + rank + ns + z.taps
        pack[at + 1 : at + 2, :] = jnp.sum(dpre, axis=0, keepdims=True)
        pack[at + 2 : at + 3, :] = jnp.sum(ds * actf, axis=0, keepdims=True)
        if at + 3 < z.pack:
            pack[at + 3 :, :] = jnp.zeros((z.pack - at - 3, c), F32)
        return got, edge

    def sum_land(ref):
        total = ref[0].astype(F32)
        for k in range(1, z.nch):
            total = total + ref[k].astype(F32)
        return total.astype(BF16)

    def back_conv(l, got, edge):
        pack = L[l].pack
        for copy in got:
            copy.wait_recv()
        edge()
        dproj = sum_land(L[l].bland)
        dproj_h = sum_land(L[l].bhalo)
        wx = v.w_x[l]
        dact = v.dact[...] + dot(dproj, wx, ((0,), (0,)))
        dconv = dact * L[l].slope[...]
        v.dc[0:t, :] = dconv
        eland = L[l].eland
        after = dot(dproj_h, wx, ((0,), (0,)))[0:HALO, :]
        v.dc[t:ext, :] = (eland[0:HALO, :] + after) * eland[HALO : 2 * HALO, :]
        dinner = jnp.zeros((t, c), F32)
        for k in range(z.taps):
            at = z.taps - 1 - k
            rows = slice(at, at + t)
            term = v.dc[rows, :] * v.conv_w[l, k : k + 1, :]
            dinner = dinner + (
                term if k == z.taps - 1 else term * valid(k, rows, c)
            )
        L[l].dm[:, 0:c] = (wide(L[l].inv[own, :], c) * dinner).astype(BF16)
        return dproj

    def back_rest(l, dproj):
        pack = L[l].pack
        pack[0 : z.xdim, :] = dot(dproj, L[l].act[...])
        dconv = v.dc[0:t, :]
        at = z.xdim + rank + ns
        for k in range(z.taps):
            row = HALO - z.taps + 1 + k
            term = dconv * L[l].inner[row : row + t, :]
            if k < z.taps - 1:
                term = term * valid(k, slice(0, t), c)
            pack[at + k : at + k + 1, :] = jnp.sum(term, axis=0, keepdims=True)
        pack[at + z.taps : at + z.taps + 1, :] = jnp.sum(dconv, axis=0, keepdims=True)

    def back_norm(l, k):
        u = R[k].full[own, :]
        x = L[l].xs[own, :]
        scaled = u * v.gfull[l : l + 1, :]
        xhat = x * wide(L[l].inv[own, :], d)
        mean = jnp.sum(scaled * xhat, axis=1, keepdims=True) * (1.0 / d)
        v.grow[...] = jnp.broadcast_to(jnp.sum(u * x, axis=0, keepdims=True), (8, d))
        L[l].gnsend[...] = v.grow[:, q_cols]
        L[l].gnland[dp] = v.grow[:, q_cols]
        arrive = dp_send(
            lambda to: L[l].gnsend, L[l].gnland.at[dp], 1, n
        )
        return L[l].g[...] + scaled - xhat * mean, arrive

    def gain_out(l, arrive):
        arrive(1, n)
        total = lax.fori_loop(
            0, n, lambda j, s: s + L[l].gnland[j], jnp.zeros((8, quarter), F32)
        )
        v.gains[l : l + 1, :] = total[0:1, :]

    def small_scatter(l):
        if not z.shared:
            v.smalls[l] = L[l].pack[...]
            return None
        rows = z.piece
        packb = L[l].packb
        packb[...] = L[l].pack[...].astype(BF16)
        piece = lambda j: pl.ds(pl.multiple_of(j * rows, rows), rows)
        arrive = dp_send(
            lambda to: packb.at[piece(to), :], L[l].rsland.at[dp], 1, n
        )
        L[l].rsland[dp] = packb[piece(dp), :]
        return arrive

    def small_gather(l, arrive):
        if not z.shared:
            return None
        rows = z.piece
        arrive(1, n)
        total = lax.fori_loop(
            0,
            n,
            lambda j, s: s + L[l].rsland[j].astype(F32),
            jnp.zeros((rows, c), F32),
        )
        mine = pl.ds(pl.multiple_of(dp * rows, rows), rows)
        L[l].small[mine, :] = total.astype(BF16)
        return dp_send(
            lambda to: L[l].small.at[mine, :], L[l].small.at[mine, :], 1, n
        )

    def small_out(l, arrive):
        if z.shared:
            arrive(1, n)
            v.smalls[l] = L[l].small[...]

    def inverse(total):
        return lax.rsqrt(total * (1.0 / d) + EPSILON)

    def norms():
        sums, sums_h = v.metas[0, 8:16, 0:t], v.metah[0, 8:16, 0:t]
        v.gfull[:, 0:quarter] = v.metas[0, 0:8, :]
        for k in range(1, z.nch):
            sums = sums + v.metas[k, 8:16, 0:t]
            sums_h = sums_h + v.metah[k, 8:16, 0:t]
            v.gfull[:, k * quarter : (k + 1) * quarter] = v.metas[k, 0:8, :]
        L[0].inv[own, :] = jnp.broadcast_to(
            jnp.transpose(inverse(sums))[:, 0:1], (t, LANES)
        )
        L[0].inv[head, :] = jnp.broadcast_to(
            jnp.transpose(inverse(sums_h))[t - HALO : t, 0:1], (HALO, LANES)
        )

    def lanes_at(l, ref, rows):
        return lambda j: ref.at[l, rows, pl.ds(pl.multiple_of(j * t, t), t)]

    def rows_at(l, ref, cols, low=0, high=t):
        return lambda j: ref.at[
            l, pl.ds(pl.multiple_of(j * t + low, high - low), high - low), cols
        ]

    def gather_hid(l):
        L[l].ht[...] = jnp.transpose(L[l].hid[own, q_cols])
        return gather(L[l].ht, lanes_at(l, v.hid_all, q_cols))

    def gather_gat(l):
        L[l].gt[...] = jnp.transpose(L[l].gated[...])
        return gather(L[l].gt, lanes_at(l, v.gat_all, slice(None)))

    def gather_gq(l):
        return gather(L[l].gq.at[:, q_cols], rows_at(l, v.gq_all, q_cols))

    def gather_dmg(l):
        cols = slice(c, 2 * c)
        return gather(L[l].dm.at[:, cols], rows_at(l, v.dmg_all, slice(None)))

    def gather_dmi(l, low=0, high=t):
        src = L[l].dm.at[low:high, 0:c]
        return gather(src, rows_at(l, v.dmi_all, slice(None), low, high))

    def quarter_at(k):
        return pl.ds(pl.multiple_of(k * quarter, quarter), quarter)

    def share(region):
        mine = region(ch)
        got = send(mine, mine, (dp, across[2]))

        def second():
            got.wait_recv()
            theirs = region(across[2])
            one = send(mine, mine, (dp, across[1]))
            two = send(theirs, theirs, (dp, across[1]))

            def done():
                one.wait_recv()
                two.wait_recv()

            return done

        return second

    def share_hid(l):
        return share(lambda k: v.hid_all.at[l, quarter_at(k), :])

    def share_gq(l):
        return share(lambda k: v.gq_all.at[l, :, quarter_at(k)])

    hid0 = gather_hid(0)
    gq1 = gather_gq(1)
    load_in(0)
    for copy in got_h + got_m:
        copy.wait_recv()
    got_edge()
    norms()
    got_p = fwd_head(0)
    load_in(1)
    got_s0 = fwd_mid(0, got_p)
    put(L[0].carry, 0, scan_sum(0))
    got_carry = dp_send(lambda to: L[0].carry.at[0], L[0].sland.at[dp], 1, n - dp)
    for copy in got_x + got_c + got_g:
        copy.wait_recv()
    got_xedge()
    loads[0][1].wait()
    got_s0(1, n)
    got_carry(1, dp + 1)
    hid0.forward()
    gq1.forward()
    scan_out(0, carry_in(0, L[0].sland, lambda k: k, dp))
    red0 = reduce_a(0, out_part(0))
    gat0 = gather_gat(0)
    red0, arrive = reduce_b(0, red0, True)
    reduce_c(0, red0, arrive).wait_recv()
    x1 = L[0].xs[...] + R[0].full[...]
    L[1].xs[...] = x1
    L[1].hid[...] = (x1 * v.gfull[1:2, :]).astype(BF16)
    L[1].inv[...] = jnp.broadcast_to(
        inverse(jnp.sum(x1 * x1, axis=1, keepdims=True)), (ext, LANES)
    )

    got_p = fwd_head(1)
    hid1 = gather_hid(1)
    gat0.forward()
    loads[1][1].wait()
    back_gate(1)
    got_s1 = fwd_mid(1, got_p)
    hid0.finish()
    share0 = share_hid(0)
    put(L[1].carry, 0, scan_sum(1))
    put(L[1].carry, 1, back_sum(1))
    got_f = dp_send(lambda to: L[1].carry.at[0], L[1].sland.at[dp], 1, n - dp)
    got_r = dp_send(lambda to: L[1].carry.at[1], L[1].rland.at[dp], n - dp, n)
    got_s1(1, n)
    got_f(1, dp + 1)
    got_r(dp + 1, n)
    hid1.forward()
    gq1.finish()
    share1 = share_gq(1)
    scan_out(1, carry_in(1, L[1].sland, lambda k: k, dp))
    gat1 = gather_gat(1)
    back_dgate(1)
    dmg1 = gather_dmg(1)
    red1 = reduce_a(1, out_part(1))

    acc_b, acc_c = back_scan(1, carry_in(1, L[1].rland, lambda k: n - 1 - k, n - 1 - dp))
    got_b, edge = back_mid(1, acc_b, acc_c)
    share0 = share0()
    red1, _ = reduce_b(1, red1, False)
    gat1.forward()
    dproj = back_conv(1, got_b, edge)
    red2 = reduce_a(2, in_part(1))
    dmg1.forward()
    dmi1 = gather_dmi(1)
    back_rest(1, dproj)
    red2, _ = reduce_b(2, red2, False)
    share1 = share1()
    reduce_c(1, red1, None).wait_recv()
    v.block_out[...] = L[1].xs[own, q_cols] + R[1].full[own, q_cols]
    reduce_c(2, red2, None).wait_recv()
    grad, gain1 = back_norm(1, 2)
    L[0].g[...] = grad
    L[0].gq[...] = grad.astype(BF16)

    back_gate(0)
    put(L[0].carry, 1, back_sum(0))
    got_r = dp_send(lambda to: L[0].carry.at[1], L[0].rland.at[dp], n - dp, n)
    gq0 = gather_gq(0)
    back_dgate(0)
    hid1.finish()
    share2 = share_hid(1)
    got_r(dp + 1, n)
    dmg0 = gather_dmg(0)
    dmi1.forward()
    small1 = small_scatter(1)
    acc_b, acc_c = back_scan(0, carry_in(0, L[0].rland, lambda k: n - 1 - k, n - 1 - dp))
    got_b, edge = back_mid(0, acc_b, acc_c)
    share2 = share2()
    gq0.forward()
    dproj = back_conv(0, got_b, edge)
    dmi0 = [gather_dmi(0, 0, t // 2), gather_dmi(0, t // 2, t)]
    red3 = reduce_a(3, in_part(0))
    dmg0.forward()
    back_rest(0, dproj)
    small0 = small_scatter(0)
    small1 = small_gather(1, small1)
    red3, _ = reduce_b(3, red3, False)
    gq0.finish()
    dmi0[0].forward()
    reduce_c(3, red3, None).wait_recv()
    share3 = share_gq(0)
    grad, gain0 = back_norm(0, 3)
    L[0].g[...] = grad
    v.input_grad[...] = L[0].g[:, q_cols]
    dmi0[1].forward()
    small0 = small_gather(0, small0)
    share3 = share3()
    gain_out(0, gain0)
    gain_out(1, gain1)
    small_out(1, small1)
    small_out(0, small0)
    for one in (share0, share1, share2, share3):
        one()
    for one in (gat0, gat1, dmg1, dmi1, dmg0, *dmi0):
        one.finish()
    for drain in drains:
        drain()
    assert counter[0] <= sems[0] and locals_used[0] <= sems[1], (counter, locals_used)


def run_blocks(z, args):
    sems = (160 + 11 * 2 * (z.ndp // 2) + 13 * z.ndp, 4 + 11)
    vmem = pl.BlockSpec(memory_space=pltpu.VMEM)
    smem = pl.BlockSpec(memory_space=pltpu.SMEM)
    anywhere = pl.BlockSpec(memory_space=pl.ANY)
    specs = dict.fromkeys(args, vmem) | dict(
        lengths=smem, w_in=anywhere, w_out=anywhere
    )
    t, d, c, n, layers = z.toks, z.width, z.chans, z.total, z.layers
    shape = jax.ShapeDtypeStruct
    outs = dict(
        block_out=(shape((t, z.quarter), F32), vmem),
        input_grad=(shape((t, z.quarter), F32), vmem),
        smalls=(shape((layers, z.pack, c), BF16 if z.shared else F32), vmem),
        gains=(shape((layers, z.quarter), F32), vmem),
        hid_all=(shape((layers, d, n), BF16), anywhere),
        gat_all=(shape((layers, c, n), BF16), anywhere),
        gq_all=(shape((layers, n, d), BF16), anywhere),
        dmi_all=(shape((layers, n, c), BF16), anywhere),
        dmg_all=(shape((layers, n, c), BF16), anywhere),
    )
    scratch = scratch_of(z)
    flags = dict(
        ss=pltpu.SemaphoreType.DMA((sems[0],)),
        rs=pltpu.SemaphoreType.DMA((sems[0],)),
        ls=pltpu.SemaphoreType.DMA((sems[1],)),
    )
    parts = [args, outs, scratch, flags]
    leaf = lambda node: not isinstance(node, (dict, list))
    trees = [jax.tree.flatten(part, is_leaf=leaf) for part in parts]
    whole = jax.tree.structure([dict(part) for part in parts], is_leaf=leaf)

    def kernel(*refs):
        merged = {}
        for part in jax.tree.unflatten(whole, refs):
            merged |= part
        block_kernel(z, sems, merged)

    results = pl.pallas_call(
        kernel,
        out_shape=[one[0] for one in trees[1][0]],
        in_specs=jax.tree.leaves(specs, is_leaf=leaf),
        out_specs=[one[1] for one in trees[1][0]],
        scratch_shapes=trees[2][0] + trees[3][0],
        compiler_params=pltpu.CompilerParams(
            collective_id=0, has_side_effects=True, vmem_limit_bytes=62 * 2**20
        ),
        name="blocks",
    )(*trees[0][0])
    return SimpleNamespace(**jax.tree.unflatten(trees[1][1], results))


def grad_kernel(z, steps, hid, gat, gq, dmi, dmg, smalls, small_ins, win, wout, *outs):
    rows = hid.shape[1]
    first = pl.program_id(2) == 0
    lhs = hid[0]
    groups = z.groups
    for k, rhs in enumerate((dmi, dmg)):
        part = dot(lhs, rhs[0])
        for j in range(groups):
            at = pl.ds(j * 2 + k, rows, stride=z.span)
            piece = part[:, j * LANES : (j + 1) * LANES]
            if steps == 1:
                win[at, :] = piece
            else:
                win[at, :] = jnp.where(first, 0.0, win[at, :]) + piece
    part = dot(gat[0], gq[0])
    if steps == 1:
        wout[0] = part
    else:
        wout[0] = jnp.where(first, 0.0, wout[0]) + part

    begin = first & (pl.program_id(0) == 0) & (pl.program_id(1) == 0)

    @pl.when(begin)
    def _():
        for src, to in zip(small_ins, outs[:3], strict=True):
            to[...] = src[...]
        at = 0
        for to in outs[3:]:
            for l in range(z.layers):
                if len(to.shape) == 3:
                    count = to.shape[1]
                    to[l] = smalls[l, at : at + count, :].astype(F32)
                else:
                    count = 1
                    to[l : l + 1, :] = smalls[l, at : at + 1, :].astype(F32)
            at += count


def weight_grads(z, r):
    blocks = 4
    deep = min(z.total, 1024)
    steps = z.total // deep
    layers, d, c = z.layers, z.width, z.chans
    rows, orow = d // blocks, c // blocks
    shape = jax.ShapeDtypeStruct
    small_shapes = (
        r.block_out,
        r.input_grad,
        r.gains,
        shape((layers, z.xdim, c), F32),
        shape((layers, z.rank, c), F32),
        shape((layers, z.states, c), F32),
        shape((layers, z.taps, c), F32),
        shape((layers, c), F32),
        shape((layers, c), F32),
        shape((layers, c), F32),
    )

    def fixed(one):
        dims = len(one.shape)
        return pl.BlockSpec(one.shape, lambda l, i, k: (0,) * dims)

    def kernel(hid, gat, gq, dmi, dmg, smalls, block_out, input_grad, gains, *outs):
        ins = (block_out, input_grad, gains)
        grad_kernel(z, steps, hid, gat, gq, dmi, dmg, smalls, ins, *outs)

    win, wout, *rest = pl.pallas_call(
        kernel,
        grid=(layers, blocks, steps),
        out_shape=[
            shape((layers * d * z.span, LANES), F32),
            shape((layers, c, d), F32),
            *[shape(one.shape, F32) for one in small_shapes],
        ],
        in_specs=[
            pl.BlockSpec((1, rows, deep), lambda l, i, k: (l, i, k)),
            pl.BlockSpec((1, orow, deep), lambda l, i, k: (l, i, k)),
            pl.BlockSpec((1, deep, d), lambda l, i, k: (l, k, 0)),
            pl.BlockSpec((1, deep, c), lambda l, i, k: (l, k, 0)),
            pl.BlockSpec((1, deep, c), lambda l, i, k: (l, k, 0)),
            fixed(r.smalls),
            fixed(r.block_out),
            fixed(r.input_grad),
            fixed(r.gains),
        ],
        out_specs=[
            pl.BlockSpec((rows * z.span, LANES), lambda l, i, k: (l * blocks + i, 0)),
            pl.BlockSpec((1, orow, d), lambda l, i, k: (l, i, 0)),
            *[fixed(one) for one in small_shapes],
        ],
        compiler_params=pltpu.CompilerParams(vmem_limit_bytes=56 * 2**20),
        name="weight_grads",
    )(
        r.hid_all,
        r.gat_all,
        r.gq_all,
        r.dmi_all,
        r.dmg_all,
        r.smalls,
        r.block_out,
        r.input_grad,
        r.gains,
    )
    win = win.reshape(layers, d, z.groups, 2, LANES).transpose(0, 1, 3, 2, 4)
    return win.reshape(layers, d, 2, c), wout, rest


def local(
    mesh,
    x_in,
    norm_gain,
    in_weight,
    conv_weight,
    conv_bias,
    xproj_weight,
    dt_weight,
    dt_bias,
    a_log,
    skip_gain,
    out_weight,
    seq_lengths,
    char_mask,
    out_probe,
):
    z = sizes_of(mesh, x_in, in_weight, xproj_weight, dt_weight, a_log, conv_weight)
    w_in = in_weight.reshape(z.layers, z.width, 2, z.groups, LANES)
    w_in = w_in.transpose(0, 1, 3, 2, 4).reshape(-1, LANES)
    r = run_blocks(
        z,
        dict(
            lengths=seq_lengths,
            x=x_in,
            gain=norm_gain,
            probe=out_probe,
            mask=char_mask.reshape(1, z.toks),
            w_in=w_in,
            conv_w=conv_weight,
            conv_b=conv_bias,
            w_x=xproj_weight,
            w_dt=dt_weight,
            dt_b=dt_bias,
            a_log=a_log,
            skip=skip_gain,
            w_out=out_weight,
        ),
    )
    if not z.shared:
        r.smalls = lax.psum(r.smalls, "dp")
    g_in, g_out, rest = weight_grads(z, r)
    block_out, input_grad, gains, g_x, g_dt, g_alog, g_conv_w = rest[:7]
    g_conv_b, g_bias, g_skip = rest[7:]
    return (
        block_out,
        input_grad,
        gains,
        g_in,
        g_conv_w,
        g_conv_b,
        g_x,
        g_dt,
        g_bias,
        g_alog,
        g_skip,
        g_out,
    )


def solution(mesh):
    return jax.shard_map(
        functools.partial(local, mesh),
        mesh=mesh,
        in_specs=(
            P("dp", "chan"),
            P(None, "chan"),
            P(None, None, None, "chan"),
            P(None, None, "chan"),
            P(None, "chan"),
            P(None, None, "chan"),
            P(None, None, "chan"),
            P(None, "chan"),
            P(None, None, "chan"),
            P(None, "chan"),
            P(None, "chan", None),
            P(),
            P("dp"),
            P("dp", "chan"),
        ),
        out_specs=(
            P("dp", "chan"),
            P("dp", "chan"),
            P(None, "chan"),
            P(None, None, None, "chan"),
            P(None, None, "chan"),
            P(None, "chan"),
            P(None, None, "chan"),
            P(None, None, "chan"),
            P(None, "chan"),
            P(None, None, "chan"),
            P(None, "chan"),
            P(None, "chan", None),
        ),
        check_vma=False,
    )
```

```python
import functools
from types import SimpleNamespace

import jax
import jax.numpy as jnp
from jax import lax
from jax.experimental import pallas as pl
from jax.experimental.pallas import tpu as pltpu
from jax.sharding import PartitionSpec as P

MESH = pl.DeviceIdType.MESH
LANES = 128
ROWS = 8
HALO = 16
EPSILON = 1e-05
RESET = 1e30
F32 = jnp.float32
BF16 = jnp.bfloat16


def dot(left, right, dims=((1,), (0,)), precision=None):
    return lax.dot_general(
        left, right, (dims, ((), ())), precision=precision, preferred_element_type=F32
    )


def silu_slope(value, sig):
    return sig * (1.0 + value * (1.0 - sig))


def wide(column, width):
    return jnp.concatenate([column] * (width // column.shape[1]), axis=1)


def sizes_of(mesh, x_in, in_weight, xproj_weight, dt_weight, a_log, conv_weight):
    z = SimpleNamespace()
    z.ndp = mesh.shape["dp"]
    z.nch = mesh.shape["chan"]
    z.toks, z.quarter = x_in.shape
    z.width = in_weight.shape[1]
    z.chans = in_weight.shape[3]
    z.layers = in_weight.shape[0]
    z.xdim = xproj_weight.shape[1]
    z.rank = dt_weight.shape[1]
    z.states = a_log.shape[1]
    z.taps = conv_weight.shape[1]
    z.half = z.width // 2
    z.total = z.toks * z.ndp
    z.groups = z.chans // LANES
    z.chunk = min(256, z.total)
    z.span = 2 * z.groups
    z.pack = 128
    assert max(z.xdim + z.taps + 1, z.rank + z.states + 2) <= z.pack
    z.shared = z.pack % (16 * z.ndp) == 0
    z.piece = z.pack // z.ndp if z.shared else z.pack
    return z


def scratch_of(z):
    t, d, c, n = z.toks, z.width, z.chans, z.ndp
    ext = t + HALO
    vm = pltpu.VMEM
    by_token = [vm((t, c), F32) for _ in range(9)]
    layer = dict(
        hid=vm((ext, d), BF16),
        inv=vm((ext, LANES), F32),
        xs=vm((ext, d), F32),
        inner=vm((ext, c), F32),
        gate=by_token[0],
        slope=by_token[1],
        actf=by_token[2],
        pre=by_token[3],
        step=by_token[4],
        stepk=by_token[5],
        u=by_token[6],
        scan=by_token[7],
        ds=by_token[8],
        act=vm((t, c), BF16),
        gated=vm((t, c), BF16),
        psend=vm((z.xdim, t), BF16),
        pland=vm((z.nch, z.xdim, t), BF16),
        stept=vm((z.rank, t), BF16),
        bce=vm((t, 2 * z.states, LANES), F32),
        dec=vm((t, z.states, c), F32),
        st=vm((t + 1, z.states, c), F32),
        ssend=vm((8, c), F32),
        ssum=vm((n, 8, c), F32),
        carry=vm((2, z.states, c), BF16),
        sland=vm((n, z.states, c), BF16),
        rland=vm((n, z.states, c), BF16),
        bsend=vm((z.xdim, t), BF16),
        bland=vm((z.nch, z.xdim, t), BF16),
        bhalo=vm((z.nch, z.xdim, t), BF16),
        esend=vm((2 * HALO, c), F32),
        eland=vm((2 * HALO, c), F32),
        dm=vm((t, 2 * c), BF16),
        ht=vm((z.quarter, t), BF16),
        sct=vm((c, t), BF16),
        gq=vm((t, d), BF16),
        g=vm((t, d), F32),
        packs=[vm((z.pack, c), F32) for _ in range(2)],
        packed=[vm((z.pack if z.shared else 16, c), BF16) for _ in range(2)],
        rsland=[vm((n if z.shared else 1, z.piece, c), BF16) for _ in range(2)],
        small=[vm((z.pack if z.shared else 16, c), BF16) for _ in range(2)],
        gnsend=vm((8, z.quarter), F32),
        gnland=vm((n, 8, z.quarter), F32),
    )
    halves = [vm((t, z.half), BF16) for _ in range(4)]
    reduction = dict(
        a_send=halves[0],
        a_land=halves[1],
        b_send=halves[2],
        b_land=halves[3],
        full=vm((ext, d), F32),
    )
    return dict(
        layers=[dict(layer) for _ in range(z.layers)],
        reductions=[dict(reduction) for _ in range(4)],
        b_halo=vm((2, HALO, z.half), BF16),
        hq=vm((t, z.quarter), BF16),
        cq=vm((t, z.quarter), BF16),
        cot=vm((t, z.quarter), F32),
        meta=vm((16, z.quarter), F32),
        metas=vm((z.nch, 16, z.quarter), F32),
        metah=vm((z.nch, 16, z.quarter), F32),
        gfull=vm((8, d), F32),
        vm=vm((3, ext, LANES), F32),
        dst=vm((t, c), F32),
        adj=vm((t, c), F32),
        dact=vm((t, c), F32),
        dgated=vm((t, c), F32),
        dc=vm((ext, c), F32),
        grow=vm((8, d), F32),
        raw=vm((d * z.span, LANES), BF16),
        stage=vm((LANES * z.span, LANES), F32),
        hidc=vm((2, d, z.chunk), BF16),
        gqc=vm((2, z.chunk, d), BF16),
        scanc=vm((2, c, z.chunk), BF16),
        gatc=vm((2, c, z.chunk), BF16),
        dmgc=vm((2, c, z.chunk), BF16),
        wi=vm((z.layers, d, 2 * c), BF16),
        wo=vm((z.layers, c, d), BF16),
    )


def block_kernel(z, sems, refs):
    v = SimpleNamespace(**refs)
    L = [SimpleNamespace(**one) for one in v.layers]
    R = [SimpleNamespace(**one) for one in v.reductions]
    t, d, c, n = z.toks, z.width, z.chans, z.ndp
    ext = t + HALO
    half, quarter, groups = z.half, z.quarter, z.groups
    rank, ns = z.rank, z.states

    dp = lax.axis_index("dp")
    ch = lax.axis_index("chan")
    bit = lax.rem(ch, 2)
    side = lax.div(ch, 2)
    across = {2: lax.rem(ch + 2, 4)}
    across[1] = ch + 1 - 2 * bit
    across[3] = lax.rem(across[1] + 2, 4)
    pair = lax.rem(dp, 2)
    twin = dp + 1 - 2 * pair
    rank_q = lax.div(dp, 2)
    nq = n // 2
    has_next = dp + 1 < n
    has_prev = dp > 0
    q_cols = pl.ds(pl.multiple_of(ch * quarter, quarter), quarter)
    h_mine = pl.ds(pl.multiple_of(bit * half, half), half)
    h_other = pl.ds(pl.multiple_of((1 - bit) * half, half), half)

    drains = []
    counter = [0]

    def alloc(count):
        base = counter[0]
        counter[0] += count
        return base

    def remote(src, dst, index, target):
        return pltpu.make_async_remote_copy(
            src_ref=src,
            dst_ref=dst,
            send_sem=v.ss.at[index],
            recv_sem=v.rs.at[index],
            device_id=target,
            device_id_type=MESH,
        )

    def send(src, dst, target):
        copy = remote(src, dst, alloc(1), target)
        copy.start()
        drains.append(copy.wait_send)
        return copy

    def bundle(total, index):
        return remote(total, total, index, (dp, across[1]))

    def send_all(copies, total):
        index = alloc(1)
        for src, dst, target in copies:
            remote(src, dst, index, target).start()
        whole = bundle(total, index)
        drains.append(whole.wait_send)
        return whole

    def chan_send(src, dst, total):
        return send_all([(src, dst, (dp, across[p])) for p in (2, 3, 1)], total)

    def edge_send(groups, step):
        there, here = (has_next, has_prev) if step > 0 else (has_prev, has_next)
        wholes = []
        for copies, total in groups:
            index = alloc(1)
            wholes.append(bundle(total, index))

            @pl.when(there)
            def _():
                for src, dst, chan in copies:
                    remote(src, dst, index, (dp + step, chan)).start()

        def drain():
            @pl.when(there)
            def _():
                for whole in wholes:
                    whole.wait_send()

        drains.append(drain)

        def arrive():
            @pl.when(here)
            def _():
                for whole in wholes:
                    whole.wait_recv()

        return arrive

    def dp_send_all(src_of, dst, total):
        index = alloc(1)

        def body(o, carry):
            to = lax.rem(dp + o, n)
            remote(src_of(to), dst, index, (to, ch)).start()
            return carry

        lax.fori_loop(1, n, body, 0)
        whole = bundle(total, index)
        drains.append(whole.wait_send)
        return whole.wait_recv

    def dp_send(src, dst, base, low, high):
        def copy_of(o):
            return remote(src, dst, base + o - 1, (lax.rem(dp + o, n), ch))

        def each(act):
            def body(o, carry):
                act(copy_of(o))
                return carry

            return body

        lax.fori_loop(low, high, each(lambda copy: copy.start()), 0)
        drains.append(
            lambda: lax.fori_loop(low, high, each(lambda copy: copy.wait_send()), 0)
        )

        def arrive(first, last):
            lax.fori_loop(first, last, each(lambda copy: copy.wait_recv()), 0)

        return arrive

    def gather(src, place, total):
        first, second = alloc(1), alloc(1)
        local = pltpu.make_async_copy(src, place(dp), v.ls.at[alloc_local()])
        local.start()

        def start(o, carry):
            to = lax.rem(rank_q + o, nq) * 2 + pair
            remote(src, place(dp), first, (to, ch)).start()
            return carry

        lax.fori_loop(1, nq, start, 0)
        remote(src, place(dp), second, (twin, ch)).start()

        def forward():
            bundle(total(nq - 1), first).wait_recv()

            def body(o, carry):
                origin = lax.rem(rank_q - o + nq, nq) * 2 + pair
                remote(place(origin), place(origin), second, (twin, ch)).start()
                return carry

            lax.fori_loop(1, nq, body, 0)

        def finish():
            bundle(total(nq - 1), first).wait_send()
            bundle(total(nq), second).wait()
            local.wait()

        return SimpleNamespace(forward=forward, finish=finish)

    locals_used = [2 * z.layers + 10]

    def alloc_local():
        locals_used[0] += 1
        return locals_used[0] - 1

    loads = []
    for l in range(z.layers):
        loads.append(
            (
                pltpu.make_async_copy(
                    v.w_in.at[pl.ds(l * d * z.span, d * z.span), :],
                    v.raw,
                    v.ls.at[2 * l],
                ),
                pltpu.make_async_copy(v.w_out.at[l], v.wo.at[l], v.ls.at[2 * l + 1]),
            )
        )
        loads[l][1].start()
    loads[0][0].start()

    def load_in(l):
        loads[l][0].wait()
        rows = LANES * z.span

        def body(k, carry):
            at = pl.ds(pl.multiple_of(k * rows, rows), rows)
            to = pl.ds(pl.multiple_of(k * LANES, LANES), LANES)
            v.stage[...] = v.raw[at, :].astype(F32)
            for g in range(groups):
                for side_of in range(2):
                    col = side_of * c + g * LANES
                    v.wi[l, to, col : col + LANES] = v.stage[
                        pl.ds(2 * g + side_of, LANES, stride=z.span), :
                    ].astype(BF16)
            return carry

        lax.fori_loop(0, d // LANES, body, 0)
        if l + 1 < z.layers:
            loads[l + 1][0].start()

    barrier = pltpu.get_barrier_semaphore()
    for p in (1, 2, 3):
        pl.semaphore_signal(
            barrier, inc=1, device_id=(dp, across[p]), device_id_type=MESH
        )

    def greet(o, carry):
        pl.semaphore_signal(
            barrier, inc=1, device_id=(lax.rem(dp + o, n), ch), device_id_type=MESH
        )
        return carry

    lax.fori_loop(1, n, greet, 0)
    for step in (1, n - 1):
        for p in (1, 2, 3):
            pl.semaphore_signal(
                barrier,
                inc=1,
                device_id=(lax.rem(dp + step, n), across[p]),
                device_id_type=MESH,
            )

    xq = v.x[...]
    v.hq[...] = (xq * v.gain[0:1, :]).astype(BF16)
    v.meta[...] = jnp.zeros_like(v.meta)
    v.meta[0 : z.layers, :] = v.gain[...]
    v.meta[8:16, 0:t] = dot(
        jnp.ones((8, quarter), F32), xq * xq, ((1,), (1,)), lax.Precision.HIGHEST
    )
    mask = jnp.broadcast_to(v.mask[...].astype(F32), (8, t))
    cot = v.probe[...] * jnp.transpose(mask)[:, 0:1]
    v.cot[...] = cot
    v.cq[...] = cot.astype(BF16)

    @pl.when(jnp.logical_not(has_prev))
    def _():
        L[0].hid[0:HALO, :] = jnp.zeros((HALO, d), BF16)
        L[0].xs[0:HALO, :] = jnp.zeros((HALO, d), F32)
        v.metah[...] = jnp.zeros_like(v.metah)
        v.b_halo[...] = jnp.zeros_like(v.b_halo)

    @pl.when(jnp.logical_not(has_next))
    def _():
        for l in range(z.layers):
            L[l].bhalo[...] = jnp.zeros_like(L[l].bhalo)
            L[l].eland[...] = jnp.zeros_like(L[l].eland)

    pl.semaphore_wait(barrier, 3 + (n - 1) + 6)

    own = pl.ds(HALO, t)
    head = pl.ds(0, HALO)
    tail = pl.ds(t - HALO, HALO)
    everyone = [ch, across[1], across[2], across[3]]
    got_h = chan_send(
        v.hq, L[0].hid.at[own, q_cols], L[0].hid.at[own, 0 : 3 * quarter]
    )
    got_m = chan_send(v.meta, v.metas.at[ch], v.metas.at[0 : z.nch - 1])
    got_edge = edge_send(
        [
            (
                [(v.hq.at[tail, :], L[0].hid.at[head, q_cols], k) for k in everyone],
                L[0].hid.at[head, :],
            ),
            ([(v.meta, v.metah.at[ch], k) for k in everyone], v.metah),
        ],
        1,
    )
    L[0].hid[own, q_cols] = v.hq[...]
    v.metas[ch] = v.meta[...]
    L[0].xs[own, q_cols] = xq
    L[1].gq[:, q_cols] = v.cq[...]
    L[1].g[:, q_cols] = cot

    position = dp * t + lax.broadcasted_iota(jnp.int32, (ext, LANES), 0)
    first = jnp.zeros((ext, LANES), jnp.int32)
    start = jnp.int32(0)
    for s in range(v.lengths.shape[0]):
        first = jnp.where(position >= start, start, first)
        start = start + v.lengths[s]
    offset = position - first
    for k in range(z.taps - 1):
        v.vm[k] = jnp.where(offset >= z.taps - 1 - k, 1.0, 0.0).astype(F32)

    def valid(k, rows, width):
        return wide(v.vm[k, rows, :], width)

    def a_of(l):
        return -jnp.exp(v.a_log[l])

    def lane(g):
        return slice(g * LANES, (g + 1) * LANES)

    def fwd_head(l):
        hid, inv = L[l].hid, L[l].inv
        inner = dot(hid[...], v.wi[l, :, 0:c])
        if l == 0:
            inner = wide(inv[...], c) * inner
        inner = inner.astype(BF16).astype(F32)
        L[l].inner[...] = inner
        conv = jnp.broadcast_to(v.conv_b[l : l + 1, :], (t, c))
        for k in range(z.taps):
            at = HALO - z.taps + 1 + k
            term = v.conv_w[l, k : k + 1, :] * L[l].inner[at : at + t, :]
            conv = conv + (term if k == z.taps - 1 else term * valid(k, slice(0, t), c))
        sig = jax.nn.sigmoid(conv)
        act = (conv * sig).astype(BF16)
        L[l].act[...] = act
        L[l].actf[...] = act.astype(F32)
        part = dot(v.w_x[l], act, ((1,), (1,))).astype(BF16)
        L[l].psend[...] = part
        land = L[l].pland
        got = chan_send(L[l].psend, land.at[ch], land.at[0 : z.nch - 1])
        L[l].pland[ch] = part
        L[l].slope[...] = silu_slope(conv, sig)
        gate = dot(hid[own, :], v.wi[l, :, c : 2 * c])
        if l == 0:
            gate = wide(inv[own, :], c) * gate
        gate = gate.astype(BF16)
        L[l].gate[...] = gate.astype(F32)
        return got

    def fwd_mid(l, got):
        got.wait_recv()
        land = L[l].pland
        proj = land[0].astype(F32)
        for k in range(1, z.nch):
            proj = proj + land[k].astype(F32)
        stept = proj[0:rank, :].astype(BF16)
        L[l].stept[...] = stept
        pre = dot(stept, v.w_dt[l], ((0,), (0,))) + v.dt_b[l : l + 1, :]
        step = jnp.maximum(pre, 0.0) + jnp.log1p(jnp.exp(-jnp.abs(pre)))
        stepk = step + (1.0 - valid(z.taps - 2, slice(0, t), c)) * RESET
        L[l].pre[...] = pre
        L[l].step[...] = step
        L[l].stepk[...] = stepk
        L[l].u[...] = step * L[l].actf[...]
        L[l].ssend[...] = jnp.broadcast_to(
            jnp.sum(stepk, axis=0, keepdims=True), (8, c)
        )
        land = L[l].ssum
        got_s = dp_send_all(lambda to: L[l].ssend, land.at[dp], land.at[0 : n - 1])
        bc = proj[rank : rank + 2 * ns, :]
        lanes = lax.broadcasted_iota(jnp.int32, (2 * ns, t), 1)
        bce = L[l].bce

        def spread(block, carry):
            for i in range(ROWS):
                tok = block * ROWS + i
                column = jnp.sum(
                    jnp.where(lanes == tok, bc, 0.0), axis=1, keepdims=True
                )
                bce[tok] = jnp.broadcast_to(column, (2 * ns, LANES))
            return carry

        lax.fori_loop(0, t // ROWS, spread, 0)
        return got_s

    def scan_sum(l):
        a = a_of(l)
        stepk, u, bce, dec = L[l].stepk, L[l].u, L[l].bce, L[l].dec

        def body(block, state):
            state = list(state)
            rows = pl.ds(pl.multiple_of(block * ROWS, ROWS), ROWS)
            sk, uu = stepk[rows, :], u[rows, :]
            for i in range(ROWS):
                tok = block * ROWS + i
                b = bce[tok, 0:ns, :]
                for g in range(groups):
                    e = jnp.exp(sk[i : i + 1, lane(g)] * a[:, lane(g)])
                    dec[tok, :, lane(g)] = e
                    state[g] = e * state[g] + uu[i : i + 1, lane(g)] * b
            return tuple(state)

        zero = jnp.zeros((ns, LANES), F32)
        return lax.fori_loop(0, t // ROWS, body, (zero,) * groups)

    def back_sum(l):
        ds, bce, dec = L[l].ds, L[l].bce, L[l].dec

        def body(k, flow):
            flow = list(flow)
            block = t // ROWS - 1 - k
            rows = pl.ds(pl.multiple_of(block * ROWS, ROWS), ROWS)
            dd = ds[rows, :]
            for i in reversed(range(ROWS)):
                tok = block * ROWS + i
                cc = bce[tok, ns : 2 * ns, :]
                for g in range(groups):
                    lam = cc * dd[i : i + 1, lane(g)] + flow[g]
                    flow[g] = dec[tok, :, lane(g)] * lam
            return tuple(flow)

        zero = jnp.zeros((ns, LANES), F32)
        return lax.fori_loop(0, t // ROWS, body, (zero,) * groups)

    def put(ref, k, parts):
        for g in range(groups):
            ref[k, :, lane(g)] = parts[g].astype(BF16)

    def carry_in(l, land, order, count):
        a = a_of(l)

        def body(k, carry):
            j = order(k)
            return (
                jnp.exp(a * L[l].ssum[j, 0:1, :]) * carry + land[j].astype(F32)
            )

        return lax.fori_loop(0, count, body, jnp.zeros((ns, c), F32))

    def scan_out(l, carry):
        u, bce, dec, st = L[l].u, L[l].bce, L[l].dec, L[l].st
        y = L[l].scan
        st[0] = carry

        def body(block, state):
            state = list(state)
            rows = pl.ds(pl.multiple_of(block * ROWS, ROWS), ROWS)
            uu = u[rows, :]
            outs = [[] for _ in range(groups)]
            for i in range(ROWS):
                tok = block * ROWS + i
                b = bce[tok, 0:ns, :]
                cc = bce[tok, ns : 2 * ns, :]
                for g in range(groups):
                    s = dec[tok, :, lane(g)] * state[g] + uu[i : i + 1, lane(g)] * b
                    st[tok + 1, :, lane(g)] = s
                    state[g] = s
                    outs[g].append(jnp.sum(cc * s, axis=0, keepdims=True))
            for g in range(groups):
                y[rows, lane(g)] = jnp.concatenate(outs[g], axis=0)
            return tuple(state)

        lax.fori_loop(
            0, t // ROWS, body, tuple(carry[:, lane(g)] for g in range(groups))
        )
        scanned = y[...] + v.skip[l : l + 1, :] * L[l].actf[...]
        y[...] = scanned
        L[l].sct[...] = jnp.transpose(scanned.astype(BF16))
        gate = L[l].gate[...]
        gated = (scanned * gate * jax.nn.sigmoid(gate)).astype(BF16)
        L[l].gated[...] = gated
        return gated

    def reduce_a(k, part_of):
        send_ref, keep_ref = R[k].a_send, R[k].full
        send_ref[...] = part_of(h_other).astype(BF16)
        got = send(send_ref, R[k].a_land, (dp, across[1]))
        keep_ref[own, h_mine] = part_of(h_mine)
        return got

    def reduce_b(k, got, edge):
        got.wait_recv()
        b_send = R[k].b_send
        b_send[...] = (
            R[k].full[own, h_mine]
            + R[k].a_land[...].astype(F32)
        ).astype(BF16)
        got = send(b_send, R[k].b_land, (dp, across[2]))
        arrive = None
        if edge:
            arrive = edge_send(
                [
                    (
                        [
                            (b_send.at[tail, :], v.b_halo.at[side], chan)
                            for chan in (ch, across[2])
                        ],
                        v.b_halo,
                    )
                ],
                1,
            )
        return got, arrive

    def reduce_c(k, got, arrive):
        got.wait_recv()
        full = R[k].full
        full[own, h_mine] = R[k].b_send[...].astype(F32) + R[k].b_land[...].astype(F32)
        region = full.at[own, h_mine]
        if arrive is not None:
            arrive()
            full[head, h_mine] = v.b_halo[0].astype(F32) + v.b_halo[1].astype(F32)
            region = full.at[:, h_mine]
        return send(region, region, (dp, across[1]))

    def reduce_all(k, part_of, edge=False):
        a = reduce_a(k, part_of)
        b, arrive = reduce_b(k, a, edge)
        reduce_c(k, b, arrive).wait_recv()

    def out_part(l):
        return lambda cols: dot(L[l].gated[...], v.wo[l, :, cols])

    def in_part(l):
        return lambda cols: dot(L[l].dm[...], v.wi[l, cols, :], ((1,), (1,)))

    def back_gate(l):
        dgated = dot(L[l].gq[...], v.wo[l], ((1,), (1,)))
        gate = L[l].gate[...]
        v.dgated[...] = dgated
        L[l].ds[...] = dgated * gate * jax.nn.sigmoid(gate)

    def back_dgate(l):
        gate = L[l].gate[...]
        sig = jax.nn.sigmoid(gate)
        dgate = v.dgated[...] * L[l].scan[...] * silu_slope(gate, sig)
        L[l].dm[:, c : 2 * c] = dgate.astype(BF16)

    def back_scan(l, flow_in):
        a = a_of(l)
        ds, u, bce, dec, st = L[l].ds, L[l].u, L[l].bce, L[l].dec, L[l].st
        stepk, actf = L[l].stepk, L[l].actf
        lanes = lax.broadcasted_iota(jnp.int32, (ns, t), 1)

        def body(k, carry):
            flow, acc, acc_b, acc_c = list(carry[0]), list(carry[1]), carry[2], carry[3]
            block = t // ROWS - 1 - k
            rows = pl.ds(pl.multiple_of(block * ROWS, ROWS), ROWS)
            dd, uu, sk, aa = ds[rows, :], u[rows, :], stepk[rows, :], actf[rows, :]
            d_step = [[] for _ in range(groups)]
            d_adj = [[] for _ in range(groups)]
            for i in reversed(range(ROWS)):
                tok = block * ROWS + i
                b = bce[tok, 0:ns, :]
                cc = bce[tok, ns : 2 * ns, :]
                sum_b = jnp.zeros((ns, LANES), F32)
                sum_c = jnp.zeros((ns, LANES), F32)
                for g in range(groups):
                    drow = dd[i : i + 1, lane(g)]
                    lam = cc * drow + flow[g]
                    flow[g] = dec[tok, :, lane(g)] * lam
                    rate = flow[g] * st[tok, :, lane(g)]
                    acc[g] = acc[g] + rate * sk[i : i + 1, lane(g)]
                    adj = jnp.sum(lam * b, axis=0, keepdims=True)
                    d_adj[g].insert(0, adj)
                    d_step[g].insert(
                        0,
                        jnp.sum(rate * a[:, lane(g)], axis=0, keepdims=True)
                        + adj * aa[i : i + 1, lane(g)],
                    )
                    sum_b = sum_b + lam * uu[i : i + 1, lane(g)]
                    sum_c = sum_c + st[tok + 1, :, lane(g)] * drow
                acc_b = jnp.where(
                    lanes == tok, jnp.sum(sum_b, axis=1, keepdims=True), acc_b
                )
                acc_c = jnp.where(
                    lanes == tok, jnp.sum(sum_c, axis=1, keepdims=True), acc_c
                )
            for g in range(groups):
                v.dst[rows, lane(g)] = jnp.concatenate(d_step[g], axis=0)
                v.adj[rows, lane(g)] = jnp.concatenate(d_adj[g], axis=0)
            return (tuple(flow), tuple(acc), acc_b, acc_c)

        zero = jnp.zeros((ns, LANES), F32)
        _, acc, acc_b, acc_c = lax.fori_loop(
            0,
            t // ROWS,
            body,
            (
                tuple(flow_in[:, lane(g)] for g in range(groups)),
                (zero,) * groups,
                jnp.zeros((ns, t), F32),
                jnp.zeros((ns, t), F32),
            ),
        )
        for g in range(groups):
            L[l].packs[0][rank : rank + ns, lane(g)] = acc[g] * a[:, lane(g)]
        return acc_b, acc_c

    def back_mid(l, acc_b, acc_c):
        pack = L[l].packs[0]
        actf = L[l].actf[...]
        ds = L[l].ds[...]
        dpre = v.dst[...] * jax.nn.sigmoid(L[l].pre[...])
        dpre_q = dpre.astype(BF16)
        bsend = L[l].bsend
        bsend[0:rank, :] = dot(v.w_dt[l], dpre_q, ((1,), (1,))).astype(BF16)
        bsend[rank : rank + ns, :] = acc_b.astype(BF16)
        bsend[rank + ns : rank + 2 * ns, :] = acc_c.astype(BF16)
        land = L[l].bland
        got = chan_send(bsend, land.at[ch], land.at[0 : z.nch - 1])
        land[ch] = bsend[...]
        dact = ds * v.skip[l : l + 1, :] + L[l].step[...] * v.adj[...]
        v.dact[...] = dact
        L[l].esend[0:HALO, :] = dact[0:HALO, :]
        L[l].esend[HALO : 2 * HALO, :] = L[l].slope[0:HALO, :]
        edge = edge_send(
            [
                ([(L[l].esend, L[l].eland, ch)], L[l].eland),
                ([(bsend, L[l].bhalo.at[ch], k) for k in everyone], L[l].bhalo),
            ],
            -1,
        )
        pack[0:rank, :] = dot(L[l].stept[...], dpre_q)
        at = rank + ns
        pack[at : at + 1, :] = jnp.sum(dpre, axis=0, keepdims=True)
        pack[at + 1 : at + 2, :] = jnp.sum(ds * actf, axis=0, keepdims=True)
        pack[at + 2 :, :] = jnp.zeros((z.pack - at - 2, c), F32)
        return got, edge

    def sum_land(ref):
        total = ref[0].astype(F32)
        for k in range(1, z.nch):
            total = total + ref[k].astype(F32)
        return total.astype(BF16)

    def back_conv(l, got, edge):
        got.wait_recv()
        edge()
        dproj = sum_land(L[l].bland)
        dproj_h = sum_land(L[l].bhalo)
        wx = v.w_x[l]
        dact = v.dact[...] + dot(dproj, wx, ((0,), (0,)))
        dconv = dact * L[l].slope[...]
        v.dc[0:t, :] = dconv
        eland = L[l].eland
        after = dot(dproj_h, wx, ((0,), (0,)))[0:HALO, :]
        v.dc[t:ext, :] = (eland[0:HALO, :] + after) * eland[HALO : 2 * HALO, :]
        dinner = jnp.zeros((t, c), F32)
        for k in range(z.taps):
            at = z.taps - 1 - k
            rows = slice(at, at + t)
            term = v.dc[rows, :] * v.conv_w[l, k : k + 1, :]
            dinner = dinner + (
                term if k == z.taps - 1 else term * valid(k, rows, c)
            )
        L[l].dm[:, 0:c] = dinner.astype(BF16)
        return dproj

    def back_rest(l, dproj):
        pack = L[l].packs[1]
        pack[0 : z.xdim, :] = dot(dproj, L[l].act[...])
        dconv = v.dc[0:t, :]
        at = z.xdim
        for k in range(z.taps):
            row = HALO - z.taps + 1 + k
            term = dconv * L[l].inner[row : row + t, :]
            if k < z.taps - 1:
                term = term * valid(k, slice(0, t), c)
            pack[at + k : at + k + 1, :] = jnp.sum(term, axis=0, keepdims=True)
        at = at + z.taps
        pack[at : at + 1, :] = jnp.sum(dconv, axis=0, keepdims=True)
        pack[at + 1 :, :] = jnp.zeros((z.pack - at - 1, c), F32)

    def back_norm(l, k):
        inv = wide(L[l].inv[own, :], d)
        u = R[k].full[own, :] * inv
        x = L[l].xs[own, :]
        scaled = u * v.gfull[l : l + 1, :]
        xhat = x * inv
        mean = jnp.sum(scaled * xhat, axis=1, keepdims=True) * (1.0 / d)
        v.grow[...] = jnp.broadcast_to(jnp.sum(u * x, axis=0, keepdims=True), (8, d))
        L[l].gnsend[...] = v.grow[:, q_cols]
        L[l].gnland[dp] = v.grow[:, q_cols]
        land = L[l].gnland
        arrive = dp_send_all(lambda to: L[l].gnsend, land.at[dp], land.at[0 : n - 1])
        return L[l].g[...] + scaled - xhat * mean, arrive

    def gain_out(l, arrive):
        arrive()
        total = lax.fori_loop(
            0, n, lambda j, s: s + L[l].gnland[j], jnp.zeros((8, quarter), F32)
        )
        v.gains[l : l + 1, :] = total[0:1, :]

    def small_scatter(l, p):
        if not z.shared:
            v.smalls[l, p] = L[l].packs[p][...]
            return None
        rows = z.piece
        packed, land = L[l].packed[p], L[l].rsland[p]
        packed[...] = L[l].packs[p][...].astype(BF16)
        piece = lambda j: pl.ds(pl.multiple_of(j * rows, rows), rows)
        arrive = dp_send_all(
            lambda to: packed.at[piece(to), :], land.at[dp], land.at[0 : n - 1]
        )
        land[dp] = packed[piece(dp), :]
        return arrive

    def small_gather(l, p, arrive):
        if not z.shared:
            return None
        rows = z.piece
        small, land = L[l].small[p], L[l].rsland[p]
        arrive()
        total = lax.fori_loop(
            0, n, lambda j, s: s + land[j].astype(F32), jnp.zeros((rows, c), F32)
        )
        mine = pl.ds(pl.multiple_of(dp * rows, rows), rows)
        small[mine, :] = total.astype(BF16)
        return dp_send_all(
            lambda to: small.at[mine, :],
            small.at[mine, :],
            small.at[0 : (n - 1) * rows, :],
        )

    def small_out(l, p, arrive):
        if z.shared:
            arrive()
            v.smalls[l, p] = L[l].small[p][...]

    def inverse(total):
        return lax.rsqrt(total * (1.0 / d) + EPSILON)

    def norms():
        sums, sums_h = v.metas[0, 8:16, 0:t], v.metah[0, 8:16, 0:t]
        v.gfull[:, 0:quarter] = v.metas[0, 0:8, :]
        for k in range(1, z.nch):
            sums = sums + v.metas[k, 8:16, 0:t]
            sums_h = sums_h + v.metah[k, 8:16, 0:t]
            v.gfull[:, k * quarter : (k + 1) * quarter] = v.metas[k, 0:8, :]
        L[0].inv[own, :] = jnp.broadcast_to(
            jnp.transpose(inverse(sums))[:, 0:1], (t, LANES)
        )
        L[0].inv[head, :] = jnp.broadcast_to(
            jnp.transpose(inverse(sums_h))[t - HALO : t, 0:1], (HALO, LANES)
        )

    def in_lanes(src, ref, l, rows):
        return gather(
            src,
            lambda j: ref.at[l, rows, pl.ds(pl.multiple_of(j * t, t), t)],
            lambda count: ref.at[l, rows, 0 : count * t],
        )

    def in_rows(src, ref, l, cols, low=0, high=t):
        m = high - low
        return gather(
            src,
            lambda j: ref.at[l, pl.ds(pl.multiple_of(j * t + low, m), m), cols],
            lambda count: ref.at[l, 0 : count * m, cols],
        )

    def gather_hid(l):
        if l == 0:
            hidden = xq * v.gain[0:1, :] * wide(L[0].inv[own, :], quarter)
            L[0].ht[...] = jnp.transpose(hidden.astype(BF16))
        else:
            L[l].ht[...] = jnp.transpose(L[l].hid[own, q_cols])
        return in_lanes(L[l].ht, v.hid_all, l, q_cols)

    def gather_scan(l):
        return in_lanes(L[l].sct, v.scan_all, l, slice(None))

    def gather_gq(l):
        return in_rows(L[l].gq.at[:, q_cols], v.gq_all, l, q_cols)

    def gather_dmi(l, low=0, high=t):
        src = L[l].dm.at[low:high, 0:c]
        return in_rows(src, v.dmi_all, l, slice(None), low, high)

    def quarter_at(k):
        return pl.ds(pl.multiple_of(k * quarter, quarter), quarter)

    def share(region, total):
        mine = region(ch)
        got = send(mine, mine, (dp, across[2]))

        def second():
            got.wait_recv()
            theirs = region(across[2])
            to = (dp, across[1])
            return send_all([(mine, mine, to), (theirs, theirs, to)], total).wait_recv

        return second

    def share_hid(l):
        return share(
            lambda k: v.hid_all.at[l, quarter_at(k), :],
            v.hid_all.at[l, 0 : 2 * quarter, :],
        )

    def share_gq(l):
        return share(
            lambda k: v.gq_all.at[l, :, quarter_at(k)],
            v.gq_all.at[l, :, 0 : 2 * quarter],
        )

    def share_rows(ref, rows):
        return share(lambda k: ref.at[rows, quarter_at(k)], ref.at[rows, 0 : 2 * quarter])

    chunks = z.total // z.chunk

    def chunk_loads(l, k):
        slot = lax.rem(k, 2)
        base = 2 * z.layers + 5 * slot
        at = pl.ds(pl.multiple_of(k * z.chunk, z.chunk), z.chunk)
        pairs = (
            (v.hid_all.at[l, :, at], v.hidc.at[slot]),
            (v.gq_all.at[l, at, :], v.gqc.at[slot]),
            (v.scan_all.at[l, :, at], v.scanc.at[slot]),
        )
        return [
            pltpu.make_async_copy(src, to, v.ls.at[base + i])
            for i, (src, to) in enumerate(pairs)
        ]

    def chunk_stores(l, k):
        slot = lax.rem(k, 2)
        base = 2 * z.layers + 5 * slot + 3
        at = pl.ds(pl.multiple_of(k * z.chunk, z.chunk), z.chunk)
        pairs = (
            (v.gatc.at[slot], v.gat_all.at[l, :, at]),
            (v.dmgc.at[slot], v.dmg_all.at[l, :, at]),
        )
        return [
            pltpu.make_async_copy(src, to, v.ls.at[base + i])
            for i, (src, to) in enumerate(pairs)
        ]

    def finish_begin(l):
        for copy in chunk_loads(l, jnp.int32(0)):
            copy.start()

    def finish_some(l, low, high):
        def body(k, carry):
            slot = lax.rem(k, 2)

            @pl.when(k + 1 < chunks)
            def _():
                for copy in chunk_loads(l, k + 1):
                    copy.start()

            @pl.when(k >= 2)
            def _():
                for copy in chunk_stores(l, k - 2):
                    copy.wait()

            loads_in = chunk_loads(l, k)
            loads_in[0].wait()
            w_gate = v.wi[l, :, c : 2 * c]
            gate = dot(w_gate, v.hidc[slot], ((0,), (0,))).astype(BF16).astype(F32)
            loads_in[1].wait()
            dgated = dot(v.wo[l], v.gqc[slot], ((1,), (1,)))
            loads_in[2].wait()
            scanned = v.scanc[slot].astype(F32)
            sig = jax.nn.sigmoid(gate)
            v.gatc[slot] = (scanned * gate * sig).astype(BF16)
            v.dmgc[slot] = (dgated * scanned * silu_slope(gate, sig)).astype(BF16)
            for copy in chunk_stores(l, k):
                copy.start()
            return carry

        lax.fori_loop(low, high, body, 0)

    def finish_end(l):
        for k in range(max(chunks - 2, 0), chunks):
            for copy in chunk_stores(l, jnp.int32(k)):
                copy.wait()

    load_in(0)
    got_h.wait_recv()
    got_m.wait_recv()
    got_edge()
    norms()
    got_p = fwd_head(0)
    share_x = share_rows(L[0].xs, own)
    share_c = share_rows(L[1].gq, slice(None))
    got_xedge = edge_send(
        [
            (
                [(v.x.at[tail, :], L[0].xs.at[head, q_cols], k) for k in everyone],
                L[0].xs.at[head, :],
            )
        ],
        1,
    )
    hid0 = gather_hid(0)
    gq1 = gather_gq(1)
    load_in(1)
    got_s0 = fwd_mid(0, got_p)
    put(L[0].carry, 0, scan_sum(0))
    got_carry = dp_send(L[0].carry.at[0], L[0].sland.at[dp], alloc(n - 1), 1, n - dp)
    share_x = share_x()
    share_c = share_c()
    share_g = share_rows(L[1].g, slice(None))
    loads[0][1].wait()
    got_s0()
    got_carry(1, dp + 1)
    hid0.forward()
    gq1.forward()
    scan_out(0, carry_in(0, L[0].sland, lambda k: k, dp))
    scan0 = gather_scan(0)
    red0 = reduce_a(0, out_part(0))
    red0, arrive = reduce_b(0, red0, True)
    share_g = share_g()
    got_c = reduce_c(0, red0, arrive)
    share_x()
    got_xedge()
    got_c.wait_recv()
    x1 = L[0].xs[...] + R[0].full[...]
    L[1].xs[...] = x1
    inv1 = inverse(jnp.sum(x1 * x1, axis=1, keepdims=True))
    L[1].hid[...] = (x1 * inv1 * v.gfull[1:2, :]).astype(BF16)
    L[1].inv[...] = jnp.broadcast_to(inv1, (ext, LANES))

    got_p = fwd_head(1)
    hid1 = gather_hid(1)
    scan0.forward()
    loads[1][1].wait()
    share_c()
    back_gate(1)
    got_s1 = fwd_mid(1, got_p)
    hid0.finish()
    share0 = share_hid(0)
    put(L[1].carry, 0, scan_sum(1))
    put(L[1].carry, 1, back_sum(1))
    base = alloc(n - 1)
    got_f = dp_send(L[1].carry.at[0], L[1].sland.at[dp], base, 1, n - dp)
    got_r = dp_send(L[1].carry.at[1], L[1].rland.at[dp], base, n - dp, n)
    got_s1()
    got_f(1, dp + 1)
    got_r(dp + 1, n)
    hid1.forward()
    gq1.finish()
    share1 = share_gq(1)
    scan_out(1, carry_in(1, L[1].sland, lambda k: k, dp))
    scan1 = gather_scan(1)
    back_dgate(1)
    red1 = reduce_a(1, out_part(1))

    acc_b, acc_c = back_scan(1, carry_in(1, L[1].rland, lambda k: n - 1 - k, n - 1 - dp))
    got_b, edge = back_mid(1, acc_b, acc_c)
    share0 = share0()
    red1, _ = reduce_b(1, red1, False)
    dproj = back_conv(1, got_b, edge)
    red2 = reduce_a(2, in_part(1))
    dmi1 = gather_dmi(1)
    back_rest(1, dproj)
    red2, _ = reduce_b(2, red2, False)
    share1 = share1()
    reduce_c(1, red1, None).wait_recv()
    share1()
    v.block_out[...] = L[1].xs[own, q_cols] + R[1].full[own, q_cols]
    scan1.forward()
    reduce_c(2, red2, None).wait_recv()
    share_g()
    grad, gain1 = back_norm(1, 2)
    L[0].g[...] = grad
    L[0].gq[...] = grad.astype(BF16)

    back_gate(0)
    put(L[0].carry, 1, back_sum(0))
    got_r = dp_send(L[0].carry.at[1], L[0].rland.at[dp], alloc(n - 1), n - dp, n)
    back_dgate(0)
    hid1.finish()
    share2 = share_hid(1)
    got_r(dp + 1, n)
    gq0 = gather_gq(0)
    dmi1.forward()
    small1 = [small_scatter(1, 0), small_scatter(1, 1)]
    acc_b, acc_c = back_scan(0, carry_in(0, L[0].rland, lambda k: n - 1 - k, n - 1 - dp))
    got_b, edge = back_mid(0, acc_b, acc_c)
    share2 = share2()
    small0 = [small_scatter(0, 0)]
    gq0.forward()
    dproj = back_conv(0, got_b, edge)
    dmi0 = [gather_dmi(0, 0, t // 2), gather_dmi(0, t // 2, t)]
    red3 = reduce_a(3, in_part(0))
    back_rest(0, dproj)
    small0.append(small_scatter(0, 1))
    red3, _ = reduce_b(3, red3, False)
    small1 = [small_gather(1, p, small1[p]) for p in range(2)]
    share2()
    scan1.finish()
    finish_begin(1)
    gq0.finish()
    share3 = share_gq(0)
    finish_some(1, 0, chunks // 2)
    got_c = reduce_c(3, red3, None)
    finish_some(1, chunks // 2, chunks)
    got_c.wait_recv()
    grad, gain0 = back_norm(0, 3)
    L[0].g[...] = grad
    v.input_grad[...] = L[0].g[:, q_cols]
    dmi0[0].forward()
    share3 = share3()
    share0()
    scan0.finish()
    share3()
    finish_end(1)
    finish_begin(0)
    small0 = [small_gather(0, p, small0[p]) for p in range(2)]
    dmi0[1].forward()
    finish_some(0, 0, chunks)
    finish_end(0)
    gain_out(0, gain0)
    gain_out(1, gain1)
    for p in range(2):
        small_out(1, p, small1[p])
        small_out(0, p, small0[p])
    for one in (dmi1, *dmi0):
        one.finish()
    for drain in drains:
        drain()
    assert (counter[0], locals_used[0]) == sems, (counter, locals_used)


def run_blocks(z, args):
    sems = (62 + 3 * (z.ndp - 1) + (8 if z.shared else 0), 23)
    vmem = pl.BlockSpec(memory_space=pltpu.VMEM)
    smem = pl.BlockSpec(memory_space=pltpu.SMEM)
    anywhere = pl.BlockSpec(memory_space=pl.ANY)
    specs = dict.fromkeys(args, vmem) | dict(
        lengths=smem, w_in=anywhere, w_out=anywhere
    )
    t, d, c, n, layers = z.toks, z.width, z.chans, z.total, z.layers
    shape = jax.ShapeDtypeStruct
    outs = dict(
        block_out=(shape((t, z.quarter), F32), vmem),
        input_grad=(shape((t, z.quarter), F32), vmem),
        smalls=(shape((layers, 2, z.pack, c), BF16 if z.shared else F32), vmem),
        gains=(shape((layers, z.quarter), F32), vmem),
        hid_all=(shape((layers, d, n), BF16), anywhere),
        gat_all=(shape((layers, c, n), BF16), anywhere),
        dmg_all=(shape((layers, c, n), BF16), anywhere),
        scan_all=(shape((layers, c, n), BF16), anywhere),
        gq_all=(shape((layers, n, d), BF16), anywhere),
        dmi_all=(shape((layers, n, c), BF16), anywhere),
    )
    scratch = scratch_of(z)
    flags = dict(
        ss=pltpu.SemaphoreType.DMA((sems[0],)),
        rs=pltpu.SemaphoreType.DMA((sems[0],)),
        ls=pltpu.SemaphoreType.DMA((sems[1],)),
    )
    parts = [args, outs, scratch, flags]
    leaf = lambda node: not isinstance(node, (dict, list))
    trees = [jax.tree.flatten(part, is_leaf=leaf) for part in parts]
    whole = jax.tree.structure([dict(part) for part in parts], is_leaf=leaf)

    def kernel(*refs):
        merged = {}
        for part in jax.tree.unflatten(whole, refs):
            merged |= part
        block_kernel(z, sems, merged)

    results = pl.pallas_call(
        kernel,
        out_shape=[one[0] for one in trees[1][0]],
        in_specs=jax.tree.leaves(specs, is_leaf=leaf),
        out_specs=[one[1] for one in trees[1][0]],
        scratch_shapes=trees[2][0] + trees[3][0],
        compiler_params=pltpu.CompilerParams(
            collective_id=0, has_side_effects=True, vmem_limit_bytes=62 * 2**20
        ),
        name="blocks",
    )(*trees[0][0])
    return SimpleNamespace(**jax.tree.unflatten(trees[1][1], results))


def grad_kernel(z, steps, ins, small_ins, win, wout, outs):
    hid, gat, dmg, gq, dmi, smalls = ins
    rows = hid.shape[1]
    first = pl.program_id(2) == 0
    lhs = hid[0]
    parts = (dot(lhs, dmi[0]), dot(lhs, dmg[0], ((1,), (1,))))
    for k, part in enumerate(parts):
        for j in range(z.groups):
            at = pl.ds(j * 2 + k, rows, stride=z.span)
            piece = part[:, j * LANES : (j + 1) * LANES]
            if steps == 1:
                win[at, :] = piece
            else:
                win[at, :] = jnp.where(first, 0.0, win[at, :]) + piece
    part = dot(gat[0], gq[0])
    if steps == 1:
        wout[0] = part
    else:
        wout[0] = jnp.where(first, 0.0, wout[0]) + part

    begin = first & (pl.program_id(0) == 0) & (pl.program_id(1) == 0)

    @pl.when(begin)
    def _():
        for src, to in zip(small_ins, outs[:3], strict=True):
            to[...] = src[...]
        at, pack = 0, 0
        for i, to in enumerate(outs[3:]):
            if i == 4:
                at, pack = 0, 1
            for l in range(z.layers):
                if len(to.shape) == 3:
                    count = to.shape[1]
                    to[l] = smalls[l, pack, at : at + count, :].astype(F32)
                else:
                    count = 1
                    to[l : l + 1, :] = smalls[l, pack, at : at + 1, :].astype(F32)
            at += count


def weight_grads(z, r):
    blocks = 2
    deep = min(z.total, 1024)
    steps = z.total // deep
    layers, d, c = z.layers, z.width, z.chans
    rows, orow = d // blocks, c // blocks
    shape = jax.ShapeDtypeStruct
    small_shapes = (
        r.block_out,
        r.input_grad,
        r.gains,
        shape((layers, z.rank, c), F32),
        shape((layers, z.states, c), F32),
        shape((layers, c), F32),
        shape((layers, c), F32),
        shape((layers, z.xdim, c), F32),
        shape((layers, z.taps, c), F32),
        shape((layers, c), F32),
    )

    def fixed(one):
        dims = len(one.shape)
        return pl.BlockSpec(one.shape, lambda l, i, k: (0,) * dims)

    def kernel(*refs):
        ins, small_ins, (win, wout), outs = refs[:6], refs[6:9], refs[9:11], refs[11:]
        grad_kernel(z, steps, ins, small_ins, win, wout, outs)

    win, wout, *rest = pl.pallas_call(
        kernel,
        grid=(layers, blocks, steps),
        out_shape=[
            shape((layers * d * z.span, LANES), F32),
            shape((layers, c, d), F32),
            *[shape(one.shape, F32) for one in small_shapes],
        ],
        in_specs=[
            pl.BlockSpec((1, rows, deep), lambda l, i, k: (l, i, k)),
            pl.BlockSpec((1, orow, deep), lambda l, i, k: (l, i, k)),
            pl.BlockSpec((1, c, deep), lambda l, i, k: (l, 0, k)),
            pl.BlockSpec((1, deep, d), lambda l, i, k: (l, k, 0)),
            pl.BlockSpec((1, deep, c), lambda l, i, k: (l, k, 0)),
            fixed(r.smalls),
            fixed(r.block_out),
            fixed(r.input_grad),
            fixed(r.gains),
        ],
        out_specs=[
            pl.BlockSpec((rows * z.span, LANES), lambda l, i, k: (l * blocks + i, 0)),
            pl.BlockSpec((1, orow, d), lambda l, i, k: (l, i, 0)),
            *[fixed(one) for one in small_shapes],
        ],
        compiler_params=pltpu.CompilerParams(vmem_limit_bytes=60 * 2**20),
        name="weight_grads",
    )(
        r.hid_all,
        r.gat_all,
        r.dmg_all,
        r.gq_all,
        r.dmi_all,
        r.smalls,
        r.block_out,
        r.input_grad,
        r.gains,
    )
    win = win.reshape(layers, d, z.groups, 2, LANES).transpose(0, 1, 3, 2, 4)
    return win.reshape(layers, d, 2, c), wout, rest


def local(
    mesh,
    x_in,
    norm_gain,
    in_weight,
    conv_weight,
    conv_bias,
    xproj_weight,
    dt_weight,
    dt_bias,
    a_log,
    skip_gain,
    out_weight,
    seq_lengths,
    char_mask,
    out_probe,
):
    z = sizes_of(mesh, x_in, in_weight, xproj_weight, dt_weight, a_log, conv_weight)
    w_in = in_weight.reshape(z.layers, z.width, 2, z.groups, LANES)
    w_in = w_in.transpose(0, 1, 3, 2, 4).reshape(-1, LANES)
    r = run_blocks(
        z,
        dict(
            lengths=seq_lengths,
            x=x_in,
            gain=norm_gain,
            probe=out_probe,
            mask=char_mask.reshape(1, z.toks),
            w_in=w_in,
            conv_w=conv_weight,
            conv_b=conv_bias,
            w_x=xproj_weight,
            w_dt=dt_weight,
            dt_b=dt_bias,
            a_log=a_log,
            skip=skip_gain,
            w_out=out_weight,
        ),
    )
    if not z.shared:
        r.smalls = lax.psum(r.smalls, "dp")
    g_in, g_out, rest = weight_grads(z, r)
    block_out, input_grad, gains, g_dt, g_alog, g_bias, g_skip = rest[:7]
    g_x, g_conv_w, g_conv_b = rest[7:]
    return (
        block_out,
        input_grad,
        gains,
        g_in,
        g_conv_w,
        g_conv_b,
        g_x,
        g_dt,
        g_bias,
        g_alog,
        g_skip,
        g_out,
    )


def solution(mesh):
    return jax.shard_map(
        functools.partial(local, mesh),
        mesh=mesh,
        in_specs=(
            P("dp", "chan"),
            P(None, "chan"),
            P(None, None, None, "chan"),
            P(None, None, "chan"),
            P(None, "chan"),
            P(None, None, "chan"),
            P(None, None, "chan"),
            P(None, "chan"),
            P(None, None, "chan"),
            P(None, "chan"),
            P(None, "chan", None),
            P(),
            P("dp"),
            P("dp", "chan"),
        ),
        out_specs=(
            P("dp", "chan"),
            P("dp", "chan"),
            P(None, "chan"),
            P(None, None, None, "chan"),
            P(None, None, "chan"),
            P(None, "chan"),
            P(None, None, "chan"),
            P(None, None, "chan"),
            P(None, "chan"),
            P(None, None, "chan"),
            P(None, "chan"),
            P(None, "chan", None),
        ),
        check_vma=False,
    )
```

```python
import functools
from types import SimpleNamespace

import jax
import jax.numpy as jnp
from jax import lax
from jax.experimental import pallas as pl
from jax.experimental.pallas import tpu as pltpu
from jax.sharding import PartitionSpec as P

MESH = pl.DeviceIdType.MESH
LANES = 128
ROWS = 8
HALO = 16
EPSILON = 1e-05
RESET = 1e30
F32 = jnp.float32
BF16 = jnp.bfloat16


def dot(left, right, dims=((1,), (0,)), precision=None):
    return lax.dot_general(
        left, right, (dims, ((), ())), precision=precision, preferred_element_type=F32
    )


def silu_slope(value, sig):
    return sig * (1.0 + value * (1.0 - sig))


def wide(column, width):
    return jnp.concatenate([column] * (width // column.shape[1]), axis=1)


def sizes_of(mesh, x_in, in_weight, xproj_weight, dt_weight, a_log, conv_weight):
    z = SimpleNamespace()
    z.ndp = mesh.shape["dp"]
    z.nch = mesh.shape["chan"]
    z.toks, z.quarter = x_in.shape
    z.width = in_weight.shape[1]
    z.chans = in_weight.shape[3]
    z.layers = in_weight.shape[0]
    z.xdim = xproj_weight.shape[1]
    z.rank = dt_weight.shape[1]
    z.states = a_log.shape[1]
    z.taps = conv_weight.shape[1]
    z.half = z.width // 2
    z.total = z.toks * z.ndp
    z.groups = z.chans // LANES
    z.chunk = min(256, z.total)
    z.span = 2 * z.groups
    z.pack = 128
    assert max(z.xdim + z.taps + 1, z.rank + z.states + 2) <= z.pack
    z.shared = z.pack % (16 * z.ndp) == 0
    z.piece = z.pack // z.ndp if z.shared else 16
    return z


def scratch_of(z):
    t, d, c, n = z.toks, z.width, z.chans, z.ndp
    ext = t + HALO
    vm = pltpu.VMEM
    by_token = [vm((t, c), F32) for _ in range(9)]
    layer = dict(
        hid=vm((ext, d), BF16),
        inv=vm((ext, LANES), F32),
        xs=vm((ext, d), F32),
        inner=vm((ext, c), F32),
        gate=by_token[0],
        slope=by_token[1],
        actf=by_token[2],
        pre=by_token[3],
        step=by_token[4],
        stepk=by_token[5],
        u=by_token[6],
        scan=by_token[7],
        ds=by_token[8],
        act=vm((t, c), BF16),
        gated=vm((t, c), BF16),
        psend=vm((z.xdim, t), BF16),
        pland=vm((z.nch, z.xdim, t), BF16),
        stept=vm((z.rank, t), BF16),
        bce=vm((t, 2 * z.states, LANES), F32),
        dec=vm((t, z.states, c), F32),
        st=vm((t + 1, z.states, c), F32),
        ssend=vm((8, LANES), F32),
        ssum=vm((n, 8, LANES), F32),
        carry=vm((2, z.states, c), BF16),
        sland=vm((n, z.states, c), BF16),
        rland=vm((n, z.states, c), BF16),
        bsend=vm((z.xdim, t), BF16),
        bland=vm((z.nch, z.xdim, t), BF16),
        bhalo=vm((z.nch, z.xdim, t), BF16),
        esend=vm((2 * HALO, c), F32),
        eland=vm((2 * HALO, c), F32),
        dm=vm((t, 2 * c), BF16),
        ht=vm((z.quarter, t), BF16),
        sct=vm((c, t), BF16),
        gq=vm((t, d), BF16),
        g=vm((t, d), F32),
        packs=[vm((z.pack, c), F32) for _ in range(2)],
        packed=[vm((z.pack if z.shared else 16, c), BF16) for _ in range(2)],
        tland=[vm((z.pack // 2 if z.shared else 16, c), BF16) for _ in range(2)],
        rsland=[vm((n // 2 if z.shared else 1, z.piece, c), BF16) for _ in range(2)],
        small=[vm((z.pack if z.shared else 16, c), BF16) for _ in range(2)],
        gnsend=vm((8, z.quarter), F32),
        gnland=vm((n, 8, z.quarter), F32),
    )
    halves = [vm((t, z.half), BF16) for _ in range(4)]
    reduction = dict(
        a_send=halves[0],
        a_land=halves[1],
        b_send=halves[2],
        b_land=halves[3],
        full=vm((ext, d), F32),
    )
    return dict(
        layers=[dict(layer) for _ in range(z.layers)],
        reductions=[dict(reduction) for _ in range(4)],
        b_halo=vm((2, HALO, z.half), BF16),
        hq=vm((t, z.quarter), BF16),
        cq=vm((t, z.quarter), BF16),
        cot=vm((t, z.quarter), F32),
        meta=vm((16, z.quarter), F32),
        metas=vm((z.nch, 16, z.quarter), F32),
        metah=vm((z.nch, 16, z.quarter), F32),
        gfull=vm((8, d), F32),
        vm=vm((3, ext, LANES), F32),
        dst=vm((t, c), F32),
        adj=vm((t, c), F32),
        dact=vm((t, c), F32),
        dgated=vm((t, c), F32),
        dc=vm((ext, c), F32),
        grow=vm((8, d), F32),
        raw=vm((d * z.span, LANES), BF16),
        stage=vm((LANES * z.span, LANES), F32),
        hidc=vm((2, d, z.chunk), BF16),
        gqc=vm((2, z.chunk, d), BF16),
        scanc=vm((2, c, z.chunk), BF16),
        gatc=vm((2, c, z.chunk), BF16),
        dmgc=vm((2, c, z.chunk), BF16),
        wi=vm((z.layers, d, 2 * c), BF16),
        wo=vm((z.layers, c, d), BF16),
    )


def block_kernel(z, sems, refs):
    v = SimpleNamespace(**refs)
    L = [SimpleNamespace(**one) for one in v.layers]
    R = [SimpleNamespace(**one) for one in v.reductions]
    t, d, c, n = z.toks, z.width, z.chans, z.ndp
    ext = t + HALO
    half, quarter, groups = z.half, z.quarter, z.groups
    rank, ns = z.rank, z.states

    dp = lax.axis_index("dp")
    ch = lax.axis_index("chan")
    bit = lax.rem(ch, 2)
    side = lax.div(ch, 2)
    across = {2: lax.rem(ch + 2, 4)}
    across[1] = ch + 1 - 2 * bit
    across[3] = lax.rem(across[1] + 2, 4)
    pair = lax.rem(dp, 2)
    twin = dp + 1 - 2 * pair
    rank_q = lax.div(dp, 2)
    nq = n // 2
    has_next = dp + 1 < n
    has_prev = dp > 0
    q_cols = pl.ds(pl.multiple_of(ch * quarter, quarter), quarter)
    h_mine = pl.ds(pl.multiple_of(bit * half, half), half)
    h_other = pl.ds(pl.multiple_of((1 - bit) * half, half), half)

    drains = []
    counter = [0]

    def alloc(count):
        base = counter[0]
        counter[0] += count
        return base

    def remote(src, dst, index, target):
        return pltpu.make_async_remote_copy(
            src_ref=src,
            dst_ref=dst,
            send_sem=v.ss.at[index],
            recv_sem=v.rs.at[index],
            device_id=target,
            device_id_type=MESH,
        )

    def send(src, dst, target):
        copy = remote(src, dst, alloc(1), target)
        copy.start()
        drains.append(copy.wait_send)
        return copy

    def bundle(total, index):
        return remote(total, total, index, (dp, across[1]))

    def send_all(copies, total):
        index = alloc(1)
        for src, dst, target in copies:
            remote(src, dst, index, target).start()
        whole = bundle(total, index)
        drains.append(whole.wait_send)
        return whole

    def chan_send(src, dst, total):
        return send_all([(src, dst, (dp, across[p])) for p in (2, 3, 1)], total)

    def edge_send(groups, step):
        there, here = (has_next, has_prev) if step > 0 else (has_prev, has_next)
        wholes = []
        for copies, total in groups:
            index = alloc(1)
            wholes.append(bundle(total, index))

            @pl.when(there)
            def _():
                for src, dst, chan in copies:
                    remote(src, dst, index, (dp + step, chan)).start()

        def drain():
            @pl.when(there)
            def _():
                for whole in wholes:
                    whole.wait_send()

        drains.append(drain)

        def arrive():
            @pl.when(here)
            def _():
                for whole in wholes:
                    whole.wait_recv()

        return arrive

    def dp_send_all(src_of, dst, total):
        index = alloc(1)

        def body(o, carry):
            to = lax.rem(dp + o, n)
            remote(src_of(to), dst, index, (to, ch)).start()
            return carry

        lax.fori_loop(1, n, body, 0)
        whole = bundle(total, index)
        drains.append(whole.wait_send)
        return whole.wait_recv

    def dp_send(src, dst, base, low, high):
        def copy_of(o):
            return remote(src, dst, base + o - 1, (lax.rem(dp + o, n), ch))

        def each(act):
            def body(o, carry):
                act(copy_of(o))
                return carry

            return body

        lax.fori_loop(low, high, each(lambda copy: copy.start()), 0)
        drains.append(
            lambda: lax.fori_loop(low, high, each(lambda copy: copy.wait_send()), 0)
        )

        def arrive(first, last):
            lax.fori_loop(first, last, each(lambda copy: copy.wait_recv()), 0)

        return arrive

    ring = nq == 4
    inner = (rank_q == 1) | (rank_q == 2)

    def gather(src, place, total):
        first, middle, second = alloc(1), alloc(1), alloc(1)
        local = pltpu.make_async_copy(src, place(dp), v.ls.at[alloc_local()])
        local.start()
        steps = (1, nq - 1) if ring else tuple(range(1, nq))
        heard = len(steps)

        def even(q):
            return q * 2 + pair

        def pass_on(q, to, index):
            remote(place(even(q)), place(even(q)), index, to).start()

        if ring:
            for o in steps:
                to = even(lax.rem(rank_q + o, nq))
                remote(src, place(dp), first, (to, ch)).start()
        else:

            def start(o, carry):
                to = even(lax.rem(rank_q + o, nq))
                remote(src, place(dp), first, (to, ch)).start()
                return carry

            lax.fori_loop(1, nq, start, 0)
        remote(src, place(dp), second, (twin, ch)).start()

        def relay1():
            bundle(total(heard), first).wait_recv()
            if ring:

                @pl.when(inner)
                def _():
                    pass_on(rank_q - 1, (even(rank_q + 1), ch), middle)
                    pass_on(rank_q + 1, (even(rank_q - 1), ch), middle)

                for o in steps:
                    pass_on(lax.rem(rank_q + o, nq), (twin, ch), second)
            else:

                def body(o, carry):
                    pass_on(lax.rem(rank_q + o, nq), (twin, ch), second)
                    return carry

                lax.fori_loop(1, nq, body, 0)

        def relay2():
            if ring:
                bundle(total(1), middle).wait_recv()
                pass_on(lax.rem(rank_q + 2, nq), (twin, ch), second)

        def finish():
            bundle(total(heard), first).wait_send()
            if ring:

                @pl.when(inner)
                def _():
                    bundle(total(2), middle).wait_send()

            bundle(total(nq), second).wait()
            local.wait()

        return SimpleNamespace(relay1=relay1, relay2=relay2, finish=finish)

    locals_used = [2 * z.layers + 10]

    def alloc_local():
        locals_used[0] += 1
        return locals_used[0] - 1

    loads = []
    for l in range(z.layers):
        loads.append(
            (
                pltpu.make_async_copy(
                    v.w_in.at[pl.ds(l * d * z.span, d * z.span), :],
                    v.raw,
                    v.ls.at[2 * l],
                ),
                pltpu.make_async_copy(v.w_out.at[l], v.wo.at[l], v.ls.at[2 * l + 1]),
            )
        )
        loads[l][1].start()
    loads[0][0].start()

    def load_in(l):
        loads[l][0].wait()
        rows = LANES * z.span

        def body(k, carry):
            at = pl.ds(pl.multiple_of(k * rows, rows), rows)
            to = pl.ds(pl.multiple_of(k * LANES, LANES), LANES)
            v.stage[...] = v.raw[at, :].astype(F32)
            for g in range(groups):
                for side_of in range(2):
                    col = side_of * c + g * LANES
                    v.wi[l, to, col : col + LANES] = v.stage[
                        pl.ds(2 * g + side_of, LANES, stride=z.span), :
                    ].astype(BF16)
            return carry

        lax.fori_loop(0, d // LANES, body, 0)
        if l + 1 < z.layers:
            loads[l + 1][0].start()

    barrier = pltpu.get_barrier_semaphore()
    for p in (1, 2, 3):
        pl.semaphore_signal(
            barrier, inc=1, device_id=(dp, across[p]), device_id_type=MESH
        )

    def greet(o, carry):
        pl.semaphore_signal(
            barrier, inc=1, device_id=(lax.rem(dp + o, n), ch), device_id_type=MESH
        )
        return carry

    lax.fori_loop(1, n, greet, 0)
    for step in (1, n - 1):
        for p in (1, 2, 3):
            pl.semaphore_signal(
                barrier,
                inc=1,
                device_id=(lax.rem(dp + step, n), across[p]),
                device_id_type=MESH,
            )

    xq = v.x[...]
    v.hq[...] = (xq * v.gain[0:1, :]).astype(BF16)
    v.meta[...] = jnp.zeros_like(v.meta)
    v.meta[0 : z.layers, :] = v.gain[...]
    v.meta[8:16, 0:t] = dot(
        jnp.ones((8, quarter), F32), xq * xq, ((1,), (1,)), lax.Precision.HIGHEST
    )
    mask = jnp.broadcast_to(v.mask[...].astype(F32), (8, t))
    cot = v.probe[...] * jnp.transpose(mask)[:, 0:1]
    v.cot[...] = cot
    v.cq[...] = cot.astype(BF16)

    @pl.when(jnp.logical_not(has_prev))
    def _():
        L[0].hid[0:HALO, :] = jnp.zeros((HALO, d), BF16)
        L[0].xs[0:HALO, :] = jnp.zeros((HALO, d), F32)
        v.metah[...] = jnp.zeros_like(v.metah)
        v.b_halo[...] = jnp.zeros_like(v.b_halo)

    @pl.when(jnp.logical_not(has_next))
    def _():
        for l in range(z.layers):
            L[l].bhalo[...] = jnp.zeros_like(L[l].bhalo)
            L[l].eland[...] = jnp.zeros_like(L[l].eland)

    pl.semaphore_wait(barrier, 3 + (n - 1) + 6)

    own = pl.ds(HALO, t)
    head = pl.ds(0, HALO)
    tail = pl.ds(t - HALO, HALO)
    everyone = [ch, across[1], across[2], across[3]]
    got_h = chan_send(
        v.hq, L[0].hid.at[own, q_cols], L[0].hid.at[own, 0 : 3 * quarter]
    )
    got_m = chan_send(v.meta, v.metas.at[ch], v.metas.at[0 : z.nch - 1])
    got_edge = edge_send(
        [
            (
                [(v.hq.at[tail, :], L[0].hid.at[head, q_cols], k) for k in everyone],
                L[0].hid.at[head, :],
            ),
            ([(v.meta, v.metah.at[ch], k) for k in everyone], v.metah),
        ],
        1,
    )
    L[0].hid[own, q_cols] = v.hq[...]
    v.metas[ch] = v.meta[...]
    L[0].xs[own, q_cols] = xq
    L[1].gq[:, q_cols] = v.cq[...]
    L[1].g[:, q_cols] = cot

    position = dp * t + lax.broadcasted_iota(jnp.int32, (ext, LANES), 0)
    first = jnp.zeros((ext, LANES), jnp.int32)
    start = jnp.int32(0)
    for s in range(v.lengths.shape[0]):
        first = jnp.where(position >= start, start, first)
        start = start + v.lengths[s]
    offset = position - first
    for k in range(z.taps - 1):
        v.vm[k] = jnp.where(offset >= z.taps - 1 - k, 1.0, 0.0).astype(F32)

    def valid(k, rows, width):
        return wide(v.vm[k, rows, :], width)

    def a_of(l):
        return -jnp.exp(v.a_log[l])

    def lane(g):
        return slice(g * LANES, (g + 1) * LANES)

    def fwd_head(l):
        hid, inv = L[l].hid, L[l].inv
        inner = dot(hid[...], v.wi[l, :, 0:c])
        if l == 0:
            inner = wide(inv[...], c) * inner
        inner = inner.astype(BF16).astype(F32)
        L[l].inner[...] = inner
        conv = jnp.broadcast_to(v.conv_b[l : l + 1, :], (t, c))
        for k in range(z.taps):
            at = HALO - z.taps + 1 + k
            term = v.conv_w[l, k : k + 1, :] * L[l].inner[at : at + t, :]
            conv = conv + (term if k == z.taps - 1 else term * valid(k, slice(0, t), c))
        sig = jax.nn.sigmoid(conv)
        act = (conv * sig).astype(BF16)
        L[l].act[...] = act
        L[l].actf[...] = act.astype(F32)
        part = dot(v.w_x[l], act, ((1,), (1,))).astype(BF16)
        L[l].psend[...] = part
        land = L[l].pland
        got = chan_send(L[l].psend, land.at[ch], land.at[0 : z.nch - 1])
        L[l].pland[ch] = part
        L[l].slope[...] = silu_slope(conv, sig)
        gate = dot(hid[own, :], v.wi[l, :, c : 2 * c])
        if l == 0:
            gate = wide(inv[own, :], c) * gate
        gate = gate.astype(BF16)
        L[l].gate[...] = gate.astype(F32)
        return got

    def fwd_mid(l, got):
        got.wait_recv()
        land = L[l].pland
        proj = land[0].astype(F32)
        for k in range(1, z.nch):
            proj = proj + land[k].astype(F32)
        stept = proj[0:rank, :].astype(BF16)
        L[l].stept[...] = stept
        pre = dot(stept, v.w_dt[l], ((0,), (0,))) + v.dt_b[l : l + 1, :]
        step = jnp.maximum(pre, 0.0) + jnp.log1p(jnp.exp(-jnp.abs(pre)))
        stepk = step + (1.0 - valid(z.taps - 2, slice(0, t), c)) * RESET
        L[l].pre[...] = pre
        L[l].step[...] = step
        L[l].stepk[...] = stepk
        L[l].u[...] = step * L[l].actf[...]
        summed = jnp.sum(stepk, axis=0, keepdims=True)
        L[l].ssend[...] = jnp.zeros((8, LANES), F32)
        for g in range(groups):
            L[l].ssend[g : g + 1, :] = summed[:, lane(g)]
        land = L[l].ssum
        got_s = dp_send_all(lambda to: L[l].ssend, land.at[dp], land.at[0 : n - 1])
        bc = proj[rank : rank + 2 * ns, :]
        lanes = lax.broadcasted_iota(jnp.int32, (2 * ns, t), 1)
        bce = L[l].bce

        def spread(block, carry):
            for i in range(ROWS):
                tok = block * ROWS + i
                column = jnp.sum(
                    jnp.where(lanes == tok, bc, 0.0), axis=1, keepdims=True
                )
                bce[tok] = jnp.broadcast_to(column, (2 * ns, LANES))
            return carry

        lax.fori_loop(0, t // ROWS, spread, 0)
        return got_s

    def scan_sum(l):
        a = a_of(l)
        stepk, u, bce, dec = L[l].stepk, L[l].u, L[l].bce, L[l].dec

        def body(block, state):
            state = list(state)
            rows = pl.ds(pl.multiple_of(block * ROWS, ROWS), ROWS)
            sk, uu = stepk[rows, :], u[rows, :]
            for i in range(ROWS):
                tok = block * ROWS + i
                b = bce[tok, 0:ns, :]
                for g in range(groups):
                    e = jnp.exp(sk[i : i + 1, lane(g)] * a[:, lane(g)])
                    dec[tok, :, lane(g)] = e
                    state[g] = e * state[g] + uu[i : i + 1, lane(g)] * b
            return tuple(state)

        zero = jnp.zeros((ns, LANES), F32)
        return lax.fori_loop(0, t // ROWS, body, (zero,) * groups)

    def back_sum(l):
        ds, bce, dec = L[l].ds, L[l].bce, L[l].dec

        def body(k, flow):
            flow = list(flow)
            block = t // ROWS - 1 - k
            rows = pl.ds(pl.multiple_of(block * ROWS, ROWS), ROWS)
            dd = ds[rows, :]
            for i in reversed(range(ROWS)):
                tok = block * ROWS + i
                cc = bce[tok, ns : 2 * ns, :]
                for g in range(groups):
                    lam = cc * dd[i : i + 1, lane(g)] + flow[g]
                    flow[g] = dec[tok, :, lane(g)] * lam
            return tuple(flow)

        zero = jnp.zeros((ns, LANES), F32)
        return lax.fori_loop(0, t // ROWS, body, (zero,) * groups)

    def put(ref, k, parts):
        for g in range(groups):
            ref[k, :, lane(g)] = parts[g].astype(BF16)

    def carry_in(l, land, order, count):
        a = a_of(l)

        def body(k, carry):
            j = order(k)
            row = jnp.concatenate(
                [L[l].ssum[j, g : g + 1, :] for g in range(groups)], axis=1
            )
            return jnp.exp(a * row) * carry + land[j].astype(F32)

        return lax.fori_loop(0, count, body, jnp.zeros((ns, c), F32))

    def scan_out(l, carry):
        u, bce, dec, st = L[l].u, L[l].bce, L[l].dec, L[l].st
        y = L[l].scan
        st[0] = carry

        def body(block, state):
            state = list(state)
            rows = pl.ds(pl.multiple_of(block * ROWS, ROWS), ROWS)
            uu = u[rows, :]
            outs = [[] for _ in range(groups)]
            for i in range(ROWS):
                tok = block * ROWS + i
                b = bce[tok, 0:ns, :]
                cc = bce[tok, ns : 2 * ns, :]
                for g in range(groups):
                    s = dec[tok, :, lane(g)] * state[g] + uu[i : i + 1, lane(g)] * b
                    st[tok + 1, :, lane(g)] = s
                    state[g] = s
                    outs[g].append(jnp.sum(cc * s, axis=0, keepdims=True))
            for g in range(groups):
                y[rows, lane(g)] = jnp.concatenate(outs[g], axis=0)
            return tuple(state)

        lax.fori_loop(
            0, t // ROWS, body, tuple(carry[:, lane(g)] for g in range(groups))
        )
        scanned = y[...] + v.skip[l : l + 1, :] * L[l].actf[...]
        y[...] = scanned
        L[l].sct[...] = jnp.transpose(scanned.astype(BF16))
        gate = L[l].gate[...]
        gated = (scanned * gate * jax.nn.sigmoid(gate)).astype(BF16)
        L[l].gated[...] = gated
        return gated

    def reduce_a(k, part_of):
        send_ref, keep_ref = R[k].a_send, R[k].full
        send_ref[...] = part_of(h_other).astype(BF16)
        got = send(send_ref, R[k].a_land, (dp, across[1]))
        keep_ref[own, h_mine] = part_of(h_mine)
        return got

    def reduce_b(k, got, edge):
        got.wait_recv()
        b_send = R[k].b_send
        b_send[...] = (
            R[k].full[own, h_mine]
            + R[k].a_land[...].astype(F32)
        ).astype(BF16)
        got = send(b_send, R[k].b_land, (dp, across[2]))
        arrive = None
        if edge:
            arrive = edge_send(
                [
                    (
                        [
                            (b_send.at[tail, :], v.b_halo.at[side], chan)
                            for chan in (ch, across[2])
                        ],
                        v.b_halo,
                    )
                ],
                1,
            )
        return got, arrive

    def reduce_c(k, got, arrive):
        got.wait_recv()
        full = R[k].full
        full[own, h_mine] = R[k].b_send[...].astype(F32) + R[k].b_land[...].astype(F32)
        region = full.at[own, h_mine]
        if arrive is not None:
            arrive()
            full[head, h_mine] = v.b_halo[0].astype(F32) + v.b_halo[1].astype(F32)
            region = full.at[:, h_mine]
        return send(region, region, (dp, across[1]))

    def reduce_all(k, part_of, edge=False):
        a = reduce_a(k, part_of)
        b, arrive = reduce_b(k, a, edge)
        reduce_c(k, b, arrive).wait_recv()

    def out_part(l):
        return lambda cols: dot(L[l].gated[...], v.wo[l, :, cols])

    def in_part(l):
        return lambda cols: dot(L[l].dm[...], v.wi[l, cols, :], ((1,), (1,)))

    def back_gate(l):
        dgated = dot(L[l].gq[...], v.wo[l], ((1,), (1,)))
        gate = L[l].gate[...]
        v.dgated[...] = dgated
        L[l].ds[...] = dgated * gate * jax.nn.sigmoid(gate)

    def back_dgate(l):
        gate = L[l].gate[...]
        sig = jax.nn.sigmoid(gate)
        dgate = v.dgated[...] * L[l].scan[...] * silu_slope(gate, sig)
        L[l].dm[:, c : 2 * c] = dgate.astype(BF16)

    def back_scan(l, flow_in):
        a = a_of(l)
        ds, u, bce, dec, st = L[l].ds, L[l].u, L[l].bce, L[l].dec, L[l].st
        stepk, actf = L[l].stepk, L[l].actf
        lanes = lax.broadcasted_iota(jnp.int32, (ns, t), 1)

        def body(k, carry):
            flow, acc, acc_b, acc_c = list(carry[0]), list(carry[1]), carry[2], carry[3]
            block = t // ROWS - 1 - k
            rows = pl.ds(pl.multiple_of(block * ROWS, ROWS), ROWS)
            dd, uu, sk, aa = ds[rows, :], u[rows, :], stepk[rows, :], actf[rows, :]
            d_step = [[] for _ in range(groups)]
            d_adj = [[] for _ in range(groups)]
            for i in reversed(range(ROWS)):
                tok = block * ROWS + i
                b = bce[tok, 0:ns, :]
                cc = bce[tok, ns : 2 * ns, :]
                sum_b = jnp.zeros((ns, LANES), F32)
                sum_c = jnp.zeros((ns, LANES), F32)
                for g in range(groups):
                    drow = dd[i : i + 1, lane(g)]
                    lam = cc * drow + flow[g]
                    flow[g] = dec[tok, :, lane(g)] * lam
                    rate = flow[g] * st[tok, :, lane(g)]
                    acc[g] = acc[g] + rate * sk[i : i + 1, lane(g)]
                    adj = jnp.sum(lam * b, axis=0, keepdims=True)
                    d_adj[g].insert(0, adj)
                    d_step[g].insert(
                        0,
                        jnp.sum(rate * a[:, lane(g)], axis=0, keepdims=True)
                        + adj * aa[i : i + 1, lane(g)],
                    )
                    sum_b = sum_b + lam * uu[i : i + 1, lane(g)]
                    sum_c = sum_c + st[tok + 1, :, lane(g)] * drow
                acc_b = jnp.where(
                    lanes == tok, jnp.sum(sum_b, axis=1, keepdims=True), acc_b
                )
                acc_c = jnp.where(
                    lanes == tok, jnp.sum(sum_c, axis=1, keepdims=True), acc_c
                )
            for g in range(groups):
                v.dst[rows, lane(g)] = jnp.concatenate(d_step[g], axis=0)
                v.adj[rows, lane(g)] = jnp.concatenate(d_adj[g], axis=0)
            return (tuple(flow), tuple(acc), acc_b, acc_c)

        zero = jnp.zeros((ns, LANES), F32)
        _, acc, acc_b, acc_c = lax.fori_loop(
            0,
            t // ROWS,
            body,
            (
                tuple(flow_in[:, lane(g)] for g in range(groups)),
                (zero,) * groups,
                jnp.zeros((ns, t), F32),
                jnp.zeros((ns, t), F32),
            ),
        )
        for g in range(groups):
            L[l].packs[0][rank : rank + ns, lane(g)] = acc[g] * a[:, lane(g)]
        return acc_b, acc_c

    def back_mid(l, acc_b, acc_c):
        pack = L[l].packs[0]
        actf = L[l].actf[...]
        ds = L[l].ds[...]
        dpre = v.dst[...] * jax.nn.sigmoid(L[l].pre[...])
        dpre_q = dpre.astype(BF16)
        bsend = L[l].bsend
        bsend[0:rank, :] = dot(v.w_dt[l], dpre_q, ((1,), (1,))).astype(BF16)
        bsend[rank : rank + ns, :] = acc_b.astype(BF16)
        bsend[rank + ns : rank + 2 * ns, :] = acc_c.astype(BF16)
        land = L[l].bland
        got = chan_send(bsend, land.at[ch], land.at[0 : z.nch - 1])
        land[ch] = bsend[...]
        dact = ds * v.skip[l : l + 1, :] + L[l].step[...] * v.adj[...]
        v.dact[...] = dact
        L[l].esend[0:HALO, :] = dact[0:HALO, :]
        L[l].esend[HALO : 2 * HALO, :] = L[l].slope[0:HALO, :]
        edge = edge_send(
            [
                ([(L[l].esend, L[l].eland, ch)], L[l].eland),
                ([(bsend, L[l].bhalo.at[ch], k) for k in everyone], L[l].bhalo),
            ],
            -1,
        )
        pack[0:rank, :] = dot(L[l].stept[...], dpre_q)
        at = rank + ns
        pack[at : at + 1, :] = jnp.sum(dpre, axis=0, keepdims=True)
        pack[at + 1 : at + 2, :] = jnp.sum(ds * actf, axis=0, keepdims=True)
        pack[at + 2 :, :] = jnp.zeros((z.pack - at - 2, c), F32)
        return got, edge

    def sum_land(ref):
        total = ref[0].astype(F32)
        for k in range(1, z.nch):
            total = total + ref[k].astype(F32)
        return total.astype(BF16)

    def back_conv(l, got, edge):
        got.wait_recv()
        edge()
        dproj = sum_land(L[l].bland)
        dproj_h = sum_land(L[l].bhalo)
        wx = v.w_x[l]
        dact = v.dact[...] + dot(dproj, wx, ((0,), (0,)))
        dconv = dact * L[l].slope[...]
        v.dc[0:t, :] = dconv
        eland = L[l].eland
        after = dot(dproj_h, wx, ((0,), (0,)))[0:HALO, :]
        v.dc[t:ext, :] = (eland[0:HALO, :] + after) * eland[HALO : 2 * HALO, :]
        dinner = jnp.zeros((t, c), F32)
        for k in range(z.taps):
            at = z.taps - 1 - k
            rows = slice(at, at + t)
            term = v.dc[rows, :] * v.conv_w[l, k : k + 1, :]
            dinner = dinner + (
                term if k == z.taps - 1 else term * valid(k, rows, c)
            )
        L[l].dm[:, 0:c] = dinner.astype(BF16)
        return dproj

    def back_rest(l, dproj):
        pack = L[l].packs[1]
        pack[0 : z.xdim, :] = dot(dproj, L[l].act[...])
        dconv = v.dc[0:t, :]
        at = z.xdim
        for k in range(z.taps):
            row = HALO - z.taps + 1 + k
            term = dconv * L[l].inner[row : row + t, :]
            if k < z.taps - 1:
                term = term * valid(k, slice(0, t), c)
            pack[at + k : at + k + 1, :] = jnp.sum(term, axis=0, keepdims=True)
        at = at + z.taps
        pack[at : at + 1, :] = jnp.sum(dconv, axis=0, keepdims=True)
        pack[at + 1 :, :] = jnp.zeros((z.pack - at - 1, c), F32)

    def back_norm(l, k):
        inv = wide(L[l].inv[own, :], d)
        u = R[k].full[own, :] * inv
        x = L[l].xs[own, :]
        scaled = u * v.gfull[l : l + 1, :]
        xhat = x * inv
        mean = jnp.sum(scaled * xhat, axis=1, keepdims=True) * (1.0 / d)
        v.grow[...] = jnp.broadcast_to(jnp.sum(u * x, axis=0, keepdims=True), (8, d))
        L[l].gnsend[...] = v.grow[:, q_cols]
        L[l].gnland[dp] = v.grow[:, q_cols]
        land = L[l].gnland
        arrive = dp_send_all(lambda to: L[l].gnsend, land.at[dp], land.at[0 : n - 1])
        return L[l].g[...] + scaled - xhat * mean, arrive

    def gain_out(l, arrive):
        arrive()
        total = lax.fori_loop(
            0, n, lambda j, s: s + L[l].gnland[j], jnp.zeros((8, quarter), F32)
        )
        v.gains[l : l + 1, :] = total[0:1, :]

    def rows_of(first, count):
        return pl.ds(pl.multiple_of(first, count), count)

    def small_sum(l, p):
        if not z.shared:
            v.smalls[l, p] = L[l].packs[p][...]
            nothing = lambda: None
            return SimpleNamespace(b=nothing, c=nothing, d=nothing, out=nothing)
        rows, part = z.piece, z.pack // 2
        pack, packed, tland = L[l].packs[p], L[l].packed[p], L[l].tland[p]
        land, small = L[l].rsland[p], L[l].small[p]
        mine, other = rows_of(pair * part, part), rows_of((1 - pair) * part, part)
        place = rows_of(pair * part + rank_q * rows, rows)
        packed[other, :] = pack[other, :].astype(BF16)
        got_a = send(packed.at[other, :], tland, (twin, ch))
        state = {}

        def even_send(src_of, dst, total):
            index = alloc(1)

            def body(o, carry):
                q = lax.rem(rank_q + o, nq)
                remote(src_of(q), dst, index, (q * 2 + pair, ch)).start()
                return carry

            lax.fori_loop(1, nq, body, 0)
            whole = bundle(total, index)
            drains.append(whole.wait_send)
            return whole

        def b():
            got_a.wait_recv()
            packed[mine, :] = (pack[mine, :] + tland[...].astype(F32)).astype(BF16)
            piece = lambda q: rows_of(pair * part + q * rows, rows)
            state[0] = even_send(
                lambda q: packed.at[piece(q), :],
                land.at[rank_q],
                land.at[0 : nq - 1],
            )
            land[rank_q] = packed[place, :]

        def c_():
            state[0].wait_recv()
            total = land[0].astype(F32)
            for k in range(1, nq):
                total = total + land[k].astype(F32)
            small[place, :] = total.astype(BF16)
            state[1] = even_send(
                lambda q: small.at[place, :],
                small.at[place, :],
                small.at[0 : (nq - 1) * rows, :],
            )

        def d_():
            state[1].wait_recv()
            state[2] = send(small.at[mine, :], small.at[mine, :], (twin, ch))

        def out():
            state[2].wait_recv()
            v.smalls[l, p] = small[...]

        return SimpleNamespace(b=b, c=c_, d=d_, out=out)

    def inverse(total):
        return lax.rsqrt(total * (1.0 / d) + EPSILON)

    def norms():
        sums, sums_h = v.metas[0, 8:16, 0:t], v.metah[0, 8:16, 0:t]
        v.gfull[:, 0:quarter] = v.metas[0, 0:8, :]
        for k in range(1, z.nch):
            sums = sums + v.metas[k, 8:16, 0:t]
            sums_h = sums_h + v.metah[k, 8:16, 0:t]
            v.gfull[:, k * quarter : (k + 1) * quarter] = v.metas[k, 0:8, :]
        L[0].inv[own, :] = jnp.broadcast_to(
            jnp.transpose(inverse(sums))[:, 0:1], (t, LANES)
        )
        L[0].inv[head, :] = jnp.broadcast_to(
            jnp.transpose(inverse(sums_h))[t - HALO : t, 0:1], (HALO, LANES)
        )

    def in_lanes(src, ref, l, rows):
        return gather(
            src,
            lambda j: ref.at[l, rows, pl.ds(pl.multiple_of(j * t, t), t)],
            lambda count: ref.at[l, rows, 0 : count * t],
        )

    def in_rows(src, ref, l, cols, low=0, high=t):
        m = high - low
        return gather(
            src,
            lambda j: ref.at[l, pl.ds(pl.multiple_of(j * t + low, m), m), cols],
            lambda count: ref.at[l, 0 : count * m, cols],
        )

    def gather_hid(l):
        if l == 0:
            hidden = xq * v.gain[0:1, :] * wide(L[0].inv[own, :], quarter)
            L[0].ht[...] = jnp.transpose(hidden.astype(BF16))
        else:
            L[l].ht[...] = jnp.transpose(L[l].hid[own, q_cols])
        return in_lanes(L[l].ht, v.hid_all, l, q_cols)

    def gather_scan(l):
        return in_lanes(L[l].sct, v.scan_all, l, slice(None))

    def gather_gq(l):
        return in_rows(L[l].gq.at[:, q_cols], v.gq_all, l, q_cols)

    def gather_dmi(l, low=0, high=t):
        src = L[l].dm.at[low:high, 0:c]
        return in_rows(src, v.dmi_all, l, slice(None), low, high)

    def quarter_at(k):
        return pl.ds(pl.multiple_of(k * quarter, quarter), quarter)

    def share(region, total):
        mine = region(ch)
        got = send(mine, mine, (dp, across[2]))

        def second():
            got.wait_recv()
            theirs = region(across[2])
            to = (dp, across[1])
            return send_all([(mine, mine, to), (theirs, theirs, to)], total).wait_recv

        return second

    def share_hid(l):
        return share(
            lambda k: v.hid_all.at[l, quarter_at(k), :],
            v.hid_all.at[l, 0 : 2 * quarter, :],
        )

    def share_gq(l):
        return share(
            lambda k: v.gq_all.at[l, :, quarter_at(k)],
            v.gq_all.at[l, :, 0 : 2 * quarter],
        )

    def share_rows(ref, rows):
        return share(lambda k: ref.at[rows, quarter_at(k)], ref.at[rows, 0 : 2 * quarter])

    chunks = z.total // z.chunk

    def chunk_loads(l, k):
        slot = lax.rem(k, 2)
        base = 2 * z.layers + 5 * slot
        at = pl.ds(pl.multiple_of(k * z.chunk, z.chunk), z.chunk)
        pairs = (
            (v.hid_all.at[l, :, at], v.hidc.at[slot]),
            (v.gq_all.at[l, at, :], v.gqc.at[slot]),
            (v.scan_all.at[l, :, at], v.scanc.at[slot]),
        )
        return [
            pltpu.make_async_copy(src, to, v.ls.at[base + i])
            for i, (src, to) in enumerate(pairs)
        ]

    def chunk_stores(l, k):
        slot = lax.rem(k, 2)
        base = 2 * z.layers + 5 * slot + 3
        at = pl.ds(pl.multiple_of(k * z.chunk, z.chunk), z.chunk)
        pairs = (
            (v.gatc.at[slot], v.gat_all.at[l, :, at]),
            (v.dmgc.at[slot], v.dmg_all.at[l, :, at]),
        )
        return [
            pltpu.make_async_copy(src, to, v.ls.at[base + i])
            for i, (src, to) in enumerate(pairs)
        ]

    def finish_begin(l):
        for copy in chunk_loads(l, jnp.int32(0)):
            copy.start()

    def finish_some(l, low, high):
        def body(k, carry):
            slot = lax.rem(k, 2)

            @pl.when(k + 1 < chunks)
            def _():
                for copy in chunk_loads(l, k + 1):
                    copy.start()

            @pl.when(k >= 2)
            def _():
                for copy in chunk_stores(l, k - 2):
                    copy.wait()

            loads_in = chunk_loads(l, k)
            loads_in[0].wait()
            w_gate = v.wi[l, :, c : 2 * c]
            gate = dot(w_gate, v.hidc[slot], ((0,), (0,))).astype(BF16).astype(F32)
            loads_in[1].wait()
            dgated = dot(v.wo[l], v.gqc[slot], ((1,), (1,)))
            loads_in[2].wait()
            scanned = v.scanc[slot].astype(F32)
            sig = jax.nn.sigmoid(gate)
            v.gatc[slot] = (scanned * gate * sig).astype(BF16)
            v.dmgc[slot] = (dgated * scanned * silu_slope(gate, sig)).astype(BF16)
            for copy in chunk_stores(l, k):
                copy.start()
            return carry

        lax.fori_loop(low, high, body, 0)

    def finish_end(l):
        for k in range(max(chunks - 2, 0), chunks):
            for copy in chunk_stores(l, jnp.int32(k)):
                copy.wait()

    load_in(0)
    got_h.wait_recv()
    got_m.wait_recv()
    got_edge()
    norms()
    got_p = fwd_head(0)
    share_x = share_rows(L[0].xs, own)
    share_c = share_rows(L[1].gq, slice(None))
    got_xedge = edge_send(
        [
            (
                [(v.x.at[tail, :], L[0].xs.at[head, q_cols], k) for k in everyone],
                L[0].xs.at[head, :],
            )
        ],
        1,
    )
    hid0 = gather_hid(0)
    gq1 = gather_gq(1)
    load_in(1)
    got_s0 = fwd_mid(0, got_p)
    put(L[0].carry, 0, scan_sum(0))
    got_carry = dp_send(L[0].carry.at[0], L[0].sland.at[dp], alloc(n - 1), 1, n - dp)
    share_x = share_x()
    share_c = share_c()
    share_g = share_rows(L[1].g, slice(None))
    loads[0][1].wait()
    got_s0()
    got_carry(1, dp + 1)
    hid0.relay1()
    gq1.relay1()
    scan_out(0, carry_in(0, L[0].sland, lambda k: k, dp))
    scan0 = gather_scan(0)
    red0 = reduce_a(0, out_part(0))
    red0, arrive = reduce_b(0, red0, True)
    share_g = share_g()
    got_c = reduce_c(0, red0, arrive)
    hid0.relay2()
    gq1.relay2()
    share_x()
    got_xedge()
    got_c.wait_recv()
    x1 = L[0].xs[...] + R[0].full[...]
    L[1].xs[...] = x1
    inv1 = inverse(jnp.sum(x1 * x1, axis=1, keepdims=True))
    L[1].hid[...] = (x1 * inv1 * v.gfull[1:2, :]).astype(BF16)
    L[1].inv[...] = jnp.broadcast_to(inv1, (ext, LANES))

    got_p = fwd_head(1)
    hid1 = gather_hid(1)
    scan0.relay1()
    loads[1][1].wait()
    share_c()
    back_gate(1)
    got_s1 = fwd_mid(1, got_p)
    scan0.relay2()
    hid0.finish()
    share0 = share_hid(0)
    gq1.finish()
    share1 = share_gq(1)
    put(L[1].carry, 0, scan_sum(1))
    put(L[1].carry, 1, back_sum(1))
    base = alloc(n - 1)
    got_f = dp_send(L[1].carry.at[0], L[1].sland.at[dp], base, 1, n - dp)
    got_r = dp_send(L[1].carry.at[1], L[1].rland.at[dp], base, n - dp, n)
    got_s1()
    got_f(1, dp + 1)
    got_r(dp + 1, n)
    hid1.relay1()
    scan_out(1, carry_in(1, L[1].sland, lambda k: k, dp))
    scan1 = gather_scan(1)
    back_dgate(1)
    red1 = reduce_a(1, out_part(1))
    hid1.relay2()

    acc_b, acc_c = back_scan(1, carry_in(1, L[1].rland, lambda k: n - 1 - k, n - 1 - dp))
    got_b, edge = back_mid(1, acc_b, acc_c)
    share0 = share0()
    share1 = share1()
    scan1.relay1()
    dproj = back_conv(1, got_b, edge)
    red2 = reduce_a(2, in_part(1))
    dmi1 = gather_dmi(1)
    back_rest(1, dproj)
    red2, _ = reduce_b(2, red2, False)
    red1, _ = reduce_b(1, red1, False)
    scan1.relay2()
    red2 = reduce_c(2, red2, None)
    hid1.finish()
    share_g()
    red2.wait_recv()
    share2 = share_hid(1)
    grad, gain1 = back_norm(1, 2)
    L[0].g[...] = grad
    L[0].gq[...] = grad.astype(BF16)

    gq0 = gather_gq(0)
    back_gate(0)
    put(L[0].carry, 1, back_sum(0))
    got_r = dp_send(L[0].carry.at[1], L[0].rland.at[dp], alloc(n - 1), n - dp, n)
    gq0.relay1()
    back_dgate(0)
    reduce_c(1, red1, None).wait_recv()
    v.block_out[...] = L[1].xs[own, q_cols] + R[1].full[own, q_cols]
    share0()
    share1()
    got_r(dp + 1, n)
    gq0.relay2()
    dmi1.relay1()
    small1 = [small_sum(1, 0), small_sum(1, 1)]
    acc_b, acc_c = back_scan(0, carry_in(0, L[0].rland, lambda k: n - 1 - k, n - 1 - dp))
    got_b, edge = back_mid(0, acc_b, acc_c)
    share2 = share2()
    small0 = [small_sum(0, 0)]
    dmi1.relay2()
    share2()
    scan1.finish()
    finish_begin(1)
    gq0.finish()
    finish_some(1, 0, chunks // 2)
    dproj = back_conv(0, got_b, edge)
    dmi0 = [gather_dmi(0, 0, t // 2), gather_dmi(0, t // 2, t)]
    share3 = share_gq(0)
    red3 = reduce_a(3, in_part(0))
    back_rest(0, dproj)
    small0.append(small_sum(0, 1))
    for one in small1:
        one.b()
    small0[0].b()
    red3, _ = reduce_b(3, red3, False)
    finish_some(1, chunks // 2, 3 * chunks // 4)
    small0[1].b()
    dmi0[0].relay1()
    for one in small1:
        one.c()
    small0[0].c()
    finish_some(1, 3 * chunks // 4, chunks)
    dmi0[1].relay1()
    got_c = reduce_c(3, red3, None)
    small0[1].c()
    share3 = share3()
    got_c.wait_recv()
    grad, gain0 = back_norm(0, 3)
    L[0].g[...] = grad
    v.input_grad[...] = L[0].g[:, q_cols]
    dmi0[0].relay2()
    scan0.finish()
    finish_end(1)
    share3()
    finish_begin(0)
    for one in small1:
        one.d()
    small0[0].d()
    finish_some(0, 0, chunks // 2)
    dmi0[1].relay2()
    small0[1].d()
    finish_some(0, chunks // 2, chunks)
    gain_out(0, gain0)
    gain_out(1, gain1)
    for one in small0 + small1:
        one.out()
    finish_end(0)
    for one in (dmi1, *dmi0):
        one.finish()
    for drain in drains:
        drain()
    assert (counter[0], locals_used[0]) == sems, (counter, locals_used)


def run_blocks(z, args):
    sems = (71 + 3 * (z.ndp - 1) + (16 if z.shared else 0), 23)
    vmem = pl.BlockSpec(memory_space=pltpu.VMEM)
    smem = pl.BlockSpec(memory_space=pltpu.SMEM)
    anywhere = pl.BlockSpec(memory_space=pl.ANY)
    specs = dict.fromkeys(args, vmem) | dict(
        lengths=smem, w_in=anywhere, w_out=anywhere
    )
    t, d, c, n, layers = z.toks, z.width, z.chans, z.total, z.layers
    shape = jax.ShapeDtypeStruct
    outs = dict(
        block_out=(shape((t, z.quarter), F32), vmem),
        input_grad=(shape((t, z.quarter), F32), vmem),
        smalls=(shape((layers, 2, z.pack, c), BF16 if z.shared else F32), vmem),
        gains=(shape((layers, z.quarter), F32), vmem),
        hid_all=(shape((layers, d, n), BF16), anywhere),
        gat_all=(shape((layers, c, n), BF16), anywhere),
        dmg_all=(shape((layers, c, n), BF16), anywhere),
        scan_all=(shape((layers, c, n), BF16), anywhere),
        gq_all=(shape((layers, n, d), BF16), anywhere),
        dmi_all=(shape((layers, n, c), BF16), anywhere),
    )
    scratch = scratch_of(z)
    flags = dict(
        ss=pltpu.SemaphoreType.DMA((sems[0],)),
        rs=pltpu.SemaphoreType.DMA((sems[0],)),
        ls=pltpu.SemaphoreType.DMA((sems[1],)),
    )
    parts = [args, outs, scratch, flags]
    leaf = lambda node: not isinstance(node, (dict, list))
    trees = [jax.tree.flatten(part, is_leaf=leaf) for part in parts]
    whole = jax.tree.structure([dict(part) for part in parts], is_leaf=leaf)

    def kernel(*refs):
        merged = {}
        for part in jax.tree.unflatten(whole, refs):
            merged |= part
        block_kernel(z, sems, merged)

    results = pl.pallas_call(
        kernel,
        out_shape=[one[0] for one in trees[1][0]],
        in_specs=jax.tree.leaves(specs, is_leaf=leaf),
        out_specs=[one[1] for one in trees[1][0]],
        scratch_shapes=trees[2][0] + trees[3][0],
        compiler_params=pltpu.CompilerParams(
            collective_id=0, has_side_effects=True, vmem_limit_bytes=62 * 2**20
        ),
        name="blocks",
    )(*trees[0][0])
    return SimpleNamespace(**jax.tree.unflatten(trees[1][1], results))


def grad_kernel(z, steps, ins, small_ins, win, wout, outs):
    hid, gat, dmg, gq, dmi, smalls = ins
    rows = hid.shape[1]
    first = pl.program_id(2) == 0
    lhs = hid[0]
    parts = (dot(lhs, dmi[0]), dot(lhs, dmg[0], ((1,), (1,))))
    for k, part in enumerate(parts):
        for j in range(z.groups):
            at = pl.ds(j * 2 + k, rows, stride=z.span)
            piece = part[:, j * LANES : (j + 1) * LANES]
            if steps == 1:
                win[at, :] = piece
            else:
                win[at, :] = jnp.where(first, 0.0, win[at, :]) + piece
    part = dot(gat[0], gq[0])
    if steps == 1:
        wout[0] = part
    else:
        wout[0] = jnp.where(first, 0.0, wout[0]) + part

    begin = first & (pl.program_id(0) == 0) & (pl.program_id(1) == 0)
    pl.when(begin)(lambda: small_outputs(z, smalls, small_ins, outs))


def small_outputs(z, smalls, small_ins, outs):
    for src, to in zip(small_ins, outs[:3], strict=True):
        to[...] = src[...]
    at, pack = 0, 0
    for i, to in enumerate(outs[3:]):
        if i == 4:
            at, pack = 0, 1
        for l in range(z.layers):
            if len(to.shape) == 3:
                count = to.shape[1]
                to[l] = smalls[l, pack, at : at + count, :].astype(F32)
            else:
                count = 1
                to[l : l + 1, :] = smalls[l, pack, at : at + 1, :].astype(F32)
        at += count


def grads_at_once(z, ins, small_ins, win, wout, outs, *scratch):
    smalls = ins[5]
    held, (winv, woutv, lsem, ssem) = scratch[:5], scratch[5:]
    layers, d, c = z.layers, z.width, z.chans
    hid, gat, dmg, gq, dmi = held
    loads = {}
    for l in range(layers):
        for i in (1, 3, 0, 4, 2):
            copy = pltpu.make_async_copy(ins[i].at[l], held[i].at[l], lsem.at[5 * l + i])
            copy.start()
            loads[l, i] = copy
    small_outputs(z, smalls, small_ins, outs)
    stores = []

    def leave(src, to):
        copy = pltpu.make_async_copy(src, to, ssem.at[len(stores)])
        copy.start()
        stores.append(copy)

    rows = d // 2
    for l in range(layers):
        loads[l, 1].wait()
        loads[l, 3].wait()
        woutv[l] = dot(gat[l], gq[l])
        leave(woutv.at[l], wout.at[l])
        loads[l, 0].wait()
        loads[l, 4].wait()
        loads[l, 2].wait()
        for half in range(2):
            lhs = hid[l, half * rows : (half + 1) * rows, :]
            base = (l * d + half * rows) * z.span
            for k in range(2):
                if k == 0:
                    part = dot(lhs, dmi[l])
                else:
                    part = dot(lhs, dmg[l], ((1,), (1,)))
                for j in range(z.groups):
                    at = pl.ds(base + j * 2 + k, rows, stride=z.span)
                    winv[at, :] = part[:, j * LANES : (j + 1) * LANES]
            span = pl.ds(base, rows * z.span)
            leave(winv.at[span, :], win.at[span, :])
    for copy in stores:
        copy.wait()


def weight_grads(z, r):
    blocks = 2
    deep = min(z.total, 1024)
    steps = z.total // deep
    layers, d, c = z.layers, z.width, z.chans
    rows, orow = d // blocks, c // blocks
    shape = jax.ShapeDtypeStruct
    small_shapes = (
        r.block_out,
        r.input_grad,
        r.gains,
        shape((layers, z.rank, c), F32),
        shape((layers, z.states, c), F32),
        shape((layers, c), F32),
        shape((layers, c), F32),
        shape((layers, z.xdim, c), F32),
        shape((layers, z.taps, c), F32),
        shape((layers, c), F32),
    )

    def fixed(one):
        dims = len(one.shape)
        return pl.BlockSpec(one.shape, lambda l, i, k: (0,) * dims)

    def kernel(*refs):
        ins, small_ins, (win, wout), rest = refs[:6], refs[6:9], refs[9:11], refs[11:]
        outs = rest[: len(small_shapes)]
        if steps == 1:
            scratch = rest[len(small_shapes) :]
            grads_at_once(z, ins, small_ins, win, wout, outs, *scratch)
        else:
            grad_kernel(z, steps, ins, small_ins, win, wout, outs)

    out_shape = [
        shape((layers * d * z.span, LANES), F32),
        shape((layers, c, d), F32),
        *[shape(one.shape, F32) for one in small_shapes],
    ]
    in_specs, out_specs, scratch, grid = None, None, (), (layers, blocks, steps)
    if steps == 1:
        grid = ()
        anywhere = [pl.BlockSpec(memory_space=pl.ANY)]
        vmem = [pl.BlockSpec(memory_space=pltpu.VMEM)]
        in_specs = anywhere * 5 + vmem * 4
        out_specs = anywhere * 2 + vmem * len(small_shapes)
        scratch = (
            *[
                pltpu.VMEM(one.shape, BF16)
                for one in (r.hid_all, r.gat_all, r.dmg_all, r.gq_all, r.dmi_all)
            ],
            pltpu.VMEM(out_shape[0].shape, F32),
            pltpu.VMEM(out_shape[1].shape, F32),
            pltpu.SemaphoreType.DMA((5 * layers,)),
            pltpu.SemaphoreType.DMA((3 * layers,)),
        )
    else:
        in_specs = [
            pl.BlockSpec((1, rows, deep), lambda l, i, k: (l, i, k)),
            pl.BlockSpec((1, orow, deep), lambda l, i, k: (l, i, k)),
            pl.BlockSpec((1, c, deep), lambda l, i, k: (l, 0, k)),
            pl.BlockSpec((1, deep, d), lambda l, i, k: (l, k, 0)),
            pl.BlockSpec((1, deep, c), lambda l, i, k: (l, k, 0)),
            fixed(r.smalls),
            fixed(r.block_out),
            fixed(r.input_grad),
            fixed(r.gains),
        ]
        out_specs = [
            pl.BlockSpec((rows * z.span, LANES), lambda l, i, k: (l * blocks + i, 0)),
            pl.BlockSpec((1, orow, d), lambda l, i, k: (l, i, 0)),
            *[fixed(one) for one in small_shapes],
        ]
    win, wout, *rest = pl.pallas_call(
        kernel,
        grid=grid,
        out_shape=out_shape,
        in_specs=in_specs,
        out_specs=out_specs,
        scratch_shapes=scratch,
        compiler_params=pltpu.CompilerParams(vmem_limit_bytes=60 * 2**20),
        name="weight_grads",
    )(
        r.hid_all,
        r.gat_all,
        r.dmg_all,
        r.gq_all,
        r.dmi_all,
        r.smalls,
        r.block_out,
        r.input_grad,
        r.gains,
    )
    win = win.reshape(layers, d, z.groups, 2, LANES).transpose(0, 1, 3, 2, 4)
    return win.reshape(layers, d, 2, c), wout, rest


def local(
    mesh,
    x_in,
    norm_gain,
    in_weight,
    conv_weight,
    conv_bias,
    xproj_weight,
    dt_weight,
    dt_bias,
    a_log,
    skip_gain,
    out_weight,
    seq_lengths,
    char_mask,
    out_probe,
):
    z = sizes_of(mesh, x_in, in_weight, xproj_weight, dt_weight, a_log, conv_weight)
    w_in = in_weight.reshape(z.layers, z.width, 2, z.groups, LANES)
    w_in = w_in.transpose(0, 1, 3, 2, 4).reshape(-1, LANES)
    r = run_blocks(
        z,
        dict(
            lengths=seq_lengths,
            x=x_in,
            gain=norm_gain,
            probe=out_probe,
            mask=char_mask.reshape(1, z.toks),
            w_in=w_in,
            conv_w=conv_weight,
            conv_b=conv_bias,
            w_x=xproj_weight,
            w_dt=dt_weight,
            dt_b=dt_bias,
            a_log=a_log,
            skip=skip_gain,
            w_out=out_weight,
        ),
    )
    if not z.shared:
        r.smalls = lax.psum(r.smalls, "dp")
    g_in, g_out, rest = weight_grads(z, r)
    block_out, input_grad, gains, g_dt, g_alog, g_bias, g_skip = rest[:7]
    g_x, g_conv_w, g_conv_b = rest[7:]
    return (
        block_out,
        input_grad,
        gains,
        g_in,
        g_conv_w,
        g_conv_b,
        g_x,
        g_dt,
        g_bias,
        g_alog,
        g_skip,
        g_out,
    )


def solution(mesh):
    return jax.shard_map(
        functools.partial(local, mesh),
        mesh=mesh,
        in_specs=(
            P("dp", "chan"),
            P(None, "chan"),
            P(None, None, None, "chan"),
            P(None, None, "chan"),
            P(None, "chan"),
            P(None, None, "chan"),
            P(None, None, "chan"),
            P(None, "chan"),
            P(None, None, "chan"),
            P(None, "chan"),
            P(None, "chan", None),
            P(),
            P("dp"),
            P("dp", "chan"),
        ),
        out_specs=(
            P("dp", "chan"),
            P("dp", "chan"),
            P(None, "chan"),
            P(None, None, None, "chan"),
            P(None, None, "chan"),
            P(None, "chan"),
            P(None, None, "chan"),
            P(None, None, "chan"),
            P(None, "chan"),
            P(None, None, "chan"),
            P(None, "chan"),
            P(None, "chan", None),
        ),
        check_vma=False,
    )
```

```python
import functools
from types import SimpleNamespace

import jax
import jax.numpy as jnp
from jax import lax
from jax.experimental import pallas as pl
from jax.experimental.pallas import tpu as pltpu
from jax.sharding import PartitionSpec as P

MESH = pl.DeviceIdType.MESH
LANES = 128
ROWS = 8
HALO = 16
EPSILON = 1e-05
RESET = 1e30
F32 = jnp.float32
BF16 = jnp.bfloat16


def dot(left, right, dims=((1,), (0,)), precision=None):
    return lax.dot_general(
        left, right, (dims, ((), ())), precision=precision, preferred_element_type=F32
    )


def silu_slope(value, sig):
    return sig * (1.0 + value * (1.0 - sig))


def side_by_side(parts):
    return jnp.concatenate([parts[k] for k in range(parts.shape[0])], axis=1)


def wide(column, width):
    return jnp.concatenate([column] * (width // column.shape[1]), axis=1)


def sizes_of(mesh, x_in, in_weight, xproj_weight, dt_weight, a_log, conv_weight):
    z = SimpleNamespace()
    z.ndp = mesh.shape["dp"]
    z.nch = mesh.shape["chan"]
    z.toks, z.quarter = x_in.shape
    z.width = in_weight.shape[1]
    z.chans = in_weight.shape[3]
    z.layers = in_weight.shape[0]
    z.xdim = xproj_weight.shape[1]
    z.rank = dt_weight.shape[1]
    z.states = a_log.shape[1]
    z.taps = conv_weight.shape[1]
    z.half = z.width // 2
    z.total = z.toks * z.ndp
    z.groups = z.chans // LANES
    z.chunk = min(256, z.total)
    z.span = 2 * z.groups
    z.pack = 128
    assert max(z.xdim + z.taps + 1, z.rank + z.states + 2) <= z.pack
    z.shared = z.pack % (16 * z.ndp) == 0
    z.piece = z.pack // z.ndp if z.shared else 16
    return z


def scratch_of(z):
    t, d, c, n = z.toks, z.width, z.chans, z.ndp
    ext = t + HALO
    vm = pltpu.VMEM
    by_token = [vm((t, c), F32) for _ in range(9)]
    layer = dict(
        hid=vm((ext, d), BF16),
        inv=vm((ext, LANES), F32),
        xs=vm((ext, d), F32),
        inner=vm((ext, c), F32),
        gate=by_token[0],
        slope=by_token[1],
        actf=by_token[2],
        pre=by_token[3],
        step=by_token[4],
        stepk=by_token[5],
        u=by_token[6],
        scan=by_token[7],
        ds=by_token[8],
        act=vm((t, c), BF16),
        gated=vm((t, c), BF16),
        psend=vm((z.xdim, t), BF16),
        pland=vm((z.nch, z.xdim, t), BF16),
        stept=vm((z.rank, t), BF16),
        bce=vm((t, 2 * z.states, LANES), F32),
        dec=vm((t, z.states, c), F32),
        st=vm((t + 1, z.states, c), F32),
        ssend=vm((8, LANES), F32),
        ssum=vm((n, 8, LANES), F32),
        carry=vm((2, z.states, c), BF16),
        sland=vm((n, z.states, c), BF16),
        rland=vm((n, z.states, c), BF16),
        bsend=vm((z.xdim, t), BF16),
        bland=vm((z.nch, z.xdim, t), BF16),
        bhalo=vm((z.nch, z.xdim, t), BF16),
        esend=vm((2 * ROWS, c), F32),
        eland=vm((2 * ROWS, c), F32),
        dm=vm((t, 2 * c), BF16),
        ht=vm((z.quarter, t), BF16),
        sct=vm((c, t), BF16),
        gq=vm((t, d), BF16),
        g=vm((t, d), F32),
        packs=[vm((z.pack, c), F32) for _ in range(2)],
        packed=[vm((z.pack if z.shared else 16, c), BF16) for _ in range(2)],
        tland=[vm((z.pack // 2 if z.shared else 16, c), BF16) for _ in range(2)],
        rsland=[vm((n // 2 if z.shared else 1, z.piece, c), BF16) for _ in range(2)],
        small=[vm((z.pack if z.shared else 16, c), BF16) for _ in range(2)],
        gnsend=vm((8, z.quarter), F32),
        gnland=vm((n, 8, z.quarter), F32),
    )
    halves = [vm((t, z.half), BF16) for _ in range(4)]
    reduction = dict(
        a_send=halves[0],
        a_land=halves[1],
        b_send=halves[2],
        b_land=halves[3],
        full=vm((ext, d), F32),
    )
    return dict(
        layers=[dict(layer) for _ in range(z.layers)],
        reductions=[dict(reduction) for _ in range(4)],
        b_halo=vm((2, HALO, z.half), BF16),
        hq=vm((t, z.quarter), BF16),
        cq=vm((t, z.quarter), BF16),
        cot=vm((t, z.quarter), F32),
        meta=vm((16, z.quarter), F32),
        metas=vm((z.nch, 16, z.quarter), F32),
        metah=vm((z.nch, 16, z.quarter), F32),
        gfull=vm((8, d), F32),
        vm=vm((3, ext, LANES), F32),
        dst=vm((t, c), F32),
        adj=vm((t, c), F32),
        dact=vm((t, c), F32),
        dgated=vm((t, c), F32),
        dc=vm((ext, c), F32),
        grow=vm((8, d), F32),
        raw=vm((d * z.span, LANES), BF16),
        stage=vm((LANES * z.span, LANES), F32),
        hidc=vm((2, d, z.chunk), BF16),
        gqc=vm((2, z.nch, z.chunk, z.quarter), BF16),
        scanc=vm((2, c, z.chunk), BF16),
        gatc=vm((2, c, z.chunk), BF16),
        dmgc=vm((2, c, z.chunk), BF16),
        wi=vm((z.layers, d, 2 * c), BF16),
        wo=vm((z.layers, c, d), BF16),
    )


def block_kernel(z, sems, refs):
    v = SimpleNamespace(**refs)
    L = [SimpleNamespace(**one) for one in v.layers]
    R = [SimpleNamespace(**one) for one in v.reductions]
    t, d, c, n = z.toks, z.width, z.chans, z.ndp
    ext = t + HALO
    half, quarter, groups = z.half, z.quarter, z.groups
    rank, ns = z.rank, z.states

    dp = lax.axis_index("dp")
    ch = lax.axis_index("chan")
    bit = lax.rem(ch, 2)
    side = lax.div(ch, 2)
    across = {2: lax.rem(ch + 2, 4)}
    across[1] = ch + 1 - 2 * bit
    across[3] = lax.rem(across[1] + 2, 4)
    pair = lax.rem(dp, 2)
    twin = dp + 1 - 2 * pair
    rank_q = lax.div(dp, 2)
    nq = n // 2
    has_next = dp + 1 < n
    has_prev = dp > 0
    q_cols = pl.ds(pl.multiple_of(ch * quarter, quarter), quarter)
    h_mine = pl.ds(pl.multiple_of(bit * half, half), half)
    h_other = pl.ds(pl.multiple_of((1 - bit) * half, half), half)

    drains = []
    counter = [0]

    def alloc(count):
        base = counter[0]
        counter[0] += count
        return base

    def remote(src, dst, index, target):
        return pltpu.make_async_remote_copy(
            src_ref=src,
            dst_ref=dst,
            send_sem=v.ss.at[index],
            recv_sem=v.rs.at[index],
            device_id=target,
            device_id_type=MESH,
        )

    def send(src, dst, target):
        copy = remote(src, dst, alloc(1), target)
        copy.start()
        drains.append(copy.wait_send)
        return copy

    def bundle(total, index):
        return remote(total, total, index, (dp, across[1]))

    def send_all(copies, total):
        index = alloc(1)
        for src, dst, target in copies:
            remote(src, dst, index, target).start()
        whole = bundle(total, index)
        drains.append(whole.wait_send)
        return whole

    def chan_send(src, dst, total):
        return send_all([(src, dst, (dp, across[p])) for p in (2, 3, 1)], total)

    def edge_send(groups, step):
        there, here = (has_next, has_prev) if step > 0 else (has_prev, has_next)
        wholes = []
        for copies, total in groups:
            index = alloc(1)
            wholes.append(bundle(total, index))

            @pl.when(there)
            def _():
                for src, dst, chan in copies:
                    remote(src, dst, index, (dp + step, chan)).start()

        def drain():
            @pl.when(there)
            def _():
                for whole in wholes:
                    whole.wait_send()

        drains.append(drain)

        def arrive():
            @pl.when(here)
            def _():
                for whole in wholes:
                    whole.wait_recv()

        return arrive

    def dp_send_all(src_of, dst, total):
        index = alloc(1)

        def body(o, carry):
            to = lax.rem(dp + o, n)
            remote(src_of(to), dst, index, (to, ch)).start()
            return carry

        lax.fori_loop(1, n, body, 0)
        whole = bundle(total, index)
        drains.append(whole.wait_send)
        return whole.wait_recv

    def dp_send(src, dst, base, low, high):
        def copy_of(o):
            return remote(src, dst, base + o - 1, (lax.rem(dp + o, n), ch))

        def each(act):
            def body(o, carry):
                act(copy_of(o))
                return carry

            return body

        lax.fori_loop(low, high, each(lambda copy: copy.start()), 0)
        drains.append(
            lambda: lax.fori_loop(low, high, each(lambda copy: copy.wait_send()), 0)
        )

        def arrive(first, last):
            lax.fori_loop(first, last, each(lambda copy: copy.wait_recv()), 0)

        return arrive

    ring = nq == 4
    inner = (rank_q == 1) | (rank_q == 2)

    def gather(src, place, total):
        first, middle, second = alloc(1), alloc(1), alloc(1)
        local = pltpu.make_async_copy(src, place(dp), v.ls.at[alloc_local()])
        local.start()
        steps = (1, nq - 1) if ring else tuple(range(1, nq))
        heard = len(steps)

        def even(q):
            return q * 2 + pair

        def pass_on(q, to, index):
            remote(place(even(q)), place(even(q)), index, to).start()

        if ring:
            for o in steps:
                to = even(lax.rem(rank_q + o, nq))
                remote(src, place(dp), first, (to, ch)).start()
        else:

            def start(o, carry):
                to = even(lax.rem(rank_q + o, nq))
                remote(src, place(dp), first, (to, ch)).start()
                return carry

            lax.fori_loop(1, nq, start, 0)
        remote(src, place(dp), second, (twin, ch)).start()

        def relay1():
            bundle(total(heard), first).wait_recv()
            if ring:

                @pl.when(inner)
                def _():
                    pass_on(rank_q - 1, (even(rank_q + 1), ch), middle)
                    pass_on(rank_q + 1, (even(rank_q - 1), ch), middle)

                for o in steps:
                    pass_on(lax.rem(rank_q + o, nq), (twin, ch), second)
            else:

                def body(o, carry):
                    pass_on(lax.rem(rank_q + o, nq), (twin, ch), second)
                    return carry

                lax.fori_loop(1, nq, body, 0)

        def relay2():
            if ring:
                bundle(total(1), middle).wait_recv()
                pass_on(lax.rem(rank_q + 2, nq), (twin, ch), second)

        def finish():
            bundle(total(heard), first).wait_send()
            if ring:

                @pl.when(inner)
                def _():
                    bundle(total(2), middle).wait_send()

            bundle(total(nq), second).wait()
            local.wait()

        return SimpleNamespace(relay1=relay1, relay2=relay2, finish=finish)

    locals_used = [2 * z.layers + 10]

    def alloc_local():
        locals_used[0] += 1
        return locals_used[0] - 1

    loads = []
    for l in range(z.layers):
        loads.append(
            (
                pltpu.make_async_copy(
                    v.w_in.at[pl.ds(l * d * z.span, d * z.span), :],
                    v.raw,
                    v.ls.at[2 * l],
                ),
                pltpu.make_async_copy(v.w_out.at[l], v.wo.at[l], v.ls.at[2 * l + 1]),
            )
        )
        loads[l][1].start()
    loads[0][0].start()

    def load_in(l):
        loads[l][0].wait()
        rows = LANES * z.span

        def body(k, carry):
            at = pl.ds(pl.multiple_of(k * rows, rows), rows)
            to = pl.ds(pl.multiple_of(k * LANES, LANES), LANES)
            v.stage[...] = v.raw[at, :].astype(F32)
            for g in range(groups):
                for side_of in range(2):
                    col = side_of * c + g * LANES
                    v.wi[l, to, col : col + LANES] = v.stage[
                        pl.ds(2 * g + side_of, LANES, stride=z.span), :
                    ].astype(BF16)
            return carry

        lax.fori_loop(0, d // LANES, body, 0)
        if l + 1 < z.layers:
            loads[l + 1][0].start()

    barrier = pltpu.get_barrier_semaphore()
    for p in (1, 2, 3):
        pl.semaphore_signal(
            barrier, inc=1, device_id=(dp, across[p]), device_id_type=MESH
        )

    def greet(o, carry):
        pl.semaphore_signal(
            barrier, inc=1, device_id=(lax.rem(dp + o, n), ch), device_id_type=MESH
        )
        return carry

    lax.fori_loop(1, n, greet, 0)
    for step in (1, n - 1):
        for p in (1, 2, 3):
            pl.semaphore_signal(
                barrier,
                inc=1,
                device_id=(lax.rem(dp + step, n), across[p]),
                device_id_type=MESH,
            )

    xq = v.x[...]
    v.hq[...] = (xq * v.gain[0:1, :]).astype(BF16)
    v.meta[...] = jnp.zeros_like(v.meta)
    v.meta[0 : z.layers, :] = v.gain[...]
    v.meta[8:16, 0:t] = dot(
        jnp.ones((8, quarter), F32), xq * xq, ((1,), (1,)), lax.Precision.HIGHEST
    )
    mask = jnp.broadcast_to(v.mask[...].astype(F32), (8, t))
    cot = v.probe[...] * jnp.transpose(mask)[:, 0:1]
    v.cot[...] = cot
    v.cq[...] = cot.astype(BF16)

    @pl.when(jnp.logical_not(has_prev))
    def _():
        L[0].hid[0:HALO, :] = jnp.zeros((HALO, d), BF16)
        L[0].xs[0:HALO, :] = jnp.zeros((HALO, d), F32)
        v.metah[...] = jnp.zeros_like(v.metah)
        v.b_halo[...] = jnp.zeros_like(v.b_halo)

    @pl.when(jnp.logical_not(has_next))
    def _():
        for l in range(z.layers):
            L[l].bhalo[...] = jnp.zeros_like(L[l].bhalo)
            L[l].eland[...] = jnp.zeros_like(L[l].eland)

    pl.semaphore_wait(barrier, 3 + (n - 1) + 6)

    own = pl.ds(HALO, t)
    head = pl.ds(0, HALO)
    tail = pl.ds(t - HALO, HALO)
    everyone = [ch, across[1], across[2], across[3]]
    got_h = chan_send(
        v.hq, L[0].hid.at[own, q_cols], L[0].hid.at[own, 0 : 3 * quarter]
    )
    got_m = chan_send(v.meta, v.metas.at[ch], v.metas.at[0 : z.nch - 1])
    got_edge = edge_send(
        [
            (
                [(v.hq.at[tail, :], L[0].hid.at[head, q_cols], k) for k in everyone],
                L[0].hid.at[head, :],
            ),
            ([(v.meta, v.metah.at[ch], k) for k in everyone], v.metah),
        ],
        1,
    )
    L[0].hid[own, q_cols] = v.hq[...]
    v.metas[ch] = v.meta[...]
    L[0].xs[own, q_cols] = xq
    L[1].gq[:, q_cols] = v.cq[...]
    L[1].g[:, q_cols] = cot

    position = dp * t + lax.broadcasted_iota(jnp.int32, (ext, LANES), 0)
    first = jnp.zeros((ext, LANES), jnp.int32)
    start = jnp.int32(0)
    for s in range(v.lengths.shape[0]):
        first = jnp.where(position >= start, start, first)
        start = start + v.lengths[s]
    offset = position - first
    for k in range(z.taps - 1):
        v.vm[k] = jnp.where(offset >= z.taps - 1 - k, 1.0, 0.0).astype(F32)

    def valid(k, rows, width):
        return wide(v.vm[k, rows, :], width)

    def a_of(l):
        return -jnp.exp(v.a_log[l])

    def lane(g):
        return slice(g * LANES, (g + 1) * LANES)

    def fwd_head(l):
        hid, inv = L[l].hid, L[l].inv
        inner = dot(hid[...], v.wi[l, :, 0:c])
        if l == 0:
            inner = wide(inv[...], c) * inner
        inner = inner.astype(BF16).astype(F32)
        L[l].inner[...] = inner
        conv = jnp.broadcast_to(v.conv_b[l : l + 1, :], (t, c))
        for k in range(z.taps):
            at = HALO - z.taps + 1 + k
            term = v.conv_w[l, k : k + 1, :] * L[l].inner[at : at + t, :]
            conv = conv + (term if k == z.taps - 1 else term * valid(k, slice(0, t), c))
        sig = jax.nn.sigmoid(conv)
        act = (conv * sig).astype(BF16)
        L[l].act[...] = act
        L[l].actf[...] = act.astype(F32)
        part = dot(v.w_x[l], act, ((1,), (1,))).astype(BF16)
        L[l].psend[...] = part
        land = L[l].pland
        got = chan_send(L[l].psend, land.at[ch], land.at[0 : z.nch - 1])
        L[l].pland[ch] = part
        L[l].slope[...] = silu_slope(conv, sig)
        gate = dot(hid[own, :], v.wi[l, :, c : 2 * c])
        if l == 0:
            gate = wide(inv[own, :], c) * gate
        gate = gate.astype(BF16)
        L[l].gate[...] = gate.astype(F32)
        return got

    def fwd_mid(l, got):
        got.wait_recv()
        land = L[l].pland
        proj = land[0].astype(F32)
        for k in range(1, z.nch):
            proj = proj + land[k].astype(F32)
        stept = proj[0:rank, :].astype(BF16)
        L[l].stept[...] = stept
        pre = dot(stept, v.w_dt[l], ((0,), (0,))) + v.dt_b[l : l + 1, :]
        step = jnp.maximum(pre, 0.0) + jnp.log1p(jnp.exp(-jnp.abs(pre)))
        stepk = step + (1.0 - valid(z.taps - 2, slice(0, t), c)) * RESET
        L[l].pre[...] = pre
        L[l].step[...] = step
        L[l].stepk[...] = stepk
        L[l].u[...] = step * L[l].actf[...]
        summed = jnp.sum(stepk, axis=0, keepdims=True)
        L[l].ssend[...] = jnp.zeros((8, LANES), F32)
        for g in range(groups):
            L[l].ssend[g : g + 1, :] = summed[:, lane(g)]
        land = L[l].ssum
        got_s = dp_send_all(lambda to: L[l].ssend, land.at[dp], land.at[0 : n - 1])
        bc = proj[rank : rank + 2 * ns, :]
        lanes = lax.broadcasted_iota(jnp.int32, (2 * ns, t), 1)
        bce = L[l].bce

        def spread(block, carry):
            for i in range(ROWS):
                tok = block * ROWS + i
                column = jnp.sum(
                    jnp.where(lanes == tok, bc, 0.0), axis=1, keepdims=True
                )
                bce[tok] = jnp.broadcast_to(column, (2 * ns, LANES))
            return carry

        lax.fori_loop(0, t // ROWS, spread, 0)
        return got_s

    def scan_sum(l):
        a = a_of(l)
        stepk, u, bce, dec = L[l].stepk, L[l].u, L[l].bce, L[l].dec

        def body(block, state):
            state = list(state)
            rows = pl.ds(pl.multiple_of(block * ROWS, ROWS), ROWS)
            sk, uu = stepk[rows, :], u[rows, :]
            for i in range(ROWS):
                tok = block * ROWS + i
                b = bce[tok, 0:ns, :]
                for g in range(groups):
                    e = jnp.exp(sk[i : i + 1, lane(g)] * a[:, lane(g)])
                    dec[tok, :, lane(g)] = e
                    state[g] = e * state[g] + uu[i : i + 1, lane(g)] * b
            return tuple(state)

        zero = jnp.zeros((ns, LANES), F32)
        return lax.fori_loop(0, t // ROWS, body, (zero,) * groups)

    def back_sum(l):
        ds, bce, dec = L[l].ds, L[l].bce, L[l].dec

        def body(k, flow):
            flow = list(flow)
            block = t // ROWS - 1 - k
            rows = pl.ds(pl.multiple_of(block * ROWS, ROWS), ROWS)
            dd = ds[rows, :]
            for i in reversed(range(ROWS)):
                tok = block * ROWS + i
                cc = bce[tok, ns : 2 * ns, :]
                for g in range(groups):
                    lam = cc * dd[i : i + 1, lane(g)] + flow[g]
                    flow[g] = dec[tok, :, lane(g)] * lam
            return tuple(flow)

        zero = jnp.zeros((ns, LANES), F32)
        return lax.fori_loop(0, t // ROWS, body, (zero,) * groups)

    def put(ref, k, parts):
        for g in range(groups):
            ref[k, :, lane(g)] = parts[g].astype(BF16)

    def carry_in(l, land, order, count):
        a = a_of(l)

        def body(k, carry):
            j = order(k)
            row = jnp.concatenate(
                [L[l].ssum[j, g : g + 1, :] for g in range(groups)], axis=1
            )
            return jnp.exp(a * row) * carry + land[j].astype(F32)

        return lax.fori_loop(0, count, body, jnp.zeros((ns, c), F32))

    def scan_out(l, carry):
        u, bce, dec, st = L[l].u, L[l].bce, L[l].dec, L[l].st
        y = L[l].scan
        st[0] = carry

        def body(block, state):
            state = list(state)
            rows = pl.ds(pl.multiple_of(block * ROWS, ROWS), ROWS)
            uu = u[rows, :]
            outs = [[] for _ in range(groups)]
            for i in range(ROWS):
                tok = block * ROWS + i
                b = bce[tok, 0:ns, :]
                cc = bce[tok, ns : 2 * ns, :]
                for g in range(groups):
                    s = dec[tok, :, lane(g)] * state[g] + uu[i : i + 1, lane(g)] * b
                    st[tok + 1, :, lane(g)] = s
                    state[g] = s
                    outs[g].append(jnp.sum(cc * s, axis=0, keepdims=True))
            for g in range(groups):
                y[rows, lane(g)] = jnp.concatenate(outs[g], axis=0)
            return tuple(state)

        lax.fori_loop(
            0, t // ROWS, body, tuple(carry[:, lane(g)] for g in range(groups))
        )
        scanned = y[...] + v.skip[l : l + 1, :] * L[l].actf[...]
        y[...] = scanned
        L[l].sct[...] = jnp.transpose(scanned.astype(BF16))
        gate = L[l].gate[...]
        gated = (scanned * gate * jax.nn.sigmoid(gate)).astype(BF16)
        L[l].gated[...] = gated
        return gated

    def reduce_a(k, part_of):
        send_ref, keep_ref = R[k].a_send, R[k].full
        send_ref[...] = part_of(h_other).astype(BF16)
        got = send(send_ref, R[k].a_land, (dp, across[1]))
        keep_ref[own, h_mine] = part_of(h_mine)
        return got

    def reduce_b(k, got, edge):
        got.wait_recv()
        b_send = R[k].b_send
        b_send[...] = (
            R[k].full[own, h_mine]
            + R[k].a_land[...].astype(F32)
        ).astype(BF16)
        got = send(b_send, R[k].b_land, (dp, across[2]))
        arrive = None
        if edge:
            arrive = edge_send(
                [
                    (
                        [
                            (b_send.at[tail, :], v.b_halo.at[side], chan)
                            for chan in (ch, across[2])
                        ],
                        v.b_halo,
                    )
                ],
                1,
            )
        return got, arrive

    def reduce_c(k, got, arrive):
        got.wait_recv()
        full = R[k].full
        full[own, h_mine] = R[k].b_send[...].astype(F32) + R[k].b_land[...].astype(F32)
        region = full.at[own, h_mine]
        if arrive is not None:
            arrive()
            full[head, h_mine] = v.b_halo[0].astype(F32) + v.b_halo[1].astype(F32)
            region = full.at[:, h_mine]
        return send(region, region, (dp, across[1]))

    def reduce_all(k, part_of, edge=False):
        a = reduce_a(k, part_of)
        b, arrive = reduce_b(k, a, edge)
        reduce_c(k, b, arrive).wait_recv()

    def out_part(l):
        return lambda cols: dot(L[l].gated[...], v.wo[l, :, cols])

    def in_part(l):
        return lambda cols: dot(L[l].dm[...], v.wi[l, cols, :], ((1,), (1,)))

    def back_gate(l):
        dgated = dot(L[l].gq[...], v.wo[l], ((1,), (1,)))
        gate = L[l].gate[...]
        v.dgated[...] = dgated
        L[l].ds[...] = dgated * gate * jax.nn.sigmoid(gate)

    def back_dgate(l):
        gate = L[l].gate[...]
        sig = jax.nn.sigmoid(gate)
        dgate = v.dgated[...] * L[l].scan[...] * silu_slope(gate, sig)
        L[l].dm[:, c : 2 * c] = dgate.astype(BF16)

    def back_scan(l, flow_in):
        a = a_of(l)
        ds, u, bce, dec, st = L[l].ds, L[l].u, L[l].bce, L[l].dec, L[l].st
        stepk, actf = L[l].stepk, L[l].actf
        lanes = lax.broadcasted_iota(jnp.int32, (ns, t), 1)

        def body(k, carry):
            flow, acc, acc_b, acc_c = list(carry[0]), list(carry[1]), carry[2], carry[3]
            block = t // ROWS - 1 - k
            rows = pl.ds(pl.multiple_of(block * ROWS, ROWS), ROWS)
            dd, uu, sk, aa = ds[rows, :], u[rows, :], stepk[rows, :], actf[rows, :]
            d_step = [[] for _ in range(groups)]
            d_adj = [[] for _ in range(groups)]
            for i in reversed(range(ROWS)):
                tok = block * ROWS + i
                b = bce[tok, 0:ns, :]
                cc = bce[tok, ns : 2 * ns, :]
                sum_b = jnp.zeros((ns, LANES), F32)
                sum_c = jnp.zeros((ns, LANES), F32)
                for g in range(groups):
                    drow = dd[i : i + 1, lane(g)]
                    lam = cc * drow + flow[g]
                    flow[g] = dec[tok, :, lane(g)] * lam
                    rate = flow[g] * st[tok, :, lane(g)]
                    acc[g] = acc[g] + rate * sk[i : i + 1, lane(g)]
                    adj = jnp.sum(lam * b, axis=0, keepdims=True)
                    d_adj[g].insert(0, adj)
                    d_step[g].insert(
                        0,
                        jnp.sum(rate * a[:, lane(g)], axis=0, keepdims=True)
                        + adj * aa[i : i + 1, lane(g)],
                    )
                    sum_b = sum_b + lam * uu[i : i + 1, lane(g)]
                    sum_c = sum_c + st[tok + 1, :, lane(g)] * drow
                acc_b = jnp.where(
                    lanes == tok, jnp.sum(sum_b, axis=1, keepdims=True), acc_b
                )
                acc_c = jnp.where(
                    lanes == tok, jnp.sum(sum_c, axis=1, keepdims=True), acc_c
                )
            for g in range(groups):
                v.dst[rows, lane(g)] = jnp.concatenate(d_step[g], axis=0)
                v.adj[rows, lane(g)] = jnp.concatenate(d_adj[g], axis=0)
            return (tuple(flow), tuple(acc), acc_b, acc_c)

        zero = jnp.zeros((ns, LANES), F32)
        _, acc, acc_b, acc_c = lax.fori_loop(
            0,
            t // ROWS,
            body,
            (
                tuple(flow_in[:, lane(g)] for g in range(groups)),
                (zero,) * groups,
                jnp.zeros((ns, t), F32),
                jnp.zeros((ns, t), F32),
            ),
        )
        for g in range(groups):
            L[l].packs[0][rank : rank + ns, lane(g)] = acc[g] * a[:, lane(g)]
        return acc_b, acc_c

    def back_mid(l, acc_b, acc_c):
        pack = L[l].packs[0]
        actf = L[l].actf[...]
        ds = L[l].ds[...]
        dpre = v.dst[...] * jax.nn.sigmoid(L[l].pre[...])
        dpre_q = dpre.astype(BF16)
        bsend = L[l].bsend
        bsend[0:rank, :] = dot(v.w_dt[l], dpre_q, ((1,), (1,))).astype(BF16)
        bsend[rank : rank + ns, :] = acc_b.astype(BF16)
        bsend[rank + ns : rank + 2 * ns, :] = acc_c.astype(BF16)
        land = L[l].bland
        got = chan_send(bsend, land.at[ch], land.at[0 : z.nch - 1])
        land[ch] = bsend[...]
        dact = ds * v.skip[l : l + 1, :] + L[l].step[...] * v.adj[...]
        v.dact[...] = dact
        L[l].esend[0:ROWS, :] = dact[0:ROWS, :]
        L[l].esend[ROWS : 2 * ROWS, :] = L[l].slope[0:ROWS, :]
        edge = edge_send(
            [
                ([(L[l].esend, L[l].eland, ch)], L[l].eland),
                ([(bsend, L[l].bhalo.at[ch], k) for k in everyone], L[l].bhalo),
            ],
            -1,
        )
        pack[0:rank, :] = dot(L[l].stept[...], dpre_q)
        at = rank + ns
        pack[at : at + 1, :] = jnp.sum(dpre, axis=0, keepdims=True)
        pack[at + 1 : at + 2, :] = jnp.sum(ds * actf, axis=0, keepdims=True)
        pack[at + 2 :, :] = jnp.zeros((z.pack - at - 2, c), F32)
        return got, edge

    def sum_land(ref):
        total = ref[0].astype(F32)
        for k in range(1, z.nch):
            total = total + ref[k].astype(F32)
        return total.astype(BF16)

    def back_conv(l, got, edge):
        got.wait_recv()
        edge()
        dproj = sum_land(L[l].bland)
        dproj_h = sum_land(L[l].bhalo)
        wx = v.w_x[l]
        dact = v.dact[...] + dot(dproj, wx, ((0,), (0,)))
        dconv = dact * L[l].slope[...]
        v.dc[0:t, :] = dconv
        eland = L[l].eland
        after = dot(dproj_h, wx, ((0,), (0,)))[0:ROWS, :]
        v.dc[t : t + ROWS, :] = (eland[0:ROWS, :] + after) * eland[ROWS : 2 * ROWS, :]
        dinner = jnp.zeros((t, c), F32)
        for k in range(z.taps):
            at = z.taps - 1 - k
            rows = slice(at, at + t)
            term = v.dc[rows, :] * v.conv_w[l, k : k + 1, :]
            dinner = dinner + (
                term if k == z.taps - 1 else term * valid(k, rows, c)
            )
        L[l].dm[:, 0:c] = dinner.astype(BF16)
        return dproj

    def back_rest(l, dproj):
        pack = L[l].packs[1]
        pack[0 : z.xdim, :] = dot(dproj, L[l].act[...])
        dconv = v.dc[0:t, :]
        at = z.xdim
        for k in range(z.taps):
            row = HALO - z.taps + 1 + k
            term = dconv * L[l].inner[row : row + t, :]
            if k < z.taps - 1:
                term = term * valid(k, slice(0, t), c)
            pack[at + k : at + k + 1, :] = jnp.sum(term, axis=0, keepdims=True)
        at = at + z.taps
        pack[at : at + 1, :] = jnp.sum(dconv, axis=0, keepdims=True)
        pack[at + 1 :, :] = jnp.zeros((z.pack - at - 1, c), F32)

    def back_norm(l, k):
        inv = wide(L[l].inv[own, :], d)
        u = R[k].full[own, :] * inv
        x = L[l].xs[own, :]
        scaled = u * v.gfull[l : l + 1, :]
        xhat = x * inv
        mean = jnp.sum(scaled * xhat, axis=1, keepdims=True) * (1.0 / d)
        v.grow[...] = jnp.broadcast_to(jnp.sum(u * x, axis=0, keepdims=True), (8, d))
        L[l].gnsend[...] = v.grow[:, q_cols]
        L[l].gnland[dp] = v.grow[:, q_cols]
        land = L[l].gnland
        arrive = dp_send_all(lambda to: L[l].gnsend, land.at[dp], land.at[0 : n - 1])
        return L[l].g[...] + scaled - xhat * mean, arrive

    def gain_out(l, arrive):
        arrive()
        total = lax.fori_loop(
            0, n, lambda j, s: s + L[l].gnland[j], jnp.zeros((8, quarter), F32)
        )
        v.gains[l : l + 1, :] = total[0:1, :]

    def rows_of(first, count):
        return pl.ds(pl.multiple_of(first, count), count)

    def small_sum(l, p):
        if not z.shared:
            v.smalls[l, p] = L[l].packs[p][...]
            nothing = lambda: None
            return SimpleNamespace(b=nothing, c=nothing, d=nothing, out=nothing)
        rows, part = z.piece, z.pack // 2
        pack, packed, tland = L[l].packs[p], L[l].packed[p], L[l].tland[p]
        land, small = L[l].rsland[p], L[l].small[p]
        mine, other = rows_of(pair * part, part), rows_of((1 - pair) * part, part)
        place = rows_of(pair * part + rank_q * rows, rows)
        packed[other, :] = pack[other, :].astype(BF16)
        got_a = send(packed.at[other, :], tland, (twin, ch))
        state = {}

        def even_send(src_of, dst, total):
            index = alloc(1)

            def body(o, carry):
                q = lax.rem(rank_q + o, nq)
                remote(src_of(q), dst, index, (q * 2 + pair, ch)).start()
                return carry

            lax.fori_loop(1, nq, body, 0)
            whole = bundle(total, index)
            drains.append(whole.wait_send)
            return whole

        def b():
            got_a.wait_recv()
            packed[mine, :] = (pack[mine, :] + tland[...].astype(F32)).astype(BF16)
            piece = lambda q: rows_of(pair * part + q * rows, rows)
            state[0] = even_send(
                lambda q: packed.at[piece(q), :],
                land.at[rank_q],
                land.at[0 : nq - 1],
            )
            land[rank_q] = packed[place, :]

        def c_():
            state[0].wait_recv()
            total = land[0].astype(F32)
            for k in range(1, nq):
                total = total + land[k].astype(F32)
            small[place, :] = total.astype(BF16)
            state[1] = even_send(
                lambda q: small.at[place, :],
                small.at[place, :],
                small.at[0 : (nq - 1) * rows, :],
            )

        def d_():
            state[1].wait_recv()
            state[2] = send(small.at[mine, :], small.at[mine, :], (twin, ch))

        def out():
            state[2].wait_recv()
            v.smalls[l, p] = small[...]

        return SimpleNamespace(b=b, c=c_, d=d_, out=out)

    def inverse(total):
        return lax.rsqrt(total * (1.0 / d) + EPSILON)

    def norms():
        sums, sums_h = v.metas[0, 8:16, 0:t], v.metah[0, 8:16, 0:t]
        v.gfull[:, 0:quarter] = v.metas[0, 0:8, :]
        for k in range(1, z.nch):
            sums = sums + v.metas[k, 8:16, 0:t]
            sums_h = sums_h + v.metah[k, 8:16, 0:t]
            v.gfull[:, k * quarter : (k + 1) * quarter] = v.metas[k, 0:8, :]
        L[0].inv[own, :] = jnp.broadcast_to(
            jnp.transpose(inverse(sums))[:, 0:1], (t, LANES)
        )
        L[0].inv[head, :] = jnp.broadcast_to(
            jnp.transpose(inverse(sums_h))[t - HALO : t, 0:1], (HALO, LANES)
        )

    def in_lanes(src, ref, l, rows):
        return gather(
            src,
            lambda j: ref.at[l, rows, pl.ds(pl.multiple_of(j * t, t), t)],
            lambda count: ref.at[l, rows, 0 : count * t],
        )

    def in_rows(src, ref, low=0, high=t):
        m = high - low
        return gather(
            src,
            lambda j: ref.at[pl.ds(pl.multiple_of(j * t + low, m), m), :],
            lambda count: ref.at[0 : count * m, :],
        )

    def gather_hid(l):
        if l == 0:
            hidden = xq * v.gain[0:1, :] * wide(L[0].inv[own, :], quarter)
            L[0].ht[...] = jnp.transpose(hidden.astype(BF16))
        else:
            L[l].ht[...] = jnp.transpose(L[l].hid[own, q_cols])
        return in_lanes(L[l].ht, v.hid_all, l, q_cols)

    def gather_scan(l):
        return in_lanes(L[l].sct, v.scan_all, l, slice(None))

    def gather_gq(l):
        return in_rows(L[l].gq.at[:, q_cols], v.gq_all.at[l, ch])

    def gather_dmi(l, low=0, high=t):
        src = L[l].dm.at[low:high, 0:c]
        return in_rows(src, v.dmi_all.at[l], low, high)

    def quarter_at(k):
        return pl.ds(pl.multiple_of(k * quarter, quarter), quarter)

    def share(region, total):
        mine = region(ch)
        got = send(mine, mine, (dp, across[2]))

        def second():
            got.wait_recv()
            theirs = region(across[2])
            to = (dp, across[1])
            return send_all([(mine, mine, to), (theirs, theirs, to)], total).wait_recv

        return second

    def share_hid(l):
        return share(
            lambda k: v.hid_all.at[l, quarter_at(k), :],
            v.hid_all.at[l, 0 : 2 * quarter, :],
        )

    def share_gq(l):
        return share(
            lambda k: v.gq_all.at[l, k],
            v.gq_all.at[l, 0:2],
        )

    def share_rows(ref, rows):
        return share(lambda k: ref.at[rows, quarter_at(k)], ref.at[rows, 0 : 2 * quarter])

    chunks = z.total // z.chunk

    def chunk_loads(l, k):
        slot = lax.rem(k, 2)
        base = 2 * z.layers + 5 * slot
        at = pl.ds(pl.multiple_of(k * z.chunk, z.chunk), z.chunk)
        pairs = (
            (v.hid_all.at[l, :, at], v.hidc.at[slot]),
            (v.gq_all.at[l, :, at, :], v.gqc.at[slot]),
            (v.scan_all.at[l, :, at], v.scanc.at[slot]),
        )
        return [
            pltpu.make_async_copy(src, to, v.ls.at[base + i])
            for i, (src, to) in enumerate(pairs)
        ]

    def chunk_stores(l, k):
        slot = lax.rem(k, 2)
        base = 2 * z.layers + 5 * slot + 3
        at = pl.ds(pl.multiple_of(k * z.chunk, z.chunk), z.chunk)
        pairs = (
            (v.gatc.at[slot], v.gat_all.at[l, :, at]),
            (v.dmgc.at[slot], v.dmg_all.at[l, :, at]),
        )
        return [
            pltpu.make_async_copy(src, to, v.ls.at[base + i])
            for i, (src, to) in enumerate(pairs)
        ]

    def finish_begin(l):
        for copy in chunk_loads(l, jnp.int32(0)):
            copy.start()

    def finish_some(l, low, high):
        def body(k, carry):
            slot = lax.rem(k, 2)

            @pl.when(k + 1 < chunks)
            def _():
                for copy in chunk_loads(l, k + 1):
                    copy.start()

            @pl.when(k >= 2)
            def _():
                for copy in chunk_stores(l, k - 2):
                    copy.wait()

            loads_in = chunk_loads(l, k)
            loads_in[0].wait()
            w_gate = v.wi[l, :, c : 2 * c]
            gate = dot(w_gate, v.hidc[slot], ((0,), (0,))).astype(BF16).astype(F32)
            loads_in[1].wait()
            dgated = dot(v.wo[l], side_by_side(v.gqc[slot]), ((1,), (1,)))
            loads_in[2].wait()
            scanned = v.scanc[slot].astype(F32)
            sig = jax.nn.sigmoid(gate)
            v.gatc[slot] = (scanned * gate * sig).astype(BF16)
            v.dmgc[slot] = (dgated * scanned * silu_slope(gate, sig)).astype(BF16)
            for copy in chunk_stores(l, k):
                copy.start()
            return carry

        lax.fori_loop(low, high, body, 0)

    def finish_end(l):
        for k in range(max(chunks - 2, 0), chunks):
            for copy in chunk_stores(l, jnp.int32(k)):
                copy.wait()

    gq1 = gather_gq(1)
    load_in(0)
    got_h.wait_recv()
    got_m.wait_recv()
    got_edge()
    norms()
    gq1.relay1()
    hid0 = gather_hid(0)
    got_p = fwd_head(0)
    gq1.relay2()
    share_x = share_rows(L[0].xs, own)
    share_c = share_rows(L[1].gq, slice(None))
    got_xedge = edge_send(
        [
            (
                [(v.x.at[tail, :], L[0].xs.at[head, q_cols], k) for k in everyone],
                L[0].xs.at[head, :],
            )
        ],
        1,
    )
    load_in(1)
    got_s0 = fwd_mid(0, got_p)
    put(L[0].carry, 0, scan_sum(0))
    got_carry = dp_send(L[0].carry.at[0], L[0].sland.at[dp], alloc(n - 1), 1, n - dp)
    gq1.finish()
    share1 = share_gq(1)
    share_x = share_x()
    share_c = share_c()
    loads[0][1].wait()
    got_s0()
    got_carry(1, dp + 1)
    hid0.relay1()
    scan_out(0, carry_in(0, L[0].sland, lambda k: k, dp))
    scan0 = gather_scan(0)
    red0 = reduce_a(0, out_part(0))
    red0, arrive = reduce_b(0, red0, True)
    got_c = reduce_c(0, red0, arrive)
    hid0.relay2()
    share_x()
    got_xedge()
    got_c.wait_recv()
    x1 = L[0].xs[...] + R[0].full[...]
    L[1].xs[...] = x1
    inv1 = inverse(jnp.sum(x1 * x1, axis=1, keepdims=True))
    L[1].hid[...] = (x1 * inv1 * v.gfull[1:2, :]).astype(BF16)
    L[1].inv[...] = jnp.broadcast_to(inv1, (ext, LANES))

    got_p = fwd_head(1)
    hid1 = gather_hid(1)
    loads[1][1].wait()
    share_c()
    back_gate(1)
    scan0.relay1()
    got_s1 = fwd_mid(1, got_p)
    scan0.relay2()
    hid0.finish()
    share0 = share_hid(0)
    share1 = share1()
    put(L[1].carry, 0, scan_sum(1))
    put(L[1].carry, 1, back_sum(1))
    base = alloc(n - 1)
    got_f = dp_send(L[1].carry.at[0], L[1].sland.at[dp], base, 1, n - dp)
    got_r = dp_send(L[1].carry.at[1], L[1].rland.at[dp], base, n - dp, n)
    got_s1()
    got_f(1, dp + 1)
    got_r(dp + 1, n)
    hid1.relay1()
    scan_out(1, carry_in(1, L[1].sland, lambda k: k, dp))
    scan1 = gather_scan(1)
    share_g = share_rows(L[1].g, slice(None))
    back_dgate(1)
    red1 = reduce_a(1, out_part(1))
    hid1.relay2()

    acc_b, acc_c = back_scan(1, carry_in(1, L[1].rland, lambda k: n - 1 - k, n - 1 - dp))
    got_b, edge = back_mid(1, acc_b, acc_c)
    scan1.relay1()
    dproj = back_conv(1, got_b, edge)
    red2 = reduce_a(2, in_part(1))
    dmi1 = gather_dmi(1)
    back_rest(1, dproj)
    red2, _ = reduce_b(2, red2, False)
    share_g = share_g()
    red1, _ = reduce_b(1, red1, False)
    scan1.relay2()
    red2 = reduce_c(2, red2, None)
    hid1.finish()
    share_g()
    red2.wait_recv()
    share2 = share_hid(1)
    grad, gain1 = back_norm(1, 2)
    L[0].g[...] = grad
    L[0].gq[...] = grad.astype(BF16)

    gq0 = gather_gq(0)
    back_gate(0)
    put(L[0].carry, 1, back_sum(0))
    got_r = dp_send(L[0].carry.at[1], L[0].rland.at[dp], alloc(n - 1), n - dp, n)
    gq0.relay1()
    back_dgate(0)
    reduce_c(1, red1, None).wait_recv()
    v.block_out[...] = L[1].xs[own, q_cols] + R[1].full[own, q_cols]
    share0 = share0()
    got_r(dp + 1, n)
    gq0.relay2()
    dmi1.relay1()
    acc_b, acc_c = back_scan(0, carry_in(0, L[0].rland, lambda k: n - 1 - k, n - 1 - dp))
    got_b, edge = back_mid(0, acc_b, acc_c)
    share2 = share2()
    small1 = [small_sum(1, 0), small_sum(1, 1)]
    small0 = [small_sum(0, 0)]
    dmi1.relay2()
    share1()
    share2()
    scan1.finish()
    finish_begin(1)
    gq0.finish()
    dproj = back_conv(0, got_b, edge)
    dmi0 = [gather_dmi(0, 0, t // 2), gather_dmi(0, t // 2, t)]
    share3 = share_gq(0)
    back_rest(0, dproj)
    small0.append(small_sum(0, 1))
    red3 = reduce_a(3, in_part(0))
    for one in small1:
        one.b()
    small0[0].b()
    red3, _ = reduce_b(3, red3, False)
    finish_some(1, 0, 3 * chunks // 4)
    small0[1].b()
    dmi0[0].relay1()
    for one in small1:
        one.c()
    small0[0].c()
    finish_some(1, 3 * chunks // 4, chunks)
    dmi0[1].relay1()
    got_c = reduce_c(3, red3, None)
    small0[1].c()
    share3 = share3()
    got_c.wait_recv()
    grad, gain0 = back_norm(0, 3)
    L[0].g[...] = grad
    v.input_grad[...] = L[0].g[:, q_cols]
    dmi0[0].relay2()
    scan0.finish()
    finish_end(1)
    share0()
    share3()
    finish_begin(0)
    for one in small1:
        one.d()
    small0[0].d()
    finish_some(0, 0, chunks // 2)
    dmi0[1].relay2()
    small0[1].d()
    finish_some(0, chunks // 2, chunks)
    gain_out(0, gain0)
    gain_out(1, gain1)
    for one in small0 + small1:
        one.out()
    finish_end(0)
    for one in (dmi1, *dmi0):
        one.finish()
    for drain in drains:
        drain()
    assert (counter[0], locals_used[0]) == sems, (counter, locals_used)


def run_blocks(z, args):
    sems = (71 + 3 * (z.ndp - 1) + (16 if z.shared else 0), 23)
    vmem = pl.BlockSpec(memory_space=pltpu.VMEM)
    smem = pl.BlockSpec(memory_space=pltpu.SMEM)
    anywhere = pl.BlockSpec(memory_space=pl.ANY)
    specs = dict.fromkeys(args, vmem) | dict(
        lengths=smem, w_in=anywhere, w_out=anywhere
    )
    t, d, c, n, layers = z.toks, z.width, z.chans, z.total, z.layers
    shape = jax.ShapeDtypeStruct
    outs = dict(
        block_out=(shape((t, z.quarter), F32), vmem),
        input_grad=(shape((t, z.quarter), F32), vmem),
        smalls=(shape((layers, 2, z.pack, c), BF16 if z.shared else F32), vmem),
        gains=(shape((layers, z.quarter), F32), vmem),
        hid_all=(shape((layers, d, n), BF16), anywhere),
        gat_all=(shape((layers, c, n), BF16), anywhere),
        dmg_all=(shape((layers, c, n), BF16), anywhere),
        scan_all=(shape((layers, c, n), BF16), anywhere),
        gq_all=(shape((layers, z.nch, n, z.quarter), BF16), anywhere),
        dmi_all=(shape((layers, n, c), BF16), anywhere),
    )
    scratch = scratch_of(z)
    flags = dict(
        ss=pltpu.SemaphoreType.DMA((sems[0],)),
        rs=pltpu.SemaphoreType.DMA((sems[0],)),
        ls=pltpu.SemaphoreType.DMA((sems[1],)),
    )
    parts = [args, outs, scratch, flags]
    leaf = lambda node: not isinstance(node, (dict, list))
    trees = [jax.tree.flatten(part, is_leaf=leaf) for part in parts]
    whole = jax.tree.structure([dict(part) for part in parts], is_leaf=leaf)

    def kernel(*refs):
        merged = {}
        for part in jax.tree.unflatten(whole, refs):
            merged |= part
        block_kernel(z, sems, merged)

    results = pl.pallas_call(
        kernel,
        out_shape=[one[0] for one in trees[1][0]],
        in_specs=jax.tree.leaves(specs, is_leaf=leaf),
        out_specs=[one[1] for one in trees[1][0]],
        scratch_shapes=trees[2][0] + trees[3][0],
        compiler_params=pltpu.CompilerParams(
            collective_id=0, has_side_effects=True, vmem_limit_bytes=62 * 2**20
        ),
        name="blocks",
    )(*trees[0][0])
    return SimpleNamespace(**jax.tree.unflatten(trees[1][1], results))


def grad_kernel(z, steps, ins, small_ins, win, wout, outs):
    hid, gat, dmg, gq, dmi, smalls = ins
    rows = hid.shape[1]
    first = pl.program_id(2) == 0
    lhs = hid[0]
    parts = (dot(lhs, dmi[0]), dot(lhs, dmg[0], ((1,), (1,))))
    for k, part in enumerate(parts):
        for j in range(z.groups):
            at = pl.ds(j * 2 + k, rows, stride=z.span)
            piece = part[:, j * LANES : (j + 1) * LANES]
            if steps == 1:
                win[at, :] = piece
            else:
                win[at, :] = jnp.where(first, 0.0, win[at, :]) + piece
    part = dot(gat[0], side_by_side(gq[0]))
    if steps == 1:
        wout[0] = part
    else:
        wout[0] = jnp.where(first, 0.0, wout[0]) + part

    begin = first & (pl.program_id(0) == 0) & (pl.program_id(1) == 0)
    pl.when(begin)(lambda: small_outputs(z, smalls, small_ins, outs))


def small_outputs(z, smalls, small_ins, outs):
    for src, to in zip(small_ins, outs[:3], strict=True):
        to[...] = src[...]
    at, pack = 0, 0
    for i, to in enumerate(outs[3:]):
        if i == 4:
            at, pack = 0, 1
        for l in range(z.layers):
            if len(to.shape) == 3:
                count = to.shape[1]
                to[l] = smalls[l, pack, at : at + count, :].astype(F32)
            else:
                count = 1
                to[l : l + 1, :] = smalls[l, pack, at : at + 1, :].astype(F32)
        at += count


def grads_at_once(z, ins, small_ins, win, wout, outs, *scratch):
    smalls = ins[5]
    held, (winv, woutv, lsem, ssem) = scratch[:5], scratch[5:]
    layers, d, c = z.layers, z.width, z.chans
    hid, gat, dmg, gq, dmi = held
    loads = {}
    for l in range(layers):
        for i in (1, 3, 0, 4, 2):
            copy = pltpu.make_async_copy(ins[i].at[l], held[i].at[l], lsem.at[5 * l + i])
            copy.start()
            loads[l, i] = copy
    small_outputs(z, smalls, small_ins, outs)
    stores = []

    def leave(src, to):
        copy = pltpu.make_async_copy(src, to, ssem.at[len(stores)])
        copy.start()
        stores.append(copy)

    rows = d // 2
    for l in range(layers):
        loads[l, 1].wait()
        loads[l, 3].wait()
        woutv[l] = dot(gat[l], side_by_side(gq[l]))
        leave(woutv.at[l], wout.at[l])
        loads[l, 0].wait()
        loads[l, 4].wait()
        loads[l, 2].wait()
        for half in range(2):
            lhs = hid[l, half * rows : (half + 1) * rows, :]
            base = (l * d + half * rows) * z.span
            for k in range(2):
                if k == 0:
                    part = dot(lhs, dmi[l])
                else:
                    part = dot(lhs, dmg[l], ((1,), (1,)))
                for j in range(z.groups):
                    at = pl.ds(base + j * 2 + k, rows, stride=z.span)
                    winv[at, :] = part[:, j * LANES : (j + 1) * LANES]
            span = pl.ds(base, rows * z.span)
            leave(winv.at[span, :], win.at[span, :])
    for copy in stores:
        copy.wait()


def weight_grads(z, r):
    blocks = 2
    deep = min(z.total, 1024)
    steps = z.total // deep
    layers, d, c = z.layers, z.width, z.chans
    rows, orow = d // blocks, c // blocks
    shape = jax.ShapeDtypeStruct
    small_shapes = (
        r.block_out,
        r.input_grad,
        r.gains,
        shape((layers, z.rank, c), F32),
        shape((layers, z.states, c), F32),
        shape((layers, c), F32),
        shape((layers, c), F32),
        shape((layers, z.xdim, c), F32),
        shape((layers, z.taps, c), F32),
        shape((layers, c), F32),
    )

    def fixed(one):
        dims = len(one.shape)
        return pl.BlockSpec(one.shape, lambda l, i, k: (0,) * dims)

    def kernel(*refs):
        ins, small_ins, (win, wout), rest = refs[:6], refs[6:9], refs[9:11], refs[11:]
        outs = rest[: len(small_shapes)]
        if steps == 1:
            scratch = rest[len(small_shapes) :]
            grads_at_once(z, ins, small_ins, win, wout, outs, *scratch)
        else:
            grad_kernel(z, steps, ins, small_ins, win, wout, outs)

    out_shape = [
        shape((layers * d * z.span, LANES), F32),
        shape((layers, c, d), F32),
        *[shape(one.shape, F32) for one in small_shapes],
    ]
    in_specs, out_specs, scratch, grid = None, None, (), (layers, blocks, steps)
    if steps == 1:
        grid = ()
        anywhere = [pl.BlockSpec(memory_space=pl.ANY)]
        vmem = [pl.BlockSpec(memory_space=pltpu.VMEM)]
        in_specs = anywhere * 5 + vmem * 4
        out_specs = anywhere * 2 + vmem * len(small_shapes)
        scratch = (
            *[
                pltpu.VMEM(one.shape, BF16)
                for one in (r.hid_all, r.gat_all, r.dmg_all, r.gq_all, r.dmi_all)
            ],
            pltpu.VMEM(out_shape[0].shape, F32),
            pltpu.VMEM(out_shape[1].shape, F32),
            pltpu.SemaphoreType.DMA((5 * layers,)),
            pltpu.SemaphoreType.DMA((3 * layers,)),
        )
    else:
        in_specs = [
            pl.BlockSpec((1, rows, deep), lambda l, i, k: (l, i, k)),
            pl.BlockSpec((1, orow, deep), lambda l, i, k: (l, i, k)),
            pl.BlockSpec((1, c, deep), lambda l, i, k: (l, 0, k)),
            pl.BlockSpec((1, z.nch, deep, z.quarter), lambda l, i, k: (l, 0, k, 0)),
            pl.BlockSpec((1, deep, c), lambda l, i, k: (l, k, 0)),
            fixed(r.smalls),
            fixed(r.block_out),
            fixed(r.input_grad),
            fixed(r.gains),
        ]
        out_specs = [
            pl.BlockSpec((rows * z.span, LANES), lambda l, i, k: (l * blocks + i, 0)),
            pl.BlockSpec((1, orow, d), lambda l, i, k: (l, i, 0)),
            *[fixed(one) for one in small_shapes],
        ]
    win, wout, *rest = pl.pallas_call(
        kernel,
        grid=grid,
        out_shape=out_shape,
        in_specs=in_specs,
        out_specs=out_specs,
        scratch_shapes=scratch,
        compiler_params=pltpu.CompilerParams(vmem_limit_bytes=60 * 2**20),
        name="weight_grads",
    )(
        r.hid_all,
        r.gat_all,
        r.dmg_all,
        r.gq_all,
        r.dmi_all,
        r.smalls,
        r.block_out,
        r.input_grad,
        r.gains,
    )
    win = win.reshape(layers, d, z.groups, 2, LANES).transpose(0, 1, 3, 2, 4)
    return win.reshape(layers, d, 2, c), wout, rest


def local(
    mesh,
    x_in,
    norm_gain,
    in_weight,
    conv_weight,
    conv_bias,
    xproj_weight,
    dt_weight,
    dt_bias,
    a_log,
    skip_gain,
    out_weight,
    seq_lengths,
    char_mask,
    out_probe,
):
    z = sizes_of(mesh, x_in, in_weight, xproj_weight, dt_weight, a_log, conv_weight)
    w_in = in_weight.reshape(z.layers, z.width, 2, z.groups, LANES)
    w_in = w_in.transpose(0, 1, 3, 2, 4).reshape(-1, LANES)
    r = run_blocks(
        z,
        dict(
            lengths=seq_lengths,
            x=x_in,
            gain=norm_gain,
            probe=out_probe,
            mask=char_mask.reshape(1, z.toks),
            w_in=w_in,
            conv_w=conv_weight,
            conv_b=conv_bias,
            w_x=xproj_weight,
            w_dt=dt_weight,
            dt_b=dt_bias,
            a_log=a_log,
            skip=skip_gain,
            w_out=out_weight,
        ),
    )
    if not z.shared:
        r.smalls = lax.psum(r.smalls, "dp")
    g_in, g_out, rest = weight_grads(z, r)
    block_out, input_grad, gains, g_dt, g_alog, g_bias, g_skip = rest[:7]
    g_x, g_conv_w, g_conv_b = rest[7:]
    return (
        block_out,
        input_grad,
        gains,
        g_in,
        g_conv_w,
        g_conv_b,
        g_x,
        g_dt,
        g_bias,
        g_alog,
        g_skip,
        g_out,
    )


def solution(mesh):
    return jax.shard_map(
        functools.partial(local, mesh),
        mesh=mesh,
        in_specs=(
            P("dp", "chan"),
            P(None, "chan"),
            P(None, None, None, "chan"),
            P(None, None, "chan"),
            P(None, "chan"),
            P(None, None, "chan"),
            P(None, None, "chan"),
            P(None, "chan"),
            P(None, None, "chan"),
            P(None, "chan"),
            P(None, "chan", None),
            P(),
            P("dp"),
            P("dp", "chan"),
        ),
        out_specs=(
            P("dp", "chan"),
            P("dp", "chan"),
            P(None, "chan"),
            P(None, None, None, "chan"),
            P(None, None, "chan"),
            P(None, "chan"),
            P(None, None, "chan"),
            P(None, None, "chan"),
            P(None, "chan"),
            P(None, None, "chan"),
            P(None, "chan"),
            P(None, "chan", None),
        ),
        check_vma=False,
    )
```
